32 devices in a mesh: rep: 16 (over z, y, core), shard: 2 (over x).
Axes of the slice: x: 2, y: 2, z: 4, core: 2. Of those that a mesh axis runs over, the one named last changes fastest.
Arguments:
- tokens: bfloat16 [16384, 1024], P(('rep', 'shard')), may hold values from -6 to 6
- segments: int32 [32, 512], P(('rep', 'shard')), may hold values from 0 to 2, as said below
- norm1_gain: bfloat16 [1024], P('shard'), may hold values from 0.099609375 to 1.8984375
- norm1_shift: bfloat16 [1024], P('shard'), may hold values from -3 to 3
- norm2_gain: bfloat16 [1024], P('shard'), may hold values from 0.099609375 to 1.8984375
- norm2_shift: bfloat16 [1024], P('shard'), may hold values from -3 to 3
- qkv_weight: bfloat16 [1024, 3072], P('shard'), may hold values from -0.1875 to 0.1875
- qkv_bias: bfloat16 [3072], P('shard'), may hold values from -3 to 3
- out_weight: bfloat16 [1024, 1024], P('shard'), may hold values from -0.5 to 0.5
- out_bias: bfloat16 [1024], P('shard'), may hold values from -2 to 2
- up_weight: bfloat16 [1024, 4096], P('shard'), may hold values from -0.1875 to 0.1875
- up_bias: bfloat16 [4096], P('shard'), may hold values from -3 to 3
- down_weight: bfloat16 [4096, 1024], P('shard'), may hold values from -0.09375 to 0.09375
- down_bias: bfloat16 [1024], P('shard'), may hold values from -2 to 2
- cotangent: bfloat16 [16384, 1024], P(('rep', 'shard')), may hold values from -6 to 6
Outputs:
- output: bfloat16 [16384, 1024], P(('rep', 'shard'))
- grad_tokens: bfloat16 [16384, 1024], P(('rep', 'shard'))
- grad_norm1_gain: float32 [1024], P('shard')
- grad_norm1_shift: float32 [1024], P('shard')
- grad_norm2_gain: float32 [1024], P('shard')
- grad_norm2_shift: float32 [1024], P('shard')
- grad_qkv_weight: float32 [1024, 3072], P('shard')
- grad_qkv_bias: float32 [3072], P('shard')
- grad_out_weight: float32 [1024, 1024], P('shard')
- grad_out_bias: float32 [1024], P('shard')
- grad_up_weight: float32 [1024, 4096], P('shard')
- grad_up_bias: float32 [4096], P('shard')
- grad_down_weight: float32 [4096, 1024], P('shard')
- grad_down_bias: float32 [1024], P('shard')
The draws below stay inside these ranges and needn't reach their ends.
Inputs may be any that keep to these rules, and one draw needn't show every extreme that they name: `segments`: in each sequence the document numbers start at 0 and never fall, and each of the 3 documents appears; one document has exactly 256 tokens and each other one has 102 tokens or more.
All inputs are finite; a program needn't handle non-finite values.
Results may differ from the reference program's by a relative error of at most 0.011.
Values may be sent and summed in bfloat16 or wider, within the bound.
No kernel may reach another device: no remote copies, remote signals or barrier semaphores. Data moves between devices by JAX's collectives and lax.ppermute only.
A program may use at most 320 MiB of HBM per device.

```python
import jax
import jax.numpy as jnp
from jax import lax

D = 1024
HEADS = 16
FF = 4096
TOK_DEV = 512
HD = 64
ROT = 16
SEQS = 32
TOKENS = 16384


def draw_segments(key, part):
    key = jax.random.fold_in(key, 11)
    key_place, key_split = jax.random.split(key)
    half = TOK_DEV // 2
    short = TOK_DEV // 5
    place = jax.random.randint(key_place, (SEQS,), 0, 3, dtype=jnp.int32)
    first = jax.random.randint(key_split, (SEQS,), short, half - short + 1, dtype=jnp.int32)
    second = half - first
    length_zero = jnp.where(place == 0, half, first)
    length_one = jnp.where(place == 1, half, jnp.where(place == 0, first, second))
    end_zero = length_zero
    end_one = length_zero + length_one
    positions = jnp.arange(TOK_DEV, dtype=jnp.int32)
    beyond_zero = (positions[None, :] >= end_zero[:, None]).astype(jnp.int32)
    beyond_one = (positions[None, :] >= end_one[:, None]).astype(jnp.int32)
    return beyond_zero + beyond_one


def block_scale(rng, shape, cuts, least, top_value):
    def one(dim, blocks):
        steps = jax.random.uniform(jax.random.fold_in(jax.random.fold_in(rng, 6), dim), (blocks,), jnp.float32, least / len(cuts), top_value / len(cuts))
        return jnp.repeat(jnp.exp(steps), shape[dim] // blocks).reshape((-1,) + (1,) * (len(shape) - dim - 1))

    factor_of = one(*cuts[0])
    for cut in cuts[1:]:
        factor_of = factor_of * one(*cut)
    return factor_of


def bell_draw(stream_key, shape, deviation, reach, shards=(), kind=jnp.bfloat16):
    array = deviation * jax.random.normal(stream_key, shape, jnp.float32)
    if shards:
        array = array * block_scale(stream_key, shape, shards, -0.22, 0.18)
    return jnp.clip(array, -reach, reach).astype(kind)


def setup_inputs(seed: int = 0) -> dict:
    streams_of = jax.random.split(jax.random.key(seed), 16)
    tokens = bell_draw(streams_of[0], (TOKENS, D), 1.0, 6.0, ((0, 32),))
    segments = draw_segments(jax.random.fold_in(streams_of[15], 71), 0)
    norm1_gain = jnp.clip(1.0 + 0.18 * jax.random.normal(streams_of[2], (D,), jnp.float32), 0.099609375, 1.8984375).astype(jnp.bfloat16)
    norm1_shift = bell_draw(streams_of[3], (D,), 0.5, 3.0, ((0, 2),))
    norm2_gain = jnp.clip(1.0 + 0.18 * jax.random.normal(streams_of[4], (D,), jnp.float32), 0.099609375, 1.8984375).astype(jnp.bfloat16)
    norm2_shift = bell_draw(streams_of[5], (D,), 0.5, 3.0, ((0, 2),))
    qkv_weight = bell_draw(streams_of[6], (D, 3 * D), D ** -0.5, 0.1875, ((0, 2),))
    qkv_bias = bell_draw(streams_of[7], (3 * D,), 0.5, 3.0, ((0, 2),))
    out_weight = bell_draw(streams_of[8], (D, D), (D // 8) ** -0.5, 0.5, ((0, 2),))
    out_bias = bell_draw(streams_of[9], (D,), 0.3, 2.0, ((0, 2),))
    up_weight = bell_draw(streams_of[10], (D, FF), D ** -0.5, 0.1875, ((0, 2),))
    up_bias = bell_draw(streams_of[11], (FF,), 0.5, 3.0, ((0, 2),))
    down_weight = bell_draw(streams_of[12], (FF, D), FF ** -0.5, 0.09375, ((0, 2),))
    down_bias = bell_draw(streams_of[13], (D,), 0.3, 2.0, ((0, 2),))
    cotangent = bell_draw(streams_of[14], (TOKENS, D), 1.0, 6.0, ((0, 32),))
    return {"tokens": tokens, "segments": segments, "norm1_gain": norm1_gain, "norm1_shift": norm1_shift, "norm2_gain": norm2_gain, "norm2_shift": norm2_shift, "qkv_weight": qkv_weight, "qkv_bias": qkv_bias, "out_weight": out_weight, "out_bias": out_bias, "up_weight": up_weight, "up_bias": up_bias, "down_weight": down_weight, "down_bias": down_bias, "cotangent": cotangent}


@jax.custom_vjp
def low(v):
    return lax.optimization_barrier(v.astype(jnp.bfloat16)).astype(jnp.float32)

@jax.custom_vjp
def low_back(v):
    return v

def low_keep(v):
    return (low(v), None)

def low_pass(kept, grad):
    return (grad,)

def back_keep(v):
    return (v, None)

def back_low(kept, grad):
    return (low(grad),)
low.defvjp(low_keep, low_pass)
low_back.defvjp(back_keep, back_low)
epsilon = 1e-05
masked_score = -1e+30
highest = lax.Precision.HIGHEST

def layer_norm(values, norm_gain, norm_shift):
    average = lax.optimization_barrier(jnp.mean(values, axis=-1, keepdims=True))
    centred = values - average
    spread = lax.optimization_barrier(jnp.mean(centred * centred, axis=-1, keepdims=True))
    return centred * lax.rsqrt(spread + epsilon) * norm_gain + norm_shift

def rotary_tables(documents):
    length = documents.shape[0]
    places = jnp.arange(length, dtype=jnp.int32)
    before = lax.optimization_barrier(jnp.sum((documents[None, :] < documents[:, None]).astype(jnp.int32), axis=1))
    offsets = (places - before).astype(jnp.float32)
    exponents = jnp.arange(0, ROT, 2, dtype=jnp.float32) / ROT
    inverse = 1.0 / 10000.0 ** exponents
    angles = offsets[:, None] * inverse[None, :]
    angles = jnp.concatenate([angles, angles], axis=-1)
    return (jnp.cos(angles), jnp.sin(angles))

def rotate(values, cosine, sine):
    turning = values[..., :ROT]
    halfway = ROT // 2
    turned = jnp.concatenate([-turning[..., halfway:], turning[..., :halfway]], axis=-1)
    moved = turning * cosine[:, None, :] + turned * sine[:, None, :]
    return jnp.concatenate([moved, values[..., ROT:]], axis=-1)

def attend(queries, keys, values, documents):
    length = documents.shape[0]
    scores = jnp.einsum('qhd,khd->hqk', queries, keys, precision=highest) * HD ** (-0.5)
    scores = low_back(scores)
    places = jnp.arange(length, dtype=jnp.int32)
    allowed = (documents[:, None] == documents[None, :]) & (places[None, :] <= places[:, None])
    scores = jnp.where(allowed[None], scores, masked_score)
    highest_score = lax.optimization_barrier(jnp.max(scores, axis=-1, keepdims=True))
    weights = jnp.exp(scores - highest_score)
    weights = weights / lax.optimization_barrier(jnp.sum(weights, axis=-1, keepdims=True))
    weights = low(weights)
    return jnp.einsum('hqk,khd->qhd', weights, values, precision=highest)

def forward(params, tokens, segments):
    gain_one, shift_one, gain_two, shift_two, qkv_weight, qkv_bias, out_weight, out_bias, up_weight, up_bias, down_weight, down_bias = params
    group_count, length, width = tokens.shape
    rows_all = tokens.reshape(group_count * length, width)
    normed_one = low(layer_norm(rows_all, gain_one, shift_one))
    mixed = low_back(jnp.dot(normed_one, qkv_weight, precision=highest) + qkv_bias)
    mixed = mixed.reshape(group_count, length, 3, HEADS, HD)

    def one_sequence(entry):
        triple, documents = entry
        cosine, sine = rotary_tables(documents)
        queries = low(rotate(triple[:, 0], cosine, sine))
        keys = low(rotate(triple[:, 1], cosine, sine))
        values = low(triple[:, 2])
        return attend(queries, keys, values, documents)
    context = lax.map(jax.checkpoint(one_sequence), (mixed, segments))
    context = low_back(low(context.reshape(group_count * length, width)))
    attn_result = jnp.dot(context, out_weight, precision=highest) + out_bias
    normed_two = low(layer_norm(rows_all, gain_two, shift_two))
    hidden = low_back(jnp.dot(normed_two, up_weight, precision=highest) + up_bias)
    active = low(jax.nn.gelu(hidden, approximate=False))
    ffn_result = jnp.dot(active, down_weight, precision=highest) + down_bias
    return (rows_all + attn_result + ffn_result).reshape(group_count, length, width)

def reference(tokens, segments, norm1_gain, norm1_shift, norm2_gain, norm2_shift, qkv_weight, qkv_bias, out_weight, out_bias, up_weight, up_bias, down_weight, down_bias, cotangent):
    params = tuple((entry.astype(jnp.float32) for entry in (norm1_gain, norm1_shift, norm2_gain, norm2_shift, qkv_weight, qkv_bias, out_weight, out_bias, up_weight, up_bias, down_weight, down_bias)))
    group_size = max(1, min(SEQS, 4096 // TOK_DEV))
    step_count = SEQS // group_size
    inputs_all = tokens.astype(jnp.float32).reshape(step_count, group_size, TOK_DEV, D)
    documents_all = segments.reshape(step_count, group_size, TOK_DEV)
    cotangents_all = cotangent.astype(jnp.float32).reshape(step_count, group_size, TOK_DEV, D)

    def one_step(totals, entry):
        block_in, documents, block_cot = entry
        result, pull_back = jax.vjp(lambda params_in, tokens_in: forward(params_in, tokens_in, documents), params, block_in)
        grads, grad_in = pull_back(block_cot)
        totals = jax.tree.map(lambda left_sum, right_sum: left_sum + right_sum, totals, grads)
        return (totals, (result.astype(jnp.bfloat16), grad_in.astype(jnp.bfloat16)))
    zeros_all = jax.tree.map(jnp.zeros_like, params)
    totals, (results, grads_in) = lax.scan(one_step, zeros_all, (inputs_all, documents_all, cotangents_all))
    output = results.reshape(TOKENS, D)
    grad_tokens = grads_in.reshape(TOKENS, D)
    return (output, grad_tokens, totals[0], totals[1], totals[2], totals[3], totals[4], totals[5], totals[6], totals[7], totals[8], totals[9], totals[10], totals[11])
```

```python
import jax
import jax.numpy as jnp
from jax import lax
from jax.sharding import PartitionSpec as P

HEADS = 16
HD = 64
ROT = 16

EPSILON = 1e-05
MASKED = -1e30
BF = jnp.bfloat16
F32 = jnp.float32


def dot(left, right, left_dim=1, right_dim=0, kind=F32):
    return lax.dot_general(
        left, right, (((left_dim,), (right_dim,)), ((), ())), preferred_element_type=kind
    )


def rotary_tables(documents):
    length = documents.shape[0]
    places = jnp.arange(length, dtype=jnp.int32)
    before = jnp.sum((documents[None, :] < documents[:, None]).astype(jnp.int32), axis=1)
    offsets = (places - before).astype(F32)
    exponents = jnp.arange(0, ROT, 2, dtype=F32) / ROT
    inverse = 1.0 / 10000.0**exponents
    angles = offsets[:, None] * inverse[None, :]
    angles = jnp.concatenate([angles, angles], axis=-1)
    return jnp.cos(angles), jnp.sin(angles)


def rotate(values, cosine, sine):
    turning = values[..., :ROT]
    halfway = ROT // 2
    turned = jnp.concatenate([-turning[..., halfway:], turning[..., :halfway]], axis=-1)
    moved = turning * cosine[:, :, None, :] + turned * sine[:, :, None, :]
    return jnp.concatenate([moved, values[..., ROT:]], axis=-1)


def build(reps):
    bits = reps.bit_length() - 1
    upper = list(range(2, bits))

    def flip(array, bit):
        return lax.ppermute(array, "rep", [(i, i ^ (1 << bit)) for i in range(reps)])

    def flip_x(array):
        return lax.ppermute(array, "shard", [(0, 1), (1, 0)])

    def on_device(
        tokens, segments, norm1_gain, norm1_shift, norm2_gain, norm2_shift, qkv_weight, qkv_bias,
        out_weight, out_bias, up_weight, up_bias, down_weight, down_bias, cotangent,
    ):
        half, width = out_weight.shape
        length = tokens.shape[0]
        ff_half = down_weight.shape[0]
        xi = lax.axis_index("shard")
        ri = lax.axis_index("rep")
        rbit = [(ri >> b) & 1 for b in range(bits)]
        ci, yi = rbit[0], rbit[1]

        def ordered(bit, own, other, axis=0):
            return jnp.where(
                bit == 0,
                jnp.concatenate([own, other], axis),
                jnp.concatenate([other, own], axis),
            )

        def pick(array, index, axis):
            return lax.dynamic_index_in_dim(array, index, axis, keepdims=False)

        heads_core = half // 2
        up_own = pick(up_weight.reshape(half, 2, 2, ff_half // 2), ci, 2).reshape(half, ff_half)
        down_own = pick(down_weight.reshape(2, ff_half // 2, width), ci, 0)
        qkv_own = pick(qkv_weight.reshape(half, 3, 2, 2, heads_core), ci, 3).reshape(half, 3 * half)
        out_own = pick(out_weight.reshape(2, heads_core, width), ci, 0)

        def fetch(own):
            rows = own.shape[0] // 2
            part = lax.dynamic_slice_in_dim(own, yi * rows, rows, 0)
            first = flip_x(part)
            second = flip(first, 1)
            return first, second

        def whole(own, pair):
            return ordered(xi, own, ordered(yi, *pair))

        small_own = jnp.concatenate(
            [norm1_gain, norm1_shift, norm2_gain, norm2_shift, out_bias, down_bias, qkv_bias, up_bias]
        )
        small_other = flip_x(small_own)
        tokens_other = flip(tokens, 0)
        cot_other = flip(cotangent, 0)
        segments_other = flip(segments, 0)
        up_pair = fetch(up_own)
        down_pair = fetch(down_own)
        qkv_pair = fetch(qkv_own)
        out_pair = fetch(out_own)

        low = jnp.where(xi == 0, small_own, small_other).astype(F32)
        high = jnp.where(xi == 0, small_other, small_own).astype(F32)
        full = []
        at = 0
        for size in [half] * 6 + [qkv_bias.shape[0], ff_half]:
            full.append(jnp.concatenate([low[at : at + size], high[at : at + size]]))
            at += size
        gain_one, shift_one, gain_two, shift_two, out_b, down_b, qkv_b, up_b = full
        qkv_bc = pick(qkv_b.reshape(3, 2, 2, heads_core), ci, 2).reshape(3 * half)
        up_bc = pick(up_b.reshape(2, 2, ff_half // 2), ci, 1).reshape(ff_half)

        both = jnp.concatenate([tokens, tokens_other], 0)
        cot = jnp.concatenate([cotangent, cot_other], 0)
        rows = both.astype(F32)
        average = jnp.mean(rows, axis=-1, keepdims=True)
        centred = rows - average
        spread = lax.rsqrt(jnp.mean(centred * centred, axis=-1, keepdims=True) + EPSILON)
        unit = centred * spread
        normed_one = (unit * gain_one + shift_one).astype(BF)
        normed_two = (unit * gain_two + shift_two).astype(BF)

        def split(array, axis):
            size = array.shape[axis] // 2
            own = lax.dynamic_slice_in_dim(array, xi * size, size, axis)
            other = lax.dynamic_slice_in_dim(array, (1 - xi) * size, size, axis)
            return own, other

        def reduce_scatter(own, other):
            total = (own.astype(F32) + flip_x(other).astype(F32)).astype(BF)
            r, cols = total.shape
            total = total.reshape((2,) * (bits - 1) + (r >> (bits - 1), cols))
            for n, bit in enumerate([1] + upper):
                axis = len(upper) if bit == 1 else 0
                keep = pick(total, rbit[bit], axis)
                send = pick(total, 1 - rbit[bit], axis)
                total = (keep.astype(F32) + flip(send, bit).astype(F32)).astype(BF)
            return total

        def gather(piece):
            for bit in [1] + upper[::-1] + [0]:
                other = flip(piece, bit)
                piece = ordered(rbit[bit], piece[None], other[None])
            return piece

        up_full = whole(up_own, up_pair)
        hidden = dot(normed_two, up_full) + up_bc
        cdf = 0.5 * (1.0 + lax.erf(hidden * (0.5**0.5)))
        active = (hidden * cdf).astype(BF)
        slope = cdf + hidden * jnp.exp(-0.5 * hidden * hidden) * ((2.0 * jnp.pi) ** -0.5)
        act_own, act_other = split(active, 1)
        down_other_grad = dot(act_other, cot, 0, 0, BF)
        down_own_grad = dot(act_own, cot, 0, 0, BF)
        down_piece = reduce_scatter(down_own_grad, down_other_grad)
        down_full = whole(down_own, down_pair)
        grad_hidden = (dot(cot, down_full, 1, 1) * slope).astype(BF)
        two_own, two_other = split(normed_two, 1)
        up_other_grad = dot(two_other, grad_hidden, 0, 0, BF)
        up_own_grad = dot(two_own, grad_hidden, 0, 0, BF)
        up_piece = reduce_scatter(up_own_grad, up_other_grad)
        grad_up_bias = jnp.sum(grad_hidden.astype(F32), axis=0)
        ffn_part = dot(active, down_full)
        grad_two = dot(grad_hidden, up_full, 1, 1)

        qkv_full = whole(qkv_own, qkv_pair)
        out_full = whole(out_own, out_pair)
        local = half // HD
        mixed = (dot(normed_one, qkv_full) + qkv_bc).reshape(2, length, 3, local, HD)
        documents = jnp.concatenate([segments, segments_other], 0)
        cosine, sine = jax.vmap(rotary_tables)(documents)
        queries = rotate(mixed[:, :, 0], cosine, sine).astype(BF)
        keys = rotate(mixed[:, :, 1], cosine, sine).astype(BF)
        values = mixed[:, :, 2].astype(BF)
        scale = HD**-0.5
        places = jnp.arange(length, dtype=jnp.int32)
        allowed = (documents[:, :, None] == documents[:, None, :]) & (
            places[None, None, :] <= places[None, :, None]
        )
        scores = jnp.einsum("sqhd,skhd->shqk", queries, keys, preferred_element_type=F32) * scale
        scores = jnp.where(allowed[:, None], scores, MASKED)
        weights = jnp.exp(scores - jnp.max(scores, axis=-1, keepdims=True))
        probs = weights / jnp.sum(weights, axis=-1, keepdims=True)
        probs_low = probs.astype(BF)
        context = jnp.einsum("shqk,skhd->sqhd", probs_low, values, preferred_element_type=F32)
        context = context.astype(BF).reshape(2 * length, half)
        attn_part = dot(context, out_full)
        grad_context = dot(cot, out_full, 1, 1).astype(BF).reshape(2, length, local, HD)
        grad_probs = jnp.einsum("sqhd,skhd->shqk", grad_context, values, preferred_element_type=F32)
        inner = jnp.sum(probs * grad_probs, axis=-1, keepdims=True)
        grad_scores = (probs * (grad_probs - inner)).astype(BF)
        grad_q = jnp.einsum("shqk,skhd->sqhd", grad_scores, keys, preferred_element_type=F32) * scale
        grad_k = jnp.einsum("shqk,sqhd->skhd", grad_scores, queries, preferred_element_type=F32) * scale
        grad_v = jnp.einsum("shqk,sqhd->skhd", probs_low, grad_context, preferred_element_type=F32)
        grad_q = rotate(grad_q, cosine, -sine)
        grad_k = rotate(grad_k, cosine, -sine)
        grad_mixed = jnp.stack([grad_q, grad_k, grad_v], axis=2).reshape(2 * length, 3 * half).astype(BF)
        one_own, one_other = split(normed_one, 1)
        qkv_other_grad = dot(one_other, grad_mixed, 0, 0, BF)
        qkv_own_grad = dot(one_own, grad_mixed, 0, 0, BF)
        qkv_piece = reduce_scatter(qkv_own_grad, qkv_other_grad)
        ctx_own, ctx_other = split(context, 1)

        def fold(array):
            return jnp.concatenate([array[:, :half], array[:, half:]], 0)

        out_piece = reduce_scatter(
            fold(dot(ctx_own, cot, 0, 0, BF)), fold(dot(ctx_other, cot, 0, 0, BF))
        )
        grad_one = dot(grad_mixed, qkv_full, 1, 1)

        def spread_core(vector, parts):
            size = vector.shape[0] // parts
            wide = jnp.stack([vector.reshape(parts, size)] * 2, axis=1)
            keep = (jnp.arange(2) == ci)[None, :, None]
            return jnp.where(keep, wide, 0.0).reshape(-1)

        column_sum = jnp.sum(cotangent.astype(F32), axis=0)
        small = jnp.concatenate(
            [
                jnp.sum(grad_one * unit, axis=0),
                jnp.sum(grad_one, axis=0),
                jnp.sum(grad_two * unit, axis=0),
                jnp.sum(grad_two, axis=0),
                column_sum,
                spread_core(jnp.sum(grad_mixed.astype(F32), axis=0), 6),
                spread_core(grad_up_bias, 2),
            ]
        ).reshape(-1, width)
        small = small + flip_x(small)
        for bit in range(bits):
            small = small + flip(small, bit)
        small = small.reshape(-1)

        part = attn_part + ffn_part
        output = (
            tokens.astype(F32)
            + (part[:length] + flip(part[length:], 0))
            + (out_b + down_b)
        ).astype(BF)
        pulled = grad_one * gain_one + grad_two * gain_two
        pulled = pulled[:length] + flip(pulled[length:], 0)
        unit_own = unit[:length]
        inward = spread[:length] * (
            pulled
            - jnp.mean(pulled, axis=-1, keepdims=True)
            - unit_own * jnp.mean(pulled * unit_own, axis=-1, keepdims=True)
        )
        grad_tokens = (cotangent.astype(F32) + inward).astype(BF)

        def rows_first(piece):
            return piece.reshape(2, -1, piece.shape[-1])

        down_all = rows_first(gather(down_piece)).reshape(ff_half, width).astype(F32)
        up_all = rows_first(gather(up_piece)).reshape(2, half, 2, ff_half // 2)
        up_all = jnp.transpose(up_all, (1, 2, 0, 3)).reshape(half, 2 * ff_half).astype(F32)
        qkv_all = rows_first(gather(qkv_piece)).reshape(2, half, 6, heads_core)
        qkv_all = jnp.transpose(qkv_all, (1, 2, 0, 3)).reshape(half, 6 * half).astype(F32)
        out_all = rows_first(gather(out_piece)).reshape(2, 2, heads_core, half)
        out_all = jnp.transpose(out_all, (0, 2, 1, 3)).reshape(half, width).astype(F32)

        def owned(start, size):
            return lax.dynamic_slice_in_dim(small, start + xi * size, size, 0)

        starts = [width * n for n in range(9)]
        bias_out = owned(starts[4], half)
        return (
            output,
            grad_tokens,
            owned(starts[0], half),
            owned(starts[1], half),
            owned(starts[2], half),
            owned(starts[3], half),
            qkv_all,
            owned(starts[5], 3 * half),
            out_all,
            bias_out,
            up_all,
            owned(starts[8], ff_half),
            down_all,
            bias_out,
        )

    return on_device


def solution(mesh):
    both = P(("rep", "shard"), None)
    vector = P("shard")
    matrix = P("shard", None)
    weights = (
        vector, vector, vector, vector, matrix, vector, matrix, vector, matrix, vector, matrix, vector,
    )
    return jax.shard_map(
        build(mesh.shape["rep"]),
        mesh=mesh,
        in_specs=(both, both) + weights + (both,),
        out_specs=(both, both) + weights,
        check_vma=False,
    )
```

```python
import jax
import jax.numpy as jnp
from jax import lax
from jax.experimental import pallas as pl
from jax.experimental.pallas import tpu as pltpu
from jax.sharding import PartitionSpec as P

HD = 64
ROT = 16
EPSILON = 1e-05
MASKED = -1e30
BF = jnp.bfloat16
F32 = jnp.float32
TILE = 512
MIB = 1 << 20
NN = (((1,), (0,)), ((), ()))
NT = (((1,), (1,)), ((), ()))
TN = (((0,), (0,)), ((), ()))


def mm(left, right, dims=NN):
    return lax.dot_general(left, right, dims, preferred_element_type=F32)


def cost(flops, nbytes):
    return pl.CostEstimate(flops=int(flops), bytes_accessed=int(nbytes), transcendentals=0)


def params(mib):
    return pltpu.CompilerParams(vmem_limit_bytes=mib * MIB)


ANY = pl.BlockSpec(memory_space=pl.ANY)


def held(shape):
    return pl.BlockSpec(shape, lambda *_: (0,) * len(shape), pipeline_mode=pl.Buffered(1))


def sds(shape, kind):
    return jax.ShapeDtypeStruct(shape, kind)


def copy_all(pairs, sems):
    copies = [pltpu.make_async_copy(a, b, sems.at[n]) for n, (a, b) in enumerate(pairs)]
    for c in copies:
        c.start()
    for c in copies:
        c.wait()


def place(index):
    return index[0], index[1], index[2], index[3]


def quarters(index):
    _, _, y, z = place(index)
    return (2 * y + z, 2 * (1 - y) + z, 2 * y + (1 - z), 2 * (1 - y) + (1 - z))


def pack_up_kernel(index, weight, out, sems):
    x, c, y, z = place(index)
    half = weight.shape[0]
    rows = half // 4
    wide = weight.shape[1] // 4
    row = pl.ds(pl.multiple_of((2 * y + z) * rows, rows), rows)
    copy_all(
        [
            (weight.at[row, pl.ds(pl.multiple_of((2 * h + c) * wide, wide), wide)], out.at[:, pl.ds(h * wide, wide)])
            for h in range(2)
        ],
        sems,
    )


def pack_rest_kernel(index, down, qkv, out_w, down_out, rest_out, sems):
    x, c, y, z = place(index)
    q = 2 * y + z
    rows = down.shape[0] // 8
    pairs = [(down.at[pl.ds(pl.multiple_of((4 * c + q) * rows, rows), rows)], down_out)]
    half = qkv.shape[0]
    rows = half // 4
    wide = half // 2
    for t in range(3):
        for h in range(2):
            col = pl.multiple_of((4 * t + 2 * h + c) * wide, wide)
            pairs.append(
                (
                    qkv.at[pl.ds(pl.multiple_of(q * rows, rows), rows), pl.ds(col, wide)],
                    rest_out.at[:, pl.ds((2 * t + h) * wide, wide)],
                )
            )
    rows = half // 8
    for h in range(2):
        pairs.append(
            (
                out_w.at[pl.ds(pl.multiple_of((4 * c + q) * rows, rows), rows), pl.ds(h * half, half)],
                rest_out.at[pl.ds(h * rows, rows), pl.ds(3 * half, half)],
            )
        )
    copy_all(pairs, sems)


def up_pairs(index, weight, pieces, dest, side):
    x, c, _, _ = place(index)
    half = weight.shape[0]
    rows = half // 4
    wide = weight.shape[1] // 4
    pairs = [
        (
            weight.at[:, pl.ds(pl.multiple_of((2 * side + c) * wide, wide), wide)],
            dest.at[pl.ds(pl.multiple_of(x * half, half), half)],
        )
    ]
    for q, piece in zip(quarters(index), pieces):
        pairs.append(
            (
                piece.at[:, pl.ds(pl.multiple_of(side * wide, wide), wide)],
                dest.at[pl.ds(pl.multiple_of((1 - x) * half + q * rows, rows), rows)],
            )
        )
    return pairs


BLOCK = 256


def gelu_parts(hidden):
    cdf = 0.5 * (1.0 + lax.erf(hidden * (0.5**0.5)))
    slope = cdf + hidden * jnp.exp(-0.5 * hidden * hidden) * ((2.0 * jnp.pi) ** -0.5)
    return (hidden * cdf).astype(BF), slope


def ffn_other_kernel(index, normed, cot, bias, weight, p0, p1, p2, p3, act, slope, grad, w_all, sems):
    x = index[0]
    j = pl.program_id(0)

    @pl.when(j == 0)
    def _():
        copy_all(up_pairs(index, weight, (p0, p1, p2, p3), w_all, 1 - x), sems)

    w = w_all[:, pl.ds(pl.multiple_of(j * BLOCK, BLOCK), BLOCK)]
    hidden = mm(normed[...], w) + bias[...]
    a, s = gelu_parts(hidden)
    act[...] = a
    slope[...] = s.astype(BF)
    g = mm(a, cot[...], TN).astype(BF)
    grad[0] = g[:, :TILE]
    grad[1] = g[:, TILE:]


def ffn_own_kernel(
    index, normed, cot, bias, down, weight, p0, p1, p2, p3,
    act, hid, grad_down, up_send, up_keep, colsum, w_all, sems,
):
    x = index[0]
    j = pl.program_id(0)

    @pl.when(j == 0)
    def _():
        copy_all(up_pairs(index, weight, (p0, p1, p2, p3), w_all, x), sems)

    w = w_all[:, pl.ds(pl.multiple_of(j * BLOCK, BLOCK), BLOCK)]
    hidden = mm(normed[...], w) + bias[...]
    a, s = gelu_parts(hidden)
    act[...] = a
    g = mm(a, cot[...], TN).astype(BF)
    grad_down[0] = g[:, :TILE]
    grad_down[1] = g[:, TILE:]
    gh = mm(cot[...], down[...], NT) * s
    low = gh.astype(BF)
    hid[...] = low
    colsum[...] = jnp.sum(low.astype(F32), axis=0, keepdims=True)
    up_send[0] = mm(normed[:, pl.ds(pl.multiple_of((1 - x) * TILE, TILE), TILE)], low, TN).astype(BF)
    up_keep[0] = mm(normed[:, pl.ds(pl.multiple_of(x * TILE, TILE), TILE)], low, TN).astype(BF)


def ffn_back_kernel(index, normed, cot, slope, d0, d1, d2, d3, hid, up_send, up_keep, colsum, d_all, sems):
    x = index[0]
    j = pl.program_id(0)
    rows = d0.shape[0]

    @pl.when(j == 0)
    def _():
        copy_all(
            [
                (piece, d_all.at[pl.ds(pl.multiple_of(q * rows, rows), rows)])
                for q, piece in zip(quarters(index), (d0, d1, d2, d3))
            ],
            sems,
        )

    d = d_all[pl.ds(pl.multiple_of(j * BLOCK, BLOCK), BLOCK), :]
    low = (mm(cot[...], d, NT) * slope[...].astype(F32)).astype(BF)
    hid[...] = low
    colsum[...] = jnp.sum(low.astype(F32), axis=0, keepdims=True)
    up_send[0] = mm(normed[:, pl.ds(pl.multiple_of((1 - x) * TILE, TILE), TILE)], low, TN).astype(BF)
    up_keep[0] = mm(normed[:, pl.ds(pl.multiple_of(x * TILE, TILE), TILE)], low, TN).astype(BF)


def ffn_last_kernel(
    index, act_o, act_x, hid_o, hid_x, down, d0, d1, d2, d3, weight, p0, p1, p2, p3,
    out, grad, w_o, w_x, d_o, d_x, sems,
):
    x, c, _, _ = place(index)

    @pl.when(pl.program_id(0) == 0)
    def _():
        rows = d0.shape[0]
        wide = d_o.shape[0]
        pairs = up_pairs(index, weight, (p0, p1, p2, p3), w_o, x)
        pairs += up_pairs(index, weight, (p0, p1, p2, p3), w_x, 1 - x)
        pairs.append((down.at[pl.ds(pl.multiple_of(c * wide, wide), wide)], d_o))
        for q, piece in zip(quarters(index), (d0, d1, d2, d3)):
            pairs.append((piece, d_x.at[pl.ds(pl.multiple_of(q * rows, rows), rows)]))
        copy_all(pairs, sems)

    out[...] = mm(act_o[...], d_o[...]) + mm(act_x[...], d_x[...])
    grad[...] = mm(hid_o[...], w_o[...], NT) + mm(hid_x[...], w_x[...], NT)


def attention_kernel(
    index, normed, cot, cosine, sine_low, sine_high, doc_col, doc_row, bias, qkv, out_w, p0, p1, p2, p3,
    send, keep, grad_normed, result, colsum, w_all, o_all, mask, sems,
):
    x, c, _, _ = place(index)
    p = pl.program_id(0)
    half = qkv.shape[0]
    quarter = half // 4
    pair = 2 * HD
    length = doc_row.shape[1]

    @pl.when(p == 0)
    def _():
        pairs = []
        own = pl.ds(pl.multiple_of(x * half, half), half)
        wide = half // 2
        for t in range(3):
            for h in range(2):
                col = pl.multiple_of((4 * t + 2 * h + c) * wide, wide)
                pairs.append((qkv.at[:, pl.ds(col, wide)], w_all.at[own, pl.ds((2 * t + h) * wide, wide)]))
        pairs.append(
            (
                out_w.at[pl.ds(pl.multiple_of(c * wide, wide), wide)],
                o_all.at[pl.ds(pl.multiple_of(x * wide, wide), wide)],
            )
        )
        eighth = half // 8
        for q, piece in zip(quarters(index), (p0, p1, p2, p3)):
            row = pl.multiple_of((1 - x) * half + q * quarter, quarter)
            pairs.append((piece.at[:, pl.ds(0, 3 * half)], w_all.at[pl.ds(row, quarter)]))
            row = pl.multiple_of((1 - x) * wide + q * eighth, eighth)
            for h in range(2):
                pairs.append(
                    (
                        piece.at[pl.ds(h * eighth, eighth), pl.ds(3 * half, half)],
                        o_all.at[pl.ds(row, eighth), pl.ds(h * half, half)],
                    )
                )
        copies = [pltpu.make_async_copy(a, b, sems.at[n]) for n, (a, b) in enumerate(pairs)]
        for copy in copies:
            copy.start()
        for s in range(2):
            keys = lax.broadcasted_iota(jnp.int32, (length, length), 0)
            queries = lax.broadcasted_iota(jnp.int32, (length, length), 1)
            same = doc_col[s * length : (s + 1) * length, :] == doc_row[s : s + 1, :]
            mask[s] = jnp.where(same & (keys <= queries), 0.0, MASKED)
        for copy in copies:
            copy.wait()

    def lanes(t):
        return pl.ds(pl.multiple_of(t * half + p * pair, pair), pair)

    w = jnp.concatenate([w_all[:, lanes(t)] for t in range(3)], axis=1)
    wo = o_all[pl.ds(pl.multiple_of(p * pair, pair), pair), :]
    b = jnp.concatenate([bias[:, lanes(t)] for t in range(3)], axis=1)
    mixed = mm(normed[...], w) + b
    cs, lo, hi = cosine[...], sine_low[...], sine_high[...]

    def turn(v, sign):
        return v * cs + sign * (pltpu.roll(v, pair - ROT // 2, 1) * lo + pltpu.roll(v, ROT // 2, 1) * hi)

    scale = HD**-0.5
    q_all = turn(mixed[:, :pair], 1.0).astype(BF)
    k_all = turn(mixed[:, pair : 2 * pair], 1.0).astype(BF)
    v_f32 = mixed[:, 2 * pair :].astype(BF).astype(F32)
    v_all = v_f32.astype(BF)
    q_all = (q_all.astype(F32) * scale).astype(BF)
    gc_all = mm(cot[...], wo, NT).astype(BF)
    lane = lax.broadcasted_iota(jnp.int32, (length, pair), 1)
    first = lane < HD
    zero = jnp.zeros((length, pair), BF)
    part = length // 2
    contexts, mixed_grads = [], []
    for s in range(2):
        row = slice(s * length, (s + 1) * length)
        q, k, v, gc = q_all[row], k_all[row], v_all[row], gc_all[row]
        k_turned = k.astype(F32).T.astype(BF)
        v_turned = v_f32[row].T.astype(BF)
        context_t, query_t, grad_k, grad_v = [], [], [], []
        for h in range(2):
            mine = first if h == 0 else ~first
            qm = jnp.where(mine, q, zero)
            gm = jnp.where(mine, gc, zero)
            rows_h = slice(h * HD, (h + 1) * HD)
            ct, qt = [], []
            dk = dv = None
            for block in range(2):
                kk = part * (block + 1)
                qs = slice(block * part, (block + 1) * part)
                scores = mm(k[:kk], qm[qs], NT) + mask[s, :kk, qs]
                weights = jnp.exp(scores - jnp.max(scores, axis=0, keepdims=True))
                probs = weights * (1.0 / jnp.sum(weights, axis=0, keepdims=True))
                low = probs.astype(BF)
                ct.append(mm(v_turned[rows_h, :kk], low))
                grad_probs = mm(v[:kk], gm[qs], NT)
                inner = jnp.sum(probs * grad_probs, axis=0, keepdims=True)
                ds = (probs * (grad_probs - inner)).astype(BF)
                qt.append(mm(k_turned[rows_h, :kk], ds))
                dv_b = mm(low, gc[qs])
                dk_b = mm(ds, q[qs])
                if block == 0:
                    dv, dk = dv_b, dk_b
                else:
                    dv = jnp.concatenate([dv + dv_b[:part], dv_b[part:]], axis=0)
                    dk = jnp.concatenate([dk + dk_b[:part], dk_b[part:]], axis=0)
            context_t.append(jnp.concatenate(ct, axis=1))
            query_t.append(jnp.concatenate(qt, axis=1))
            grad_k.append(dk)
            grad_v.append(dv)
        contexts.append(jnp.concatenate(context_t, axis=0).T.astype(BF))
        dq = jnp.concatenate(query_t, axis=0).T * scale
        dk = jnp.where(first, grad_k[0], grad_k[1])
        dv = jnp.where(first, grad_v[0], grad_v[1])
        mixed_grads.append((dq, dk, dv))
    context = jnp.concatenate(contexts, axis=0)
    dq, dk, dv = (jnp.concatenate([m[n] for m in mixed_grads], axis=0) for n in range(3))
    grad_mixed = jnp.concatenate([turn(dq, -1.0), turn(dk, -1.0), dv], axis=1).astype(BF)
    total = jnp.sum(grad_mixed.astype(F32), axis=0, keepdims=True)
    for ref, side in ((keep, x), (send, 1 - x)):
        g = mm(normed[:, pl.ds(pl.multiple_of(side * half, half), half)], grad_mixed, TN).astype(BF)
        for t in range(3):
            ref[t, :, pl.ds(pl.multiple_of(p * pair, pair), pair)] = g[:, t * pair : (t + 1) * pair]
    for t in range(3):
        colsum[:, lanes(t)] = total[:, t * pair : (t + 1) * pair]
    g = mm(context, cot[...], TN).astype(BF)
    low_row = pl.multiple_of(lax.rem(p, 2) * pair, pair)

    def store_out(ref):
        for h in range(2):
            ref[3, pl.ds(low_row + h * (half // 2), pair), :] = g[:, h * half : (h + 1) * half]

    @pl.when(p // 2 == x)
    def _():
        store_out(keep)

    @pl.when(p // 2 != x)
    def _():
        store_out(send)

    @pl.when(p == 0)
    def _():
        result[...] = mm(context, wo)
        grad_normed[...] = mm(grad_mixed, w, NT)

    @pl.when(p != 0)
    def _():
        result[...] += mm(context, wo)
        grad_normed[...] += mm(grad_mixed, w, NT)


def norm_kernel(tokens, gains, one, two):
    rows = tokens[...].astype(F32)
    centred = rows - jnp.mean(rows, axis=-1, keepdims=True)
    unit = centred * lax.rsqrt(jnp.mean(centred * centred, axis=-1, keepdims=True) + EPSILON)
    one[...] = (unit * gains[0:1, :] + gains[1:2, :]).astype(BF)
    two[...] = (unit * gains[2:3, :] + gains[3:4, :]).astype(BF)


def tail_kernel(tokens, gains, grad_one, grad_two, sums, send, keep):
    i = pl.program_id(0)
    steps = pl.num_programs(0)
    rows = tokens[...].astype(F32)
    centred = rows - jnp.mean(rows, axis=-1, keepdims=True)
    unit = centred * lax.rsqrt(jnp.mean(centred * centred, axis=-1, keepdims=True) + EPSILON)
    one, two = grad_one[...], grad_two[...]
    part = jnp.concatenate(
        [jnp.sum(v, axis=0, keepdims=True) for v in (one * unit, one, two * unit, two)], axis=0
    )
    pulled = one * gains[0:1, :] + two * gains[2:3, :]

    @pl.when(i == 0)
    def _():
        sums[...] = part

    @pl.when(i != 0)
    def _():
        sums[...] += part

    @pl.when(i < steps // 2)
    def _():
        send[...] = pulled

    @pl.when(i >= steps // 2)
    def _():
        keep[...] = pulled


def halve_kernel(index, keep, recv, send_out, keep_out):
    bit = index[0]
    keep_out[...] = (keep[:, :, bit].astype(F32) + recv[:, :, bit].astype(F32)).astype(BF)
    send_out[...] = (keep[:, :, 1 - bit].astype(F32) + recv[:, :, 1 - bit].astype(F32)).astype(BF)


def widen_kernel(piece, out):
    out[...] = piece[...].astype(F32).reshape(out.shape)


def widen_kernel_at(index, piece, out):
    out[...] = piece[...].astype(F32).reshape(out.shape)


def build(reps):
    bits = reps.bit_length() - 1
    order = list(range(1, bits))

    def flip(array, bit):
        return lax.ppermute(array, "rep", [(i, i ^ (1 << bit)) for i in range(reps)])

    def flip_x(array):
        return lax.ppermute(array, "shard", [(0, 1), (1, 0)])

    def on_device(
        tokens, segments, norm1_gain, norm1_shift, norm2_gain, norm2_shift, qkv_weight, qkv_bias,
        out_weight, out_bias, up_weight, up_bias, down_weight, down_bias, cotangent,
    ):
        half, width = out_weight.shape
        length = tokens.shape[0]
        ff_half = down_weight.shape[0]
        units = ff_half // 2
        toks = 2 * length
        xi = lax.axis_index("shard").astype(jnp.int32)
        ri = lax.axis_index("rep").astype(jnp.int32)
        rbit = [(ri >> b) & 1 for b in range(bits)]
        ci = rbit[0]
        index = jnp.stack([xi, ci, rbit[1], rbit[2]])

        def call(kernel, grid, in_specs, out_specs, out_shape, scratch=(), mib=32, est=None):
            return pl.pallas_call(
                kernel,
                grid_spec=pltpu.PrefetchScalarGridSpec(
                    num_scalar_prefetch=1,
                    grid=grid,
                    in_specs=in_specs,
                    out_specs=out_specs,
                    scratch_shapes=list(scratch),
                ),
                out_shape=out_shape,
                compiler_params=params(mib),
                cost_estimate=est,
            )

        up_part = call(
            pack_up_kernel, (), [ANY], ANY, sds((half // 4, 2 * units), BF),
            [pltpu.SemaphoreType.DMA((2,))],
        )(index, up_weight)
        down_part, rest_part = call(
            pack_rest_kernel, (), [ANY] * 3, [ANY] * 2,
            [sds((units // 4, width), BF), sds((half // 4, 4 * half), BF)],
            [pltpu.SemaphoreType.DMA((9,))],
        )(index, down_weight, qkv_weight, out_weight)

        def fetch(part):
            own = flip_x(part)
            over_y = flip(own, 1)
            return own, over_y, flip(own, 2), flip(over_y, 2)

        def lay(vector, rows, at, total):
            v = vector.astype(F32).reshape(rows, half)
            return jnp.pad(v, ((at, total - at - rows), (0, 0)))

        small_own = (
            lay(norm1_gain, 1, 0, 13) + lay(norm1_shift, 1, 1, 13) + lay(norm2_gain, 1, 2, 13)
            + lay(norm2_shift, 1, 3, 13) + lay(out_bias, 1, 4, 13) + lay(down_bias, 1, 5, 13)
            + lay(qkv_bias, 3, 6, 13) + lay(up_bias, 4, 9, 13)
        )
        small_other = flip_x(small_own)
        tokens_other = flip(tokens, 0)
        up_pieces = fetch(up_part)
        cot_other = flip(cotangent, 0)
        segments_other = flip(segments, 0)
        down_pieces = fetch(down_part)
        rest_pieces = fetch(rest_part)

        low = jnp.where(xi == 0, small_own, small_other)
        high = jnp.where(xi == 0, small_other, small_own)
        gains = jnp.concatenate([low[:6], high[:6]], axis=1)
        qkv_b = jnp.concatenate([low[6:9], high[6:9]], axis=0).reshape(3, 2, 2, half // 2)
        qkv_b = lax.dynamic_index_in_dim(qkv_b, ci, 2, keepdims=False).reshape(1, 3 * half)
        up_b = jnp.concatenate([low[9:13], high[9:13]], axis=0).reshape(2, 2, units)
        up_b = lax.dynamic_index_in_dim(up_b, ci, 1, keepdims=False)
        up_b_own = lax.dynamic_slice_in_dim(up_b, xi, 1, 0)
        up_b_other = lax.dynamic_slice_in_dim(up_b, 1 - xi, 1, 0)

        both = jnp.concatenate([tokens, tokens_other], 0)
        cot = jnp.concatenate([cotangent, cot_other], 0)
        rows = 256
        normed_one, normed_two = pl.pallas_call(
            norm_kernel,
            grid=(toks // rows,),
            in_specs=[pl.BlockSpec((rows, width), lambda i: (i, 0)), held((6, width))],
            out_specs=[pl.BlockSpec((rows, width), lambda i: (i, 0))] * 2,
            out_shape=[sds((toks, width), BF)] * 2,
            compiler_params=params(24),
            cost_estimate=cost(20 * toks * width, 6 * toks * width),
        )(both, gains)

        steps = units // BLOCK
        column = pl.BlockSpec((toks, BLOCK), lambda j, *_: (0, j))
        bias_block = pl.BlockSpec((1, BLOCK), lambda j, *_: (0, j))
        down_block = pl.BlockSpec((2, BLOCK, TILE), lambda j, *_: (j // 2, j % 2, 0))
        up_block = pl.BlockSpec((1, TILE, BLOCK), lambda j, *_: (j // 2, 0, j % 2))
        four = sds((4, TILE, TILE), BF)
        two = sds((2, TILE, TILE), BF)
        unit_act = sds((toks, units), BF)
        full = held((toks, width))
        w_scratch = pltpu.VMEM((width, units), BF)
        one_mm = 2 * toks * width * units
        act_x, slope_x, down_send = call(
            ffn_other_kernel, (steps,), [full, full, bias_block] + [ANY] * 5,
            [column, column, down_block], [unit_act, unit_act, four],
            [w_scratch, pltpu.SemaphoreType.DMA((5,))], 40, cost(2 * one_mm, 14 * MIB),
        )(index, normed_two, cot, up_b_other, up_weight, *up_pieces)
        act_o, hid_o, down_keep, up_send_o, up_keep_o, colsum_o = call(
            ffn_own_kernel, (steps,),
            [full, full, bias_block, pl.BlockSpec((BLOCK, width), lambda j, i: (i[1] * steps + j, 0))] + [ANY] * 5,
            [column, column, down_block, up_block, up_block, bias_block],
            [unit_act, unit_act, four, two, two, sds((1, units), F32)],
            [w_scratch, pltpu.SemaphoreType.DMA((5,))], 40, cost(4 * one_mm, 18 * MIB),
        )(index, normed_two, cot, up_b_own, down_weight, up_weight, *up_pieces)
        hid_x, up_send_x, up_keep_x, colsum_x = call(
            ffn_back_kernel, (steps,), [full, full, column] + [ANY] * 4,
            [column, up_block, up_block, bias_block],
            [unit_act, two, two, sds((1, units), F32)],
            [pltpu.VMEM((units, width), BF), pltpu.SemaphoreType.DMA((4,))], 40, cost(2 * one_mm, 14 * MIB),
        )(index, normed_two, cot, slope_x, *down_pieces)
        token_rows = pl.BlockSpec((rows, units), lambda i, *_: (i, 0))
        token_out = pl.BlockSpec((rows, width), lambda i, *_: (i, 0))
        wide_f32 = sds((toks, width), F32)
        ffn_part, grad_two = call(
            ffn_last_kernel, (toks // rows,), [token_rows] * 4 + [ANY] * 10, [token_out] * 2, [wide_f32] * 2,
            [w_scratch, w_scratch, pltpu.VMEM((units, width), BF), pltpu.VMEM((units, width), BF),
             pltpu.SemaphoreType.DMA((15,))], 40, cost(4 * one_mm, 24 * MIB),
        )(index, act_o, act_x, hid_o, hid_x, down_weight, *down_pieces, up_weight, *up_pieces)

        documents = jnp.concatenate([segments, segments_other], 0)
        before = jnp.sum((documents[:, None, :] < documents[:, :, None]).astype(jnp.int32), axis=2)
        offsets = (jnp.arange(length, dtype=jnp.int32)[None] - before).astype(F32).reshape(toks, 1)
        inverse = 1.0 / 10000.0 ** (jnp.arange(0, ROT, 2, dtype=F32) / ROT)
        angles = offsets * inverse[None, :]
        cos8, sin8 = jnp.cos(angles), jnp.sin(angles)
        rest = jnp.ones((toks, HD - ROT), F32)
        none8 = jnp.zeros((toks, ROT // 2), F32)
        cosine = jnp.concatenate([cos8, cos8, rest] * 2, axis=1)
        sine_low = jnp.concatenate([-sin8, none8, 0.0 * rest] * 2, axis=1)
        sine_high = jnp.concatenate([none8, sin8, 0.0 * rest] * 2, axis=1)

        pair = 2 * HD
        table = held((toks, pair))
        rest_send, rest_keep, grad_one, attn_part, colsum_q = call(
            attention_kernel, (half // pair,),
            [full, full, table, table, table, held((toks, 1)), held((2, length)), held((1, 3 * half))] + [ANY] * 6,
            [held((4, TILE, TILE)), held((4, TILE, TILE)), full, full, held((1, 3 * half))],
            [four, four, wide_f32, wide_f32, sds((1, 3 * half), F32)],
            [pltpu.VMEM((width, 3 * half), BF), pltpu.VMEM((half, width), BF),
             pltpu.VMEM((2, length, length), F32), pltpu.SemaphoreType.DMA((19,))],
            56, cost(13e9 + 20e9, 24 * MIB),
        )(
            index, normed_one, cot, cosine, sine_low, sine_high, documents.reshape(toks, 1), documents, qkv_b,
            qkv_weight, out_weight, *rest_pieces,
        )

        def halve(keep, recv, bit):
            n, r, cols = keep.shape
            m = (reps // 2) >> bit
            small = r // (2 * m)
            view = (n, m, 2, small, cols)
            block = pl.BlockSpec((1, m, 2, small, cols), lambda t, *_: (t, 0, 0, 0, 0))
            out_block = pl.BlockSpec((1, m, small, cols), lambda t, *_: (t, 0, 0, 0))
            send_next, keep_next = call(
                halve_kernel, (n,), [block, block], [out_block] * 2, [sds((n, m, small, cols), BF)] * 2,
                (), 24, cost(2 * n * r * cols, 6 * n * r * cols),
            )(rbit[bit].reshape(1), keep.reshape(view), recv.reshape(view))
            return send_next.reshape(n, r // 2, cols), keep_next.reshape(n, r // 2, cols)

        def reduce_scatter(keep, recv):
            for bit in order:
                send, keep = halve(keep, recv, bit)
                recv = flip(send, bit)
            return (keep.astype(F32) + recv.astype(F32)).astype(BF)

        recv_down = flip_x(down_send)
        recv_up_x = flip_x(up_send_o)
        recv_up_o = flip_x(up_send_x)
        recv_rest = flip_x(rest_send)
        down_piece = reduce_scatter(down_keep, recv_down)
        up_piece_x = reduce_scatter(up_keep_x, recv_up_x)
        up_piece_o = reduce_scatter(up_keep_o, recv_up_o)
        rest_piece = reduce_scatter(rest_keep, recv_rest)
        first_piece = jnp.concatenate([down_piece, up_piece_o, up_piece_x], axis=0)
        r = first_piece.shape[1]
        first = lax.all_gather(first_piece, "rep", axis=0, tiled=False).reshape(reps // 2, 2, 8, r, TILE)
        second = lax.all_gather(rest_piece, "rep", axis=0, tiled=False).reshape(reps // 2, 2, 4, r, TILE)

        many = reps // 2
        down_grad = pl.pallas_call(
            widen_kernel, grid=(2, 2, 2),
            in_specs=[pl.BlockSpec((many, 1, 1, r, TILE), lambda c, i, j: (0, c, 2 * i + j, 0, 0))],
            out_specs=pl.BlockSpec((TILE, TILE), lambda c, i, j: (2 * c + i, j)),
            out_shape=sds((ff_half, width), F32), compiler_params=params(24),
            cost_estimate=cost(ff_half * width, 6 * ff_half * width),
        )(first)
        up_grad = call(
            widen_kernel_at, (2, 2, 2),
            [pl.BlockSpec((many, 1, 1, r, TILE), lambda c, o, j, i: (0, c, 4 + 2 * o + j, 0, 0))],
            pl.BlockSpec((TILE, TILE), lambda c, o, j, i: (0, 4 * (i[0] ^ o) + 2 * c + j)),
            sds((half, 2 * ff_half), F32), (), 24, cost(ff_half * width, 6 * ff_half * width),
        )(index, first)
        qkv_grad = pl.pallas_call(
            widen_kernel, grid=(2, 3, 2),
            in_specs=[pl.BlockSpec((many, 1, 1, r, half // 2), lambda c, t, h: (0, c, t, 0, h))],
            out_specs=pl.BlockSpec((half, half // 2), lambda c, t, h: (0, 4 * t + 2 * h + c)),
            out_shape=sds((half, 6 * half), F32), compiler_params=params(24),
            cost_estimate=cost(half * width, 6 * half * 6 * half),
        )(second)
        out_grad = pl.pallas_call(
            widen_kernel, grid=(2, 2),
            in_specs=[pl.BlockSpec((many // 2, 1, 1, r, TILE), lambda c, h: (h, c, 3, 0, 0))],
            out_specs=pl.BlockSpec((half // 2, half), lambda c, h: (c, h)),
            out_shape=sds((half, width), F32), compiler_params=params(24),
            cost_estimate=cost(half * width, 6 * half * width),
        )(second)

        part = ffn_part + attn_part
        output = (
            tokens.astype(F32) + (part[:length] + flip(part[length:], 0)) + (gains[4:5] + gains[5:6])
        ).astype(BF)
        blocks = toks // rows

        def turned(i):
            return ((i + blocks // 2) % blocks, 0)

        row_block = pl.BlockSpec((rows, width), turned)
        sums, pulled_send, pulled_keep = pl.pallas_call(
            tail_kernel,
            grid=(blocks,),
            in_specs=[row_block, held((6, width)), row_block, row_block],
            out_specs=[
                pl.BlockSpec((4, width), lambda i: (0, 0)),
                pl.BlockSpec((rows, width), lambda i: (jnp.minimum(i, blocks // 2 - 1), 0)),
                pl.BlockSpec((rows, width), lambda i: (jnp.maximum(i - blocks // 2, 0), 0)),
            ],
            out_shape=[sds((4, width), F32), sds((length, width), F32), sds((length, width), F32)],
            compiler_params=params(32),
            cost_estimate=cost(20 * toks * width, 14 * toks * width),
        )(both, gains, grad_one, grad_two)
        pulled = pulled_keep + flip(pulled_send, 0)
        own_rows = tokens.astype(F32)
        centred = own_rows - jnp.mean(own_rows, axis=-1, keepdims=True)
        spread = lax.rsqrt(jnp.mean(centred * centred, axis=-1, keepdims=True) + EPSILON)
        unit = centred * spread
        inward = spread * (
            pulled
            - jnp.mean(pulled, axis=-1, keepdims=True)
            - unit * jnp.mean(pulled * unit, axis=-1, keepdims=True)
        )
        grad_tokens = (cotangent.astype(F32) + inward).astype(BF)

        def spread_core(vector, parts):
            size = vector.size // parts
            v = vector.reshape(parts, 1, size)
            keep = (jnp.arange(2) == ci)[None, :, None]
            return jnp.where(keep, v, 0.0).reshape(-1, width)

        column_sum = jnp.sum(cotangent.astype(F32), axis=0, keepdims=True)
        colsum_up = jnp.where(
            xi == 0, jnp.concatenate([colsum_o, colsum_x], 0), jnp.concatenate([colsum_x, colsum_o], 0)
        )
        small = jnp.concatenate([sums, column_sum, spread_core(colsum_q, 6), spread_core(colsum_up, 2)], axis=0)
        small = small + flip_x(small)
        for bit in range(bits):
            small = small + flip(small, bit)

        def owned(row, count=1):
            v = small[row : row + count].reshape(2, -1)
            return lax.dynamic_index_in_dim(v, xi, 0, keepdims=False)

        bias_out = owned(4)
        return (
            output, grad_tokens, owned(0), owned(1), owned(2), owned(3), qkv_grad, owned(5, 3),
            out_grad, bias_out, up_grad, owned(8, 4), down_grad, bias_out,
        )

    return on_device


def solution(mesh):
    both = P(("rep", "shard"), None)
    vector = P("shard")
    matrix = P("shard", None)
    weights = (
        vector, vector, vector, vector, matrix, vector, matrix, vector, matrix, vector, matrix, vector,
    )
    return jax.shard_map(
        build(mesh.shape["rep"]),
        mesh=mesh,
        in_specs=(both, both) + weights + (both,),
        out_specs=(both, both) + weights,
        check_vma=False,
    )
```

```python
from functools import partial

import jax
import jax.numpy as jnp
from jax import lax
from jax.experimental import pallas as pl
from jax.experimental.pallas import tpu as pltpu
from jax.sharding import PartitionSpec as P

HD = 64
ROT = 16
EPSILON = 1e-05
MASKED = -1e30
BF = jnp.bfloat16
F32 = jnp.float32
TILE = 512
MIB = 1 << 20
NN = (((1,), (0,)), ((), ()))
NT = (((1,), (1,)), ((), ()))
TN = (((0,), (0,)), ((), ()))


def mm(left, right, dims=NN):
    return lax.dot_general(left, right, dims, preferred_element_type=F32)


def cost(flops, nbytes):
    return pl.CostEstimate(flops=int(flops), bytes_accessed=int(nbytes), transcendentals=0)


def params():
    return pltpu.CompilerParams(vmem_limit_bytes=62 * MIB)


ANY = pl.BlockSpec(memory_space=pltpu.HBM)


def held(shape):
    return pl.BlockSpec(shape, lambda *_: (0,) * len(shape), pipeline_mode=pl.Buffered(1))


def sds(shape, kind):
    return jax.ShapeDtypeStruct(shape, kind)


def copy_all(pairs, sems, first=0):
    copies = [pltpu.make_async_copy(a, b, sems.at[first + n]) for n, (a, b) in enumerate(pairs)]
    for c in copies:
        c.start()
    for c in copies:
        c.wait()


def place(index):
    return index[0], index[1], index[2], index[3]


def quarters(index):
    _, _, y, z = place(index)
    return (2 * y + z, 2 * (1 - y) + z, 2 * y + (1 - z), 2 * (1 - y) + (1 - z))


def pack_up_kernel(index, first, second, first_out, second_out):
    first_out[...] = first[...]
    second_out[...] = second[...]


def pack_kernel(index, *refs):
    ins, outs = refs[:16], refs[16:]
    for n in range(2):
        down, *qkv, out_w = ins[8 * n : 8 * n + 8]
        down_out, rest_out = outs[2 * n : 2 * n + 2]
        down_out[...] = down[...]
        wide = qkv[0].shape[1]
        for m, piece in enumerate(qkv):
            rest_out[:, m * wide : (m + 1) * wide] = piece[...]
        rows, width = out_w.shape
        for h in range(2):
            rest_out[h * rows : (h + 1) * rows, 6 * wide :] = out_w[:, h * (width // 2) : (h + 1) * (width // 2)]


def touch_kernel(index, *refs):
    pass


def up_pairs(index, weight, pieces, dest, side):
    x, c, y, _ = place(index)
    half = weight.shape[0]
    rows = half // 2
    wide = weight.shape[1] // 4
    pairs = [
        (
            weight.at[:, pl.ds(pl.multiple_of((2 * side + c) * wide, wide), wide)],
            dest.at[pl.ds(pl.multiple_of(x * half, half), half)],
        )
    ]
    for q, piece in zip((y, 1 - y), pieces):
        pairs.append((piece, dest.at[pl.ds(pl.multiple_of((1 - x) * half + q * rows, rows), rows)]))
    return pairs


BLOCK = 512


def gelu_parts(hidden):
    cdf = 0.5 * (1.0 + lax.erf(hidden * (0.5**0.5)))
    slope = cdf + hidden * jnp.exp(-0.5 * hidden * hidden) * ((2.0 * jnp.pi) ** -0.5)
    return (hidden * cdf).astype(BF), slope


def by_bit(ref, rows, bit, parts):
    for k, part in enumerate(parts):
        for n in range(ref.shape[0] // (2 * rows)):
            here = pl.ds(pl.multiple_of((2 * n + (bit ^ k)) * rows, rows), rows)
            yield k, n, part, ref[here, :]


def ffn_other_kernel(
    index, normed, cot, bias, weight, p0, p1, act, slope, a_send, b_keep, b_send, w_all, g_all, sems
):
    x, _, y, _ = place(index)
    j = pl.program_id(0)

    @pl.when(j == 0)
    def _():
        copy_all(up_pairs(index, weight, (p0, p1), w_all, 1 - x), sems)

    w = w_all[:, pl.ds(pl.multiple_of(j * BLOCK, BLOCK), BLOCK)]
    hidden = mm(normed[...], w) + bias[...]
    a, s = gelu_parts(hidden)
    act[...] = a
    slope[...] = s.astype(BF)
    g = mm(a, cot[...], TN).astype(BF)

    @pl.when(j == 0)
    def _():
        for t in range(2):
            a_send[t] = g[:, t * TILE : (t + 1) * TILE]

    @pl.when(j == 1)
    def _():
        g_all[...] = g
        for _k, _n, part, half in by_bit(g_all, TILE // 2, y, (b_keep, b_send)):
            for t in range(2):
                part[t] = half[:, t * TILE : (t + 1) * TILE]


def ffn_own_kernel(
    index, normed, normed_t, cot, bias, down, weight, p0, p1, other_keep, other_send,
    act, hid, a_keep, b_keep, b_send, up_keep, up_send, colsum, w_all, g_all, u_all, sems,
):
    x, _, y, z = place(index)
    j = pl.program_id(0)

    @pl.when(j == 0)
    def _():
        copy_all(up_pairs(index, weight, (p0, p1), w_all, x), sems)

    w = w_all[:, pl.ds(pl.multiple_of(j * BLOCK, BLOCK), BLOCK)]
    hidden = mm(normed[...], w) + bias[...]
    a, s = gelu_parts(hidden)
    act[...] = a
    g = mm(a, cot[...], TN).astype(BF)

    @pl.when(j == 0)
    def _():
        for t in range(2):
            a_keep[t] = g[:, t * TILE : (t + 1) * TILE]

    @pl.when(j == 1)
    def _():
        g_all[...] = g
        for _k, _n, part, half in by_bit(g_all, TILE // 2, y, (b_keep, b_send)):
            for t in range(2):
                part[2 + t] = half[:, t * TILE : (t + 1) * TILE]
        b_keep[:2] = other_keep[...]
        b_send[:2] = other_send[...]

    low = (mm(cot[...], down[...], NT) * s).astype(BF)
    hid[...] = low
    colsum[...] = jnp.sum(low.astype(F32), axis=0, keepdims=True)
    u_all[...] = mm(normed_t[...], low).astype(BF)
    for _k, n, part, half in by_bit(u_all, up_keep.shape[3], z, (up_keep, up_send)):
        part[0, n // 2, n % 2] = half


def ffn_back_kernel(
    index, normed_t, cot, slope, d0, d1, d2, d3, hid, up_keep, up_send, colsum, d_all, u_all, sems
):
    z = index[3]
    j = pl.program_id(0)
    rows = d0.shape[0]

    @pl.when(j == 0)
    def _():
        copy_all(
            [
                (piece, d_all.at[pl.ds(pl.multiple_of(q * rows, rows), rows)])
                for q, piece in zip(quarters(index), (d0, d1, d2, d3))
            ],
            sems,
        )

    d = d_all[pl.ds(pl.multiple_of(j * BLOCK, BLOCK), BLOCK), :]
    low = (mm(cot[...], d, NT) * slope[...].astype(F32)).astype(BF)
    hid[...] = low
    colsum[...] = jnp.sum(low.astype(F32), axis=0, keepdims=True)
    u_all[...] = mm(normed_t[...], low).astype(BF)
    for _k, n, part, half in by_bit(u_all, up_keep.shape[3], z, (up_keep, up_send)):
        part[0, n // 2, n % 2] = half


def qkv_pairs(index, group, qkv, pieces, dest):
    x, c, _, _ = place(index)
    half = qkv.shape[0]
    quarter, wide = half // 4, half // 2
    own = pl.ds(pl.multiple_of(x * half, half), half)
    pairs = []
    for t in range(3):
        col = pl.multiple_of((4 * t + 2 * group + c) * wide, wide)
        pairs.append((qkv.at[:, pl.ds(col, wide)], dest.at[own, pl.ds(t * wide, wide)]))
    for q, piece in zip(quarters(index), pieces):
        row = pl.ds(pl.multiple_of((1 - x) * half + q * quarter, quarter), quarter)
        for t in range(3):
            pairs.append((piece.at[:, pl.ds((2 * t + group) * wide, wide)], dest.at[row, pl.ds(t * wide, wide)]))
    return pairs


def load_out(index, group, out_w, pieces, dest, sems, first):
    x, c, _, _ = place(index)
    half = out_w.shape[0]
    eighth, wide = half // 8, half // 2

    @pl.when(x == group)
    def _():
        copy_all([(out_w.at[pl.ds(pl.multiple_of(c * wide, wide), wide)], dest)], sems, first)

    @pl.when(x != group)
    def _():
        pairs = []
        for q, piece in zip(quarters(index), pieces):
            row = pl.ds(pl.multiple_of(q * eighth, eighth), eighth)
            for h in range(2):
                source = piece.at[pl.ds(h * eighth, eighth), pl.ds(3 * half, half)]
                pairs.append((source, dest.at[row, pl.ds(h * half, half)]))
        copy_all(pairs, sems, first + 1)


def attention_kernel(
    group, index, normed, normed_t, cot, cosine, sine_low, sine_high, doc_col, doc_row, bias,
    qkv, out_w, p0, p1, p2, p3, *refs
):
    if group == 0:
        send, keep, out_grad, context_out, mixed_out, colsum, w_all, o_all, mask, sems = refs
    else:
        early, send, keep, out_send, out_keep, context_out, mixed_out, colsum, w_all, o_all, mask, late, sems = refs
        out_grad = late
    x, c, y, _ = place(index)
    half = qkv.shape[0]
    wide = half // 2
    pair = 2 * HD
    length = doc_row.shape[1]

    def prepare():
        pairs = qkv_pairs(index, group, qkv, (p0, p1, p2, p3), w_all)
        copies = [pltpu.make_async_copy(a, b, sems.at[n]) for n, (a, b) in enumerate(pairs)]
        for copy in copies:
            copy.start()
        load_out(index, group, out_w, (p0, p1, p2, p3), o_all, sems, len(pairs))
        for s in range(2):
            keys = lax.broadcasted_iota(jnp.int32, (length, length), 0)
            queries = lax.broadcasted_iota(jnp.int32, (length, length), 1)
            same = doc_col[s * length : (s + 1) * length, :] == doc_row[s : s + 1, :]
            mask[s] = jnp.where(same & (keys <= queries), 0.0, MASKED)
        for copy in copies:
            copy.wait()

    prepare()
    for p in range(wide // pair):
        def lanes(t, p=p):
            return pl.ds(t * wide + p * pair, pair)

        w = jnp.concatenate([w_all[:, lanes(t)] for t in range(3)], axis=1)
        wo = o_all[pl.ds(p * pair, pair), :]
        b = jnp.concatenate([bias[:, lanes(t)] for t in range(3)], axis=1)
        mixed = mm(normed[...], w) + b
        cs, lo, hi = cosine[...], sine_low[...], sine_high[...]

        def turn(v, sign):
            return v * cs + sign * (pltpu.roll(v, pair - ROT // 2, 1) * lo + pltpu.roll(v, ROT // 2, 1) * hi)

        scale = HD**-0.5
        q_all = turn(mixed[:, :pair], 1.0).astype(BF)
        k_all = turn(mixed[:, pair : 2 * pair], 1.0).astype(BF)
        v_f32 = mixed[:, 2 * pair :].astype(BF).astype(F32)
        v_all = v_f32.astype(BF)
        q_all = (q_all.astype(F32) * scale).astype(BF)
        gc_all = mm(cot[...], wo, NT).astype(BF)
        lane = lax.broadcasted_iota(jnp.int32, (length, pair), 1)
        first = lane < HD
        zero = jnp.zeros((length, pair), BF)
        part = length // 2
        contexts, contexts_t, mixed_grads = [], [], []
        for s in range(2):
            row = slice(s * length, (s + 1) * length)
            q, k, v, gc = q_all[row], k_all[row], v_all[row], gc_all[row]
            k_turned = k.astype(F32).T.astype(BF)
            v_turned = v_f32[row].T.astype(BF)
            context_t, query_t, grad_k, grad_v = [], [], [], []
            for h in range(2):
                mine = first if h == 0 else ~first
                qm = jnp.where(mine, q, zero)
                gm = jnp.where(mine, gc, zero)
                rows_h = slice(h * HD, (h + 1) * HD)
                ct, qt = [], []
                dk = dv = None
                for block in range(2):
                    kk = part * (block + 1)
                    qs = slice(block * part, (block + 1) * part)
                    scores = mm(k[:kk], qm[qs], NT) + mask[s, :kk, qs]
                    weights = jnp.exp(scores - jnp.max(scores, axis=0, keepdims=True))
                    probs = weights * (1.0 / jnp.sum(weights, axis=0, keepdims=True))
                    low = probs.astype(BF)
                    ct.append(mm(v_turned[rows_h, :kk], low))
                    grad_probs = mm(v[:kk], gm[qs], NT)
                    inner = jnp.sum(probs * grad_probs, axis=0, keepdims=True)
                    ds = (probs * (grad_probs - inner)).astype(BF)
                    qt.append(mm(k_turned[rows_h, :kk], ds))
                    dv_b = mm(low, gc[qs])
                    dk_b = mm(ds, q[qs])
                    if block == 0:
                        dv, dk = dv_b, dk_b
                    else:
                        dv = jnp.concatenate([dv + dv_b[:part], dv_b[part:]], axis=0)
                        dk = jnp.concatenate([dk + dk_b[:part], dk_b[part:]], axis=0)
                context_t.append(jnp.concatenate(ct, axis=1))
                query_t.append(jnp.concatenate(qt, axis=1))
                grad_k.append(dk)
                grad_v.append(dv)
            turned = jnp.concatenate(context_t, axis=0)
            contexts.append(turned.T.astype(BF))
            contexts_t.append(turned.astype(BF))
            dq = jnp.concatenate(query_t, axis=0).T * scale
            dk = jnp.where(first, grad_k[0], grad_k[1])
            dv = jnp.where(first, grad_v[0], grad_v[1])
            mixed_grads.append((dq, dk, dv))
        context = jnp.concatenate(contexts, axis=0)
        dq, dk, dv = (jnp.concatenate([m[n] for m in mixed_grads], axis=0) for n in range(3))
        grad_mixed = jnp.concatenate([turn(dq, -1.0), turn(dk, -1.0), dv], axis=1).astype(BF)
        total = jnp.sum(grad_mixed.astype(F32), axis=0, keepdims=True)
        place_p = pl.ds(p * pair, pair)
        context_out[:, place_p] = context
        for t in range(3):
            mixed_out[:, lanes(t)] = grad_mixed[:, t * pair : (t + 1) * pair]
            colsum[:, lanes(t)] = total[:, t * pair : (t + 1) * pair]
        if group == 0:
            for ref, side in ((keep, x), (send, 1 - x)):
                g = mm(normed_t[pl.ds(pl.multiple_of(side * half, half), half), :], grad_mixed).astype(BF)
                for t in range(3):
                    ref[t, :, place_p] = g[:, t * pair : (t + 1) * pair]
        else:
            for ref, side in ((keep, y), (send, 1 - y)):
                for xr in range(2):
                    rows = pl.ds(pl.multiple_of(xr * half + side * wide, wide), wide)
                    g = mm(normed_t[rows, :], grad_mixed).astype(BF)
                    for t in range(3):
                        ref[t, xr, :, place_p] = g[:, t * pair : (t + 1) * pair]
        g = mm(jnp.concatenate(contexts_t, axis=1), cot[...]).astype(BF)
        for h in range(2):
            for cc in range(2):
                start = h * half + cc * wide
                out_grad[cc, pl.ds(h * wide + p * pair, pair), :] = g[:, start : start + wide]

    if group == 1:

        @pl.when(x == 0)
        def _():
            out_send[...] = late[...]
            out_keep[...] = early[...]

        @pl.when(x == 1)
        def _():
            out_send[...] = early[...]
            out_keep[...] = late[...]


def norm_kernel(index, tokens, other, cot, cot_other, gains, one, two, one_t, two_t, cot_out):
    mine = pl.program_id(0) < pl.num_programs(0) // 2
    rows = jnp.where(mine, tokens[...], other[...]).astype(F32)
    centred = rows - jnp.mean(rows, axis=-1, keepdims=True)
    unit = centred * lax.rsqrt(jnp.mean(centred * centred, axis=-1, keepdims=True) + EPSILON)
    first = unit * gains[0:1, :] + gains[1:2, :]
    second = unit * gains[2:3, :] + gains[3:4, :]
    one[...] = first.astype(BF)
    two[...] = second.astype(BF)
    one_t[...] = first.T.astype(BF)
    two_t[...] = second.T.astype(BF)
    cot_out[...] = jnp.where(mine, cot[...], cot_other[...])


def dense_ffn_kernel(
    index, act_o, act_x, hid_o, hid_x, down, d0, d1, d2, d3, up, p0, p1, q0, q1,
    out, grad, w_o, w_x, d_o, d_x, sems,
):
    x, c = index[0], index[1]
    i = pl.program_id(0)
    rows_d, wide = d0.shape[0], d_o.shape[0]
    for_down = [(down.at[pl.ds(pl.multiple_of(c * wide, wide), wide)], d_o)]
    for q, piece in zip(quarters(index), (d0, d1, d2, d3)):
        for_down.append((piece, d_x.at[pl.ds(pl.multiple_of(q * rows_d, rows_d), rows_d)]))
    for_up = up_pairs(index, up, (p0, p1), w_x, 1 - x) + up_pairs(index, up, (q0, q1), w_o, x)
    copies = [pltpu.make_async_copy(a, b, sems.at[n]) for n, (a, b) in enumerate(for_down + for_up)]

    @pl.when(i == 0)
    def _():
        for copy in copies:
            copy.start()
        for copy in copies[: len(for_down)]:
            copy.wait()

    out[...] = mm(act_o[...], d_o[...]) + mm(act_x[...], d_x[...])

    @pl.when(i == 0)
    def _():
        for copy in copies[len(for_down) :]:
            copy.wait()

    grad[...] = mm(hid_o[...], w_o[...], NT) + mm(hid_x[...], w_x[...], NT)


def dense_last_kernel(
    index, tokens, gains, ffn, grad_two, context_a, context_b, mixed_a, mixed_b, qkv, out_w, r0, r1, r2, r3,
    sums, pulled_send, pulled_keep, part_send, part_keep, m_a, m_b, o_a, o_b, sems,
):
    i = pl.program_id(0)
    steps = pl.num_programs(0)
    rest = (r0, r1, r2, r3)
    pairs = qkv_pairs(index, 0, qkv, rest, m_a) + qkv_pairs(index, 1, qkv, rest, m_b)
    copies = [pltpu.make_async_copy(a, b, sems.at[n]) for n, (a, b) in enumerate(pairs)]

    @pl.when(i == 0)
    def _():
        for copy in copies:
            copy.start()
        load_out(index, 0, out_w, rest, o_a, sems, len(pairs))
        load_out(index, 1, out_w, rest, o_b, sems, len(pairs))

    part = ffn[...] + mm(context_a[...], o_a[...]) + mm(context_b[...], o_b[...])

    @pl.when(i == 0)
    def _():
        for copy in copies:
            copy.wait()

    two = grad_two[...]
    one = mm(mixed_a[...], m_a[...], NT) + mm(mixed_b[...], m_b[...], NT)
    rows = tokens[...].astype(F32)
    centred = rows - jnp.mean(rows, axis=-1, keepdims=True)
    unit = centred * lax.rsqrt(jnp.mean(centred * centred, axis=-1, keepdims=True) + EPSILON)
    sums_here = jnp.concatenate(
        [jnp.sum(v, axis=0, keepdims=True) for v in (one * unit, one, two * unit, two)], axis=0
    )
    pulled = one * gains[0:1, :] + two * gains[2:3, :]

    @pl.when(i == 0)
    def _():
        sums[...] = sums_here

    @pl.when(i != 0)
    def _():
        sums[...] += sums_here

    @pl.when(i < steps // 2)
    def _():
        pulled_send[...] = pulled
        part_send[...] = part

    @pl.when(i >= steps // 2)
    def _():
        pulled_keep[...] = pulled
        part_keep[...] = part


def last_kernel(tokens, cot, gains, pulled_keep, pulled_recv, part_keep, part_recv, out, grad):
    rows = tokens[...].astype(F32)
    centred = rows - jnp.mean(rows, axis=-1, keepdims=True)
    spread = lax.rsqrt(jnp.mean(centred * centred, axis=-1, keepdims=True) + EPSILON)
    unit = centred * spread
    pulled = pulled_keep[...] + pulled_recv[...]
    inward = spread * (
        pulled
        - jnp.mean(pulled, axis=-1, keepdims=True)
        - unit * jnp.mean(pulled * unit, axis=-1, keepdims=True)
    )
    grad[...] = (cot[...].astype(F32) + inward).astype(BF)
    out[...] = (rows + (part_keep[...] + part_recv[...]) + (gains[4:5, :] + gains[5:6, :])).astype(BF)


def tables_kernel(index, doc_col, doc_row, inverse, cosine, sine_low, sine_high):
    length = doc_row.shape[1]
    lane = lax.broadcasted_iota(jnp.int32, (length, 2 * HD), 1) % HD
    for s in range(2):
        rows = slice(s * length, (s + 1) * length)
        before = jnp.sum((doc_row[s : s + 1, :] < doc_col[rows, :]).astype(F32), axis=1, keepdims=True)
        offsets = lax.broadcasted_iota(jnp.int32, (length, 1), 0).astype(F32) - before
        angles = offsets * inverse[...]
        sine = jnp.sin(angles)
        cosine[rows, :] = jnp.where(lane < ROT, jnp.cos(angles), 1.0)
        sine_low[rows, :] = jnp.where(lane < ROT // 2, -sine, 0.0)
        sine_high[rows, :] = jnp.where((lane >= ROT // 2) & (lane < ROT), sine, 0.0)


def split_kernel(groups, index, *refs):
    outs = refs[sum(count for count, _ in groups) :]
    at = used = 0
    for g, (count, n) in enumerate(groups):
        addends = refs[used : used + count]
        used += count
        for t in range(n):
            for k, out in enumerate(outs):
                side = index[g] ^ k
                total = addends[0][t, side].astype(F32)
                for ref in addends[1:]:
                    total += ref[t, side].astype(F32)
                out[at] = total.astype(BF)
            at += 1


def stack_kernel(index, *refs):
    *pieces, out = refs
    for n, piece in enumerate(pieces):
        out[n] = piece[...]


def place_rows(index, y_rel, z_rel, rows, many):
    row = ((y_rel ^ index[2]) * many + (z_rel ^ index[4])) * rows
    return pl.ds(pl.multiple_of(row, rows), rows)


def join_kernel(index, down_keep, down_recv, up_keep, up_recv, c_keep, c_recv, out):
    half = c_keep.shape[2]
    for t in range(4):
        out[t] = (down_keep[t].astype(F32) + down_recv[t].astype(F32)).astype(BF)
        out[4 + t] = (up_keep[t].astype(F32) + up_recv[t ^ 2].astype(F32)).astype(BF)
        for n, c in enumerate((t, 3 + t) if t < 3 else (6, 7)):
            out[8 + t, :, n * half : (n + 1) * half] = (c_keep[c].astype(F32) + c_recv[c].astype(F32)).astype(BF)


def sum_kernel(index, one, two, out):
    out[...] = one[...] + two[...]


def reverse(k, count):
    out = 0
    while count > 1:
        out, k, count = 2 * out + k % 2, k // 2, count // 2
    return out


def widen_kernel(index, piece, down, up, qkv, out, slots, sems):
    many, _, _, _, rows, _ = piece.shape
    x = index[0]
    c = pl.program_id(0)
    quarter = TILE // 2

    def moves(job, core):
        slot = slots.at[job % 3]
        if job < 2:
            row = pl.multiple_of((2 * core + job) * TILE, TILE)
            return [(slot, down.at[pl.ds(row, TILE), :])]
        if job < 4:
            col = pl.multiple_of((4 * (x ^ (job - 2)) + 2 * core) * TILE, TILE)
            return [(slot, up.at[:, pl.ds(col, 2 * TILE)])]
        pairs = []
        for n in range(2 if job == 4 else 1):
            for g in range(2):
                col = pl.multiple_of((4 * (2 * (job - 4) + n) + 2 * g + core) * quarter, quarter)
                pairs.append((slot.at[:, pl.ds(n * TILE + g * quarter, quarter)], qkv.at[:, pl.ds(col, quarter)]))
        if job == 5:
            row = pl.multiple_of(core * quarter, quarter)
            for h in range(2):
                pairs.append(
                    (slot.at[pl.ds(h * quarter, quarter), pl.ds(TILE, TILE)], out.at[pl.ds(row, quarter), pl.ds(h * TILE, TILE)])
                )
        return pairs

    def copies(job, core):
        return [pltpu.make_async_copy(a, b, sems.at[job % 3, n]) for n, (a, b) in enumerate(moves(job, core))]

    def settle(job, core):
        for copy in copies(job, core):
            copy.wait()

    for job in range(6):
        if job < 3:

            @pl.when(c > 0)
            def _(job=job):
                settle(job + 3, c - 1)

        else:
            settle(job - 3, c)
        tiles = (2 * job, 2 * job + 1)
        for n, tile in enumerate(tiles):
            for y in range(2):
                for z in range(many):
                    row = (y * many + reverse(z, many)) * rows
                    slots[job % 3, row : row + rows, n * TILE : (n + 1) * TILE] = piece[z, y, 0, tile].astype(F32)
        for copy in copies(job, c):
            copy.start()

    @pl.when(c == pl.num_programs(0) - 1)
    def _():
        for job in range(3, 6):
            settle(job, c)


def build(reps):
    bits = reps.bit_length() - 1
    many = reps // 4

    def flip(array, bit):
        return lax.ppermute(array, "rep", [(i, i ^ (1 << bit)) for i in range(reps)])

    def hop(array, k):
        return lax.ppermute(array, "rep", [(i, i ^ (k << 2)) for i in range(reps)])

    def flip_x(array):
        return lax.ppermute(array, "shard", [(0, 1), (1, 0)])

    def call(kernel, grid, in_specs, out_specs, out_shape, scratch=(), est=None, after=(), aliases=()):
        n_in, n_after, n_out = len(in_specs), len(after), len(out_shape)

        def wrapped(index, *refs):
            rest = refs[n_in + n_after :]
            kernel(index, *refs[:n_in], *rest[:n_out], *rest[n_out + 1 :])
            rest[n_out][...] = jnp.zeros((8, 128), F32)

        run = pl.pallas_call(
            wrapped,
            grid_spec=pltpu.PrefetchScalarGridSpec(
                num_scalar_prefetch=1,
                grid=grid,
                in_specs=list(in_specs) + [ANY] * n_after,
                out_specs=list(out_specs) + [pl.BlockSpec((8, 128), lambda *_: (0, 0))],
                scratch_shapes=list(scratch),
            ),
            out_shape=list(out_shape) + [sds((8, 128), F32)],
            compiler_params=params(),
            cost_estimate=est,
            input_output_aliases=dict(aliases),
        )
        return lambda index, *args: run(index, *args, *after)

    def on_device(
        tokens, segments, norm1_gain, norm1_shift, norm2_gain, norm2_shift, qkv_weight, qkv_bias,
        out_weight, out_bias, up_weight, up_bias, down_weight, down_bias, cotangent,
    ):
        half, width = out_weight.shape
        length = tokens.shape[0]
        ff_half = down_weight.shape[0]
        units = ff_half // 2
        toks = 2 * length
        xi = lax.axis_index("shard").astype(jnp.int32)
        ri = lax.axis_index("rep").astype(jnp.int32)
        rbit = [(ri >> b) & 1 for b in range(bits)]
        ci, yi = rbit[0], rbit[1]
        z_order = 0 * ri
        for bit in range(2, bits):
            z_order = 2 * z_order + rbit[bit]
        index = jnp.stack([xi, ci, yi, rbit[2], z_order])

        dma = pltpu.SemaphoreType.DMA
        wide = half // 2
        pair_rows = (half // 2, units)

        def corner(i, n):
            return 2 * (i[2] ^ n) + (i[3] ^ n)

        def from_qkv(n, t, h):
            return pl.BlockSpec((half // 4, wide), lambda g, i: (corner(i, n), 4 * t + 2 * h + i[1]))

        def whole(shape):
            return pl.BlockSpec(shape, lambda *_: (0,) * len(shape))

        up_first, up_second, mark = call(
            pack_up_kernel, (1,),
            [pl.BlockSpec(pair_rows, lambda n, i: (i[2], 2 * i[0] + i[1])),
             pl.BlockSpec(pair_rows, lambda n, i: (i[2], 2 * (1 - i[0]) + i[1]))],
            [whole(pair_rows)] * 2, [sds(pair_rows, BF)] * 2, (), cost(1, 4 * MIB),
        )(index, up_weight, up_weight)

        def touch(arrays, after):
            n = len(arrays)
            shapes = [sds(a.shape, a.dtype) for a in arrays]
            return call(
                touch_kernel, (1,), [ANY] * n, [ANY] * n, shapes, (), cost(1, 1), after, {1 + k: k for k in range(n)}
            )(index, *arrays)

        def lay(vector, at, total):
            return jnp.pad(vector.astype(F32), (at, total - at - vector.shape[0]))

        tokens_other = flip(tokens, 0)
        up_first = flip_x(up_first)
        cot_other = flip(cotangent, 0)
        vectors = [norm1_gain, norm1_shift, norm2_gain, norm2_shift, out_bias, down_bias, qkv_bias, up_bias]
        starts = [sum(v.shape[0] for v in vectors[:n]) for n in range(len(vectors) + 1)]
        small_own = sum(lay(v, s, starts[-1]) for v, s in zip(vectors, starts))
        small_other = flip_x(small_own)
        segments_other = flip(segments, 0)

        low = jnp.where(xi == 0, small_own, small_other).reshape(-1, half)
        high = jnp.where(xi == 0, small_other, small_own).reshape(-1, half)
        gains = jnp.concatenate([low[:6], high[:6]], axis=1)
        qkv_b = jnp.concatenate([low[6:9], high[6:9]], axis=0).reshape(3, 2, 2, wide)
        qkv_b = lax.dynamic_index_in_dim(qkv_b, ci, 2, keepdims=False)
        up_b = jnp.concatenate([low[9:13], high[9:13]], axis=0).reshape(2, 2, units)
        up_b = lax.dynamic_index_in_dim(up_b, ci, 1, keepdims=False)
        up_b_own = lax.dynamic_slice_in_dim(up_b, xi, 1, 0)
        up_b_other = lax.dynamic_slice_in_dim(up_b, 1 - xi, 1, 0)

        rows = 256
        blocks = toks // rows

        def lower(i, *_):
            return (jnp.minimum(i, blocks // 2 - 1), 0)

        def upper_half(i, *_):
            return (jnp.maximum(i - blocks // 2, 0), 0)

        row_out = pl.BlockSpec((rows, width), lambda i, *_: (i, 0))
        column_out = pl.BlockSpec((width, rows), lambda i, *_: (0, i))
        turned_acts = sds((width, toks), BF)
        first_half, second_half = pl.BlockSpec((rows, width), lower), pl.BlockSpec((rows, width), upper_half)
        normed_one, normed_two, one_t, two_t, cot, mark = call(
            norm_kernel, (blocks,), [first_half, second_half] * 2 + [held((6, width))],
            [row_out, row_out, column_out, column_out, row_out],
            [sds((toks, width), BF)] * 2 + [turned_acts] * 2 + [sds((toks, width), BF)], (),
            cost(20 * toks * width, 14 * toks * width), [mark],
        )(index, tokens, tokens_other, cotangent, cot_other, gains)
        up_first, up_second, mark = touch([up_first, up_second], [mark])
        first_pieces = (up_first, flip(up_first, 1))
        up_second = flip_x(up_second)
        part_shapes = [(units // 4, width), (half // 4, 4 * half)] * 2
        in_specs, sources = [], []
        for n in range(2):
            in_specs.append(pl.BlockSpec((units // 4, width), lambda g, i, n=n: (4 * i[1] + corner(i, n), 0)))
            in_specs += [from_qkv(n, t, h) for t in range(3) for h in range(2)]
            in_specs.append(pl.BlockSpec((half // 8, width), lambda g, i, n=n: (4 * i[1] + corner(i, n), 0)))
            sources += [down_weight] + [qkv_weight] * 6 + [out_weight]
        down_part, rest_part, down_far, rest_far, mark = call(
            pack_kernel, (1,), in_specs,
            [whole(s) for s in part_shapes], [sds(s, BF) for s in part_shapes], (), cost(1, 8 * MIB), [mark],
        )(index, *sources)
        down_part, down_far = flip_x(down_part), flip_x(down_far)
        rest_part, rest_far = flip_x(rest_part), flip_x(rest_far)

        documents = jnp.concatenate([segments, segments_other], 0)
        doc_col = documents.reshape(toks, 1)
        pair = 2 * HD
        inverse = 1.0 / 10000.0 ** (jnp.arange(0, ROT, 2, dtype=F32) / ROT)
        inverse = jnp.concatenate([inverse, inverse, jnp.zeros((HD - ROT,), F32)] * 2).reshape(1, pair)
        cosine, sine_low, sine_high, mark = call(
            tables_kernel, (1,), [whole((toks, 1)), whole((2, length)), whole((1, pair))], [whole((toks, pair))] * 3,
            [sds((toks, pair), F32)] * 3, (), cost(100 * toks * pair, 12 * toks * pair), [mark],
        )(index, doc_col, documents, inverse)

        up_second, mark = touch([up_second], [mark])
        second_pieces = (up_second, flip(up_second, 1))
        steps = units // BLOCK
        column = pl.BlockSpec((toks, BLOCK), lambda j, *_: (0, j))
        bias_block = pl.BlockSpec((1, BLOCK), lambda j, *_: (0, j))
        by_z = pl.BlockSpec((1, 2, 2, half // 4, BLOCK), lambda j, *_: (j, 0, 0, 0, 0))
        z_shape = sds((2, 2, 2, half // 4, TILE), BF)
        two_tiles, two_halves = sds((2, TILE, TILE), BF), sds((2, TILE // 2, TILE), BF)
        four_halves = sds((4, TILE // 2, TILE), BF)
        unit_act = sds((toks, units), BF)
        full = held((toks, width))
        w_scratch = pltpu.VMEM((width, units), BF)
        d_scratch = pltpu.VMEM((units, width), BF)
        g_scratch = pltpu.VMEM((width, BLOCK), BF)
        one_mm = 2 * toks * width * units
        act_x, slope_x, da_send, other_keep, other_send, mark = call(
            ffn_other_kernel, (steps,), [full, full, bias_block] + [ANY] * 3,
            [column, column, whole(two_tiles.shape), whole(two_halves.shape), whole(two_halves.shape)],
            [unit_act, unit_act, two_tiles, two_halves, two_halves],
            [w_scratch, pltpu.VMEM((BLOCK, width), BF), dma((3,))], cost(5 * one_mm, 14 * MIB), [mark],
        )(index, normed_two, cot, up_b_other, up_weight, *first_pieces)
        down_part, mark = touch([down_part], [mark])
        down_pieces = (down_part, flip(down_part, 1), flip(down_part, 2), down_far)
        act_o, hid_o, da_keep, db_keep, db_send, uo_keep, uo_send, colsum_o, mark = call(
            ffn_own_kernel, (steps,),
            [full, full, full, bias_block, pl.BlockSpec((BLOCK, width), lambda j, i: (i[1] * steps + j, 0))]
            + [ANY] * 3 + [held(two_halves.shape)] * 2,
            [column, column, whole(two_tiles.shape), whole(four_halves.shape), whole(four_halves.shape), by_z, by_z, bias_block],
            [unit_act, unit_act, two_tiles, four_halves, four_halves, z_shape, z_shape, sds((1, units), F32)],
            [w_scratch, pltpu.VMEM((BLOCK, width), BF), g_scratch, dma((3,))], cost(8 * one_mm, 18 * MIB), [mark],
        )(index, normed_two, two_t, cot, up_b_own, down_weight, up_weight, *second_pieces, other_keep, other_send)
        rest_part, mark = touch([rest_part], [mark])
        rest_pieces = (rest_part, flip(rest_part, 1), flip(rest_part, 2), rest_far)
        da_send, db_send, mark = touch([da_send, db_send], [mark])
        da_recv, db_recv = flip_x(da_send), flip(db_send, 1)
        hid_x, ux_keep, ux_send, colsum_x, mark = call(
            ffn_back_kernel, (steps,), [full, full, column] + [ANY] * 4,
            [column, by_z, by_z, bias_block],
            [unit_act, z_shape, z_shape, sds((1, units), F32)],
            [d_scratch, g_scratch, dma((4,))], cost(4 * one_mm, 14 * MIB), [mark],
        )(index, two_t, cot, slope_x, *down_pieces)
        uo_recv, ux_recv = flip(uo_send, 2), flip(ux_send, 2)

        table = held((toks, pair))
        sum_shape = sds((1, 3 * wide), F32)
        out_tiles = sds((2, half, wide), BF)
        x_tiles = sds((3, half, wide), BF)
        y_tiles = sds((3, 2, wide, wide), BF)
        heads_out = [sds((toks, wide), BF), sds((toks, 3 * wide), BF), sum_shape]

        def attend(group, extra, shapes, scratch, after):
            specs = [full, full, full, table, table, table, held((toks, 1)), held((2, length)), held((1, 3 * wide))]
            return call(
                partial(attention_kernel, group), (1,),
                specs + [ANY] * 6 + [held(e.shape) for e in extra],
                [held(s.shape) for s in shapes], shapes,
                [pltpu.VMEM((width, 3 * wide), BF), pltpu.VMEM((wide, width), BF),
                 pltpu.VMEM((2, length, length), F32)] + scratch + [dma((24,))],
                cost(30e9, 16 * MIB), after,
            )(
                index, normed_one, one_t, cot, cosine, sine_low, sine_high, doc_col, documents,
                qkv_b[:, group].reshape(1, 3 * wide), qkv_weight, out_weight, *rest_pieces, *extra,
            )

        a_send, a_keep, out_early, context_a, mixed_a, colsum_a, mark = attend(
            0, [], [x_tiles, x_tiles, out_tiles] + heads_out, [], [mark]
        )

        def split(groups, ways, after):
            cols = groups[0][0][0].shape[-1]
            small = groups[0][0][0].size // groups[0][1] // cols // ways
            views = [(n, ways, small, cols) for addends, n, _ in groups for _ in addends]
            total = sum(n for _, n, _ in groups)
            out = (total, small, cols)
            return call(
                partial(split_kernel, [(len(addends), n) for addends, n, _ in groups]), (1,),
                [whole(v) for v in views], [whole(out)] * ways, [sds(out, BF)] * ways, (),
                cost(4 * total * small * cols, 12 * total * small * cols), after,
            )(
                jnp.stack([side for _, _, side in groups]),
                *[a.reshape(v) for a, v in zip([a for addends, _, _ in groups for a in addends], views)],
            )

        def add(parts, after):
            n = parts[0].size // parts[0].shape[-1] // parts[0].shape[-2]
            return split([(parts, n, 0 * xi)], 1, after)

        def stack(pieces, after):
            shape = (len(pieces),) + pieces[0].shape
            return call(
                stack_kernel, (1,), [whole(shape[1:])] * len(pieces), [whole(shape)], [sds(shape, BF)], (),
                cost(1, 4 * pieces[0].size * len(pieces)), after,
            )(index, *pieces)

        token_rows = pl.BlockSpec((rows, units), lambda i, *_: (i, 0))
        token_out = pl.BlockSpec((rows, width), lambda i, *_: (i, 0))
        wide_f32 = sds((toks, width), F32)

        def turned(cols):
            return pl.BlockSpec((rows, cols), lambda i, *_: ((i + blocks // 2) % blocks, 0))

        sums_block = pl.BlockSpec((4, width), lambda i, *_: (0, 0))
        send_block, keep_block = pl.BlockSpec((rows, width), lower), pl.BlockSpec((rows, width), upper_half)
        own_f32 = sds((length, width), F32)
        m_scratch = pltpu.VMEM((width, 3 * wide), BF)
        out_scratch = pltpu.VMEM((wide, width), BF)

        def dense_last(i, tokens_ref, other_ref, *refs):
            mine = pl.program_id(0) >= blocks // 2
            dense_last_kernel(i, jnp.where(mine, tokens_ref[...], other_ref[...]), *refs)

        a_recv = flip_x(a_send)
        last_bits = list(range(3, bits))
        one = 1 + 0 * xi

        da_keep, da_send, mark = split([([da_keep, da_recv], 2, yi)], 2, [mark])
        da_recv = flip(da_send, 1)
        db_keep, db_send, mark = split([([db_keep, db_recv], 1, one)], 2, [mark])
        db_recv = flip_x(db_send)
        uo_keep, uo_send, mark = split([([uo_keep, uo_recv], 4, yi)], 2, [mark])
        uo_recv = flip(uo_send, 1)
        b_send, b_keep, out_send, out_keep, context_b, mixed_b, colsum_b, mark = attend(
            1, [out_early], [y_tiles, y_tiles, out_tiles, out_tiles] + heads_out,
            [pltpu.VMEM((2, half, wide), BF)], [mark],
        )
        b_recv = flip(b_send, 1)
        out_recv = flip_x(out_send)
        d_keep, d_send, mark = split([([da_keep, da_recv], 2, rbit[2]), ([db_keep, db_recv], 2, rbit[2])], 2, [mark])
        d_recv = flip(d_send, 2)
        a_keep, a_send, mark = split([([a_keep, a_recv], 3, yi)], 2, [mark])
        a_recv = flip(a_send, 1)
        ux_keep, ux_send, mark = split([([ux_keep, ux_recv], 4, yi)], 2, [mark])
        ux_recv = flip(ux_send, 1)
        for bit in last_bits:
            uo_keep, uo_send, mark = split([([uo_keep, uo_recv], 4, rbit[bit])], 2, [mark])
            uo_recv = flip(uo_send, bit)
        out_keep, out_send, mark = split([([out_keep, out_recv], 2, yi)], 2, [mark])
        out_recv = flip(out_send, 1)
        b_keep, b_send, mark = split([([b_keep, b_recv], 3, xi)], 2, [mark])
        b_recv = flip_x(b_send)
        for bit in last_bits:
            d_keep, d_send, mark = split([([d_keep, d_recv], 4, rbit[bit])], 2, [mark])
            d_recv = flip(d_send, bit)
        for bit in last_bits:
            ux_keep, ux_send, mark = split([([ux_keep, ux_recv], 4, rbit[bit])], 2, [mark])
            ux_recv = flip(ux_send, bit)
        c_keep, c_send, mark = split(
            [([k, v], n, rbit[2]) for k, v, n in ((a_keep, a_recv, 3), (b_keep, b_recv, 3), (out_keep, out_recv, 2))], 2, [mark]
        )
        c_recv = flip(c_send, 2)
        u_keep, u_send, mark = split([([uo_keep, uo_recv], 2, xi), ([ux_keep, ux_recv], 2, xi)], 2, [mark])
        u_recv = flip_x(u_send)
        for bit in last_bits:
            c_keep, c_send, mark = split([([c_keep, c_recv], 8, rbit[bit])], 2, [mark])
            c_recv = flip(c_send, bit)
        r = half // reps * 2
        piece, mark = call(
            join_kernel, (1,), [whole((4, r, TILE))] * 4 + [whole((8, r, wide))] * 2, [whole((12, r, TILE))],
            [sds((12, r, TILE), BF)], (), cost(1, 1), [mark],
        )(index, d_keep, d_recv, u_keep, u_recv, c_keep, c_recv)
        gathered = lax.all_gather(piece, "rep", axis=0, tiled=False).reshape(many, 2, 2, 12, r, TILE)

        ffn_part, grad_two, mark = call(
            dense_ffn_kernel, (blocks,), [token_rows] * 4 + [ANY] * 10, [token_out] * 2, [wide_f32] * 2,
            [w_scratch, w_scratch, d_scratch, d_scratch, dma((15,))], cost(6 * one_mm, 24 * MIB), [mark],
        )(index, act_o, act_x, hid_o, hid_x, down_weight, *down_pieces, up_weight, *first_pieces, *second_pieces)
        sums, pulled_send, pulled_keep, part_send, part_keep, mark = call(
            dense_last, (blocks,),
            [keep_block, send_block, held((6, width)), turned(width), turned(width)] + [turned(wide)] * 2
            + [turned(3 * wide)] * 2 + [ANY] * 6,
            [sums_block, send_block, keep_block, send_block, keep_block],
            [sds((4, width), F32)] + [own_f32] * 4,
            [m_scratch, m_scratch, out_scratch, out_scratch, dma((40,))],
            cost(4 * one_mm, 30 * MIB), [mark],
        )(
            index, tokens, tokens_other, gains, ffn_part, grad_two, context_a, context_b, mixed_a, mixed_b,
            qkv_weight, out_weight, *rest_pieces,
        )
        pulled_recv = flip(pulled_send, 0)
        part_recv = flip(part_send, 0)

        def spread_core(vector, parts):
            size = vector.size // parts
            v = vector.reshape(parts, 1, size)
            keep = (jnp.arange(2) == ci)[None, :, None]
            return jnp.where(keep, v, 0.0).reshape(-1, width)

        column_sum = jnp.sum(cotangent.astype(F32), axis=0, keepdims=True)
        colsum_up = jnp.where(
            xi == 0, jnp.concatenate([colsum_o, colsum_x], 0), jnp.concatenate([colsum_x, colsum_o], 0)
        )
        colsum_q = jnp.stack([colsum_a.reshape(3, wide), colsum_b.reshape(3, wide)], axis=1)
        small = jnp.concatenate([sums, column_sum, spread_core(colsum_q, 6), spread_core(colsum_up, 2)], axis=0)

        def meet(own, other, after):
            return call(
                sum_kernel, (1,), [whole(own.shape)] * 2, [whole(own.shape)], [sds(own.shape, F32)], (), cost(1, 1), after,
            )(index, own, other)

        small, mark = meet(small, flip_x(small), [mark])
        for n in range(bits):
            small, mark = meet(small, flip(small, n), [mark])
            if n == 0:
                output, grad_tokens, mark = call(
                    lambda i, *refs: last_kernel(*refs), (length // rows,),
                    [token_out, token_out, held((6, width))] + [token_out] * 4, [token_out] * 2,
                    [sds((length, width), BF)] * 2, (), cost(40 * length * width, 24 * length * width), [mark],
                )(index, tokens, cotangent, gains, pulled_keep, pulled_recv, part_keep, part_recv)

        down_grad, up_grad, qkv_grad, out_grad, mark = call(
            widen_kernel, (2,), [pl.BlockSpec((many, 2, 1, 12, r, TILE), lambda c, i: (0, 0, c, 0, 0, 0))], [ANY] * 4,
            [sds((ff_half, width), F32), sds((half, 2 * ff_half), F32), sds((half, 6 * half), F32), sds((half, width), F32)],
            [pltpu.VMEM((3, TILE, 2 * TILE), F32), dma((3, 4))], cost(1, 40 * MIB), [mark],
        )(index, gathered)

        def owned(row, count=1):
            v = small[row : row + count].reshape(2, -1)
            return lax.dynamic_index_in_dim(v, xi, 0, keepdims=False)

        bias_out = owned(4)
        return (
            output, grad_tokens, owned(0), owned(1), owned(2), owned(3), qkv_grad, owned(5, 3),
            out_grad, bias_out, up_grad, owned(8, 4), down_grad, bias_out,
        )

    return on_device


def solution(mesh):
    both = P(("rep", "shard"), None)
    vector = P("shard")
    matrix = P("shard", None)
    weights = (
        vector, vector, vector, vector, matrix, vector, matrix, vector, matrix, vector, matrix, vector,
    )
    return jax.shard_map(
        build(mesh.shape["rep"]),
        mesh=mesh,
        in_specs=(both, both) + weights + (both,),
        out_specs=(both, both) + weights,
        check_vma=False,
    )
```

```python
from functools import partial

import jax
import jax.numpy as jnp
from jax import lax
from jax.experimental import pallas as pl
from jax.experimental.pallas import tpu as pltpu
from jax.sharding import PartitionSpec as P

HD = 64
ROT = 16
EPSILON = 1e-05
MASKED = -1e30
BF = jnp.bfloat16
F32 = jnp.float32
TILE = 512
MIB = 1 << 20
NN = (((1,), (0,)), ((), ()))
NT = (((1,), (1,)), ((), ()))
TN = (((0,), (0,)), ((), ()))


def mm(left, right, dims=NN):
    return lax.dot_general(left, right, dims, preferred_element_type=F32)


def cost(flops, nbytes):
    return pl.CostEstimate(flops=int(flops), bytes_accessed=int(nbytes), transcendentals=0)


def params(mib=62):
    return pltpu.CompilerParams(vmem_limit_bytes=mib * MIB)


ANY = pl.BlockSpec(memory_space=pltpu.HBM)


def held(shape):
    return pl.BlockSpec(shape, lambda *_: (0,) * len(shape), pipeline_mode=pl.Buffered(1))


def sds(shape, kind):
    return jax.ShapeDtypeStruct(shape, kind)


def copy_all(pairs, sems, first=0):
    copies = [pltpu.make_async_copy(a, b, sems.at[first + n]) for n, (a, b) in enumerate(pairs)]
    for c in copies:
        c.start()
    for c in copies:
        c.wait()


def place(index):
    return index[0], index[1], index[2], index[3]


def quarters(index):
    _, _, y, z = place(index)
    return (2 * y + z, 2 * (1 - y) + z, 2 * y + (1 - z), 2 * (1 - y) + (1 - z))


def pack_up_kernel(index, first, second, first_out, second_out):
    first_out[...] = first[...]
    second_out[...] = second[...]


def pack_kernel(index, *refs):
    ins, outs = refs[:16], refs[16:]
    for n in range(2):
        down, *qkv, out_w = ins[8 * n : 8 * n + 8]
        down_out, rest_out = outs[2 * n : 2 * n + 2]
        down_out[...] = down[...]
        wide = qkv[0].shape[1]
        for m, piece in enumerate(qkv):
            rest_out[:, m * wide : (m + 1) * wide] = piece[...]
        rows, width = out_w.shape
        for h in range(2):
            rest_out[h * rows : (h + 1) * rows, 6 * wide :] = out_w[:, h * (width // 2) : (h + 1) * (width // 2)]


def touch_kernel(index, *refs):
    pass


def up_pairs(index, weight, pieces, dest, side):
    x, c, y, _ = place(index)
    half = weight.shape[0]
    rows = half // 2
    wide = weight.shape[1] // 4
    pairs = [
        (
            weight.at[:, pl.ds(pl.multiple_of((2 * side + c) * wide, wide), wide)],
            dest.at[pl.ds(pl.multiple_of(x * half, half), half)],
        )
    ]
    for q, piece in zip((y, 1 - y), pieces):
        pairs.append((piece, dest.at[pl.ds(pl.multiple_of((1 - x) * half + q * rows, rows), rows)]))
    return pairs


BLOCK = 512


def gelu_parts(hidden):
    cdf = 0.5 * (1.0 + lax.erf(hidden * (0.5**0.5)))
    slope = cdf + hidden * jnp.exp(-0.5 * hidden * hidden) * ((2.0 * jnp.pi) ** -0.5)
    return (hidden * cdf).astype(BF), slope


def by_bit(ref, rows, bit, parts):
    for k, part in enumerate(parts):
        for n in range(ref.shape[0] // (2 * rows)):
            here = pl.ds(pl.multiple_of((2 * n + (bit ^ k)) * rows, rows), rows)
            yield k, n, part, ref[here, :]


def ffn_other_kernel(
    index, normed, cot, bias, weight, p0, p1, act, slope, a_send, b_keep, b_send, w_all, g_all, sems
):
    x, _, y, _ = place(index)
    j = pl.program_id(0)

    @pl.when(j == 0)
    def _():
        copy_all(up_pairs(index, weight, (p0, p1), w_all, 1 - x), sems)

    w = w_all[:, pl.ds(pl.multiple_of(j * BLOCK, BLOCK), BLOCK)]
    hidden = mm(normed[...], w) + bias[...]
    a, s = gelu_parts(hidden)
    act[...] = a
    slope[...] = s.astype(BF)
    g = mm(a, cot[...], TN).astype(BF)

    @pl.when(j == 0)
    def _():
        for t in range(2):
            a_send[t] = g[:, t * TILE : (t + 1) * TILE]

    @pl.when(j == 1)
    def _():
        g_all[...] = g
        for _k, _n, part, half in by_bit(g_all, TILE // 2, y, (b_keep, b_send)):
            for t in range(2):
                part[t] = half[:, t * TILE : (t + 1) * TILE]


def ffn_own_kernel(
    index, normed, normed_t, cot, bias, down, weight, p0, p1, other_keep, other_send,
    act, hid, a_keep, b_keep, b_send, up_keep, up_send, colsum, w_all, g_all, u_all, sems,
):
    x, _, y, z = place(index)
    j = pl.program_id(0)

    @pl.when(j == 0)
    def _():
        copy_all(up_pairs(index, weight, (p0, p1), w_all, x), sems)

    w = w_all[:, pl.ds(pl.multiple_of(j * BLOCK, BLOCK), BLOCK)]
    hidden = mm(normed[...], w) + bias[...]
    a, s = gelu_parts(hidden)
    act[...] = a
    g = mm(a, cot[...], TN).astype(BF)

    @pl.when(j == 0)
    def _():
        for t in range(2):
            a_keep[t] = g[:, t * TILE : (t + 1) * TILE]

    @pl.when(j == 1)
    def _():
        g_all[...] = g
        for _k, _n, part, half in by_bit(g_all, TILE // 2, y, (b_keep, b_send)):
            for t in range(2):
                part[2 + t] = half[:, t * TILE : (t + 1) * TILE]
        b_keep[:2] = other_keep[...]
        b_send[:2] = other_send[...]

    low = (mm(cot[...], down[...], NT) * s).astype(BF)
    hid[...] = low
    colsum[...] = jnp.sum(low.astype(F32), axis=0, keepdims=True)
    u_all[...] = mm(normed_t[...], low).astype(BF)
    for _k, n, part, half in by_bit(u_all, up_keep.shape[3], z, (up_keep, up_send)):
        part[0, n // 2, n % 2] = half


def ffn_back_kernel(
    index, normed_t, cot, slope, d0, d1, d2, d3, hid, up_keep, up_send, colsum, d_all, u_all, sems
):
    y = index[2]
    j = pl.program_id(0)
    rows = d0.shape[0]

    @pl.when(j == 0)
    def _():
        copy_all(
            [
                (piece, d_all.at[pl.ds(pl.multiple_of(q * rows, rows), rows)])
                for q, piece in zip(quarters(index), (d0, d1, d2, d3))
            ],
            sems,
        )

    d = d_all[pl.ds(pl.multiple_of(j * BLOCK, BLOCK), BLOCK), :]
    low = (mm(cot[...], d, NT) * slope[...].astype(F32)).astype(BF)
    hid[...] = low
    colsum[...] = jnp.sum(low.astype(F32), axis=0, keepdims=True)
    u_all[...] = mm(normed_t[...], low).astype(BF)
    for _k, n, part, half in by_bit(u_all, up_keep.shape[2], y, (up_keep, up_send)):
        part[0, n] = half


def qkv_pairs(index, group, qkv, pieces, dest):
    x, c, _, _ = place(index)
    half = qkv.shape[0]
    quarter, wide = half // 4, half // 2
    own = pl.ds(pl.multiple_of(x * half, half), half)
    pairs = []
    for t in range(3):
        col = pl.multiple_of((4 * t + 2 * group + c) * wide, wide)
        pairs.append((qkv.at[:, pl.ds(col, wide)], dest.at[own, pl.ds(t * wide, wide)]))
    for q, piece in zip(quarters(index), pieces):
        row = pl.ds(pl.multiple_of((1 - x) * half + q * quarter, quarter), quarter)
        for t in range(3):
            pairs.append((piece.at[:, pl.ds((2 * t + group) * wide, wide)], dest.at[row, pl.ds(t * wide, wide)]))
    return pairs


def load_out(index, group, out_w, pieces, dest, sems, first):
    x, c, _, _ = place(index)
    half = out_w.shape[0]
    eighth, wide = half // 8, half // 2

    @pl.when(x == group)
    def _():
        copy_all([(out_w.at[pl.ds(pl.multiple_of(c * wide, wide), wide)], dest)], sems, first)

    @pl.when(x != group)
    def _():
        pairs = []
        for q, piece in zip(quarters(index), pieces):
            row = pl.ds(pl.multiple_of(q * eighth, eighth), eighth)
            for h in range(2):
                source = piece.at[pl.ds(h * eighth, eighth), pl.ds(3 * half, half)]
                pairs.append((source, dest.at[row, pl.ds(h * half, half)]))
        copy_all(pairs, sems, first + 1)


def attention_kernel(
    group, index, normed, normed_t, cot, cosine, sine_low, sine_high, doc_col, doc_row, bias,
    qkv, out_w, p0, p1, p2, p3, *refs
):
    if group == 0:
        send, keep, out_grad, context_out, mixed_out, colsum, w_all, o_all, mask, sems = refs
    else:
        early, send, keep, out_send, out_keep, context_out, mixed_out, colsum, w_all, o_all, mask, late, sems = refs
        out_grad = late
    x, c, y, _ = place(index)
    half = qkv.shape[0]
    wide = half // 2
    pair = 2 * HD
    length = doc_row.shape[1]

    def prepare():
        pairs = qkv_pairs(index, group, qkv, (p0, p1, p2, p3), w_all)
        copies = [pltpu.make_async_copy(a, b, sems.at[n]) for n, (a, b) in enumerate(pairs)]
        for copy in copies:
            copy.start()
        load_out(index, group, out_w, (p0, p1, p2, p3), o_all, sems, len(pairs))
        for s in range(2):
            keys = lax.broadcasted_iota(jnp.int32, (length, length), 0)
            queries = lax.broadcasted_iota(jnp.int32, (length, length), 1)
            same = doc_col[s * length : (s + 1) * length, :] == doc_row[s : s + 1, :]
            mask[s] = jnp.where(same & (keys <= queries), 0.0, MASKED)
        for copy in copies:
            copy.wait()

    prepare()
    pairs_here = wide // pair
    cs, lo, hi = cosine[...], sine_low[...], sine_high[...]

    def turn(v, sign):
        return v * cs + sign * (pltpu.roll(v, pair - ROT // 2, 1) * lo + pltpu.roll(v, ROT // 2, 1) * hi)

    scale = HD**-0.5
    mixed_all = mm(normed[...], w_all[...]) + bias[...]
    gc_both = mm(cot[...], o_all[...], NT).astype(BF)
    lane = lax.broadcasted_iota(jnp.int32, (length, pair), 1)
    first = lane < HD
    zero = jnp.zeros((length, pair), BF)
    part = length // 2
    turned_all = []
    for p in range(pairs_here):
        mixed = [mixed_all[:, t * wide + p * pair : t * wide + (p + 1) * pair] for t in range(3)]
        q_all = (turn(mixed[0], 1.0).astype(BF).astype(F32) * scale).astype(BF)
        k_all = turn(mixed[1], 1.0).astype(BF)
        v_all = mixed[2].astype(BF)
        gc_all = gc_both[:, p * pair : (p + 1) * pair]
        contexts_t, mixed_grads = [], []
        for s in range(2):
            row = slice(s * length, (s + 1) * length)
            q, k, v, gc = q_all[row], k_all[row], v_all[row], gc_all[row]
            k_turned, v_turned = k.T, v.T
            context_t, query_t, grad_k, grad_v = [], [], [], []
            mine = [first, ~first]
            qm = [jnp.where(m, q, zero) for m in mine]
            gm = [jnp.where(m, gc, zero) for m in mine]
            cts, qts, dks, dvs = [[], []], [[], []], [None, None], [None, None]
            for block in range(2):
                kk = part * (block + 1)
                qs = slice(block * part, (block + 1) * part)
                hs = range(2)
                scores = [mm(k[:kk], qm[h][qs], NT) + mask[s, :kk, qs] for h in hs]
                grad_probs = [mm(v[:kk], gm[h][qs], NT) for h in hs]
                weights = [jnp.exp(x - jnp.max(x, axis=0, keepdims=True)) for x in scores]
                probs = [x * (1.0 / jnp.sum(x, axis=0, keepdims=True)) for x in weights]
                low = [x.astype(BF) for x in probs]
                inner = [jnp.sum(a * b, axis=0, keepdims=True) for a, b in zip(probs, grad_probs)]
                ds = [(a * (b - c)).astype(BF) for a, b, c in zip(probs, grad_probs, inner)]
                for h in hs:
                    rows_h = slice(h * HD, (h + 1) * HD)
                    cts[h].append(mm(v_turned[rows_h, :kk], low[h]))
                    qts[h].append(mm(k_turned[rows_h, :kk], ds[h]))
                    dv_b, dk_b = mm(low[h], gc[qs]), mm(ds[h], q[qs])
                    if block == 0:
                        dvs[h], dks[h] = dv_b, dk_b
                    else:
                        dvs[h] = jnp.concatenate([dvs[h] + dv_b[:part], dv_b[part:]], axis=0)
                        dks[h] = jnp.concatenate([dks[h] + dk_b[:part], dk_b[part:]], axis=0)
            turned = jnp.concatenate([jnp.concatenate(c, axis=1) for c in cts], axis=0).astype(BF)
            contexts_t.append(turned)
            context_out[row, p * pair : (p + 1) * pair] = turned.T
            dq = jnp.concatenate([jnp.concatenate(c, axis=1) for c in qts], axis=0).T * scale
            mixed_grads.append((dq, jnp.where(first, dks[0], dks[1]), jnp.where(first, dvs[0], dvs[1])))
        dq, dk, dv = (jnp.concatenate([m[n] for m in mixed_grads], axis=0) for n in range(3))
        for t, v in enumerate((turn(dq, -1.0), turn(dk, -1.0), dv)):
            mixed_out[:, t * wide + p * pair : t * wide + (p + 1) * pair] = v.astype(BF)
        turned_all.append(jnp.concatenate(contexts_t, axis=1))
    grad_mixed = mixed_out[...]
    colsum[...] = jnp.sum(grad_mixed.astype(F32), axis=0, keepdims=True)
    if group == 0:
        for ref, side in ((keep, x), (send, 1 - x)):
            g = mm(normed_t[pl.ds(pl.multiple_of(side * half, half), half), :], grad_mixed).astype(BF)
            for t in range(3):
                ref[t] = g[:, t * wide : (t + 1) * wide]
    else:
        for ref, side in ((keep, y), (send, 1 - y)):
            for xr in range(2):
                rows = pl.ds(pl.multiple_of(xr * half + side * wide, wide), wide)
                g = mm(normed_t[rows, :], grad_mixed).astype(BF)
                for t in range(3):
                    ref[t, xr] = g[:, t * wide : (t + 1) * wide]
    g = mm(jnp.concatenate(turned_all, axis=0), cot[...]).astype(BF)
    for h in range(2):
        for cc in range(2):
            start = h * half + cc * wide
            out_grad[cc, h * wide : (h + 1) * wide, :] = g[:, start : start + wide]

    if group == 1:

        @pl.when(x == 0)
        def _():
            out_send[...] = late[...]
            out_keep[...] = early[...]

        @pl.when(x == 1)
        def _():
            out_send[...] = early[...]
            out_keep[...] = late[...]


def norm_kernel(index, tokens, other, cot, cot_other, gains, one, two, one_t, two_t, cot_out):
    mine = pl.program_id(0) < pl.num_programs(0) // 2
    rows = jnp.where(mine, tokens[...], other[...]).astype(F32)
    centred = rows - jnp.mean(rows, axis=-1, keepdims=True)
    unit = centred * lax.rsqrt(jnp.mean(centred * centred, axis=-1, keepdims=True) + EPSILON)
    first = unit * gains[0:1, :] + gains[1:2, :]
    second = unit * gains[2:3, :] + gains[3:4, :]
    one[...] = first.astype(BF)
    two[...] = second.astype(BF)
    one_t[...] = first.T.astype(BF)
    two_t[...] = second.T.astype(BF)
    cot_out[...] = jnp.where(mine, cot[...], cot_other[...])


def dense_ffn_kernel(
    index, act_o, act_x, hid_o, hid_x, down, d0, d1, d2, d3, up, p0, p1, q0, q1,
    out, grad, w_o, w_x, d_o, d_x, sems,
):
    x, c = index[0], index[1]
    i = pl.program_id(0)
    rows_d, wide = d0.shape[0], d_o.shape[0]
    for_down = [(down.at[pl.ds(pl.multiple_of(c * wide, wide), wide)], d_o)]
    for q, piece in zip(quarters(index), (d0, d1, d2, d3)):
        for_down.append((piece, d_x.at[pl.ds(pl.multiple_of(q * rows_d, rows_d), rows_d)]))
    for_up = up_pairs(index, up, (p0, p1), w_x, 1 - x) + up_pairs(index, up, (q0, q1), w_o, x)
    copies = [pltpu.make_async_copy(a, b, sems.at[n]) for n, (a, b) in enumerate(for_down + for_up)]

    @pl.when(i == 0)
    def _():
        for copy in copies:
            copy.start()
        for copy in copies[: len(for_down)]:
            copy.wait()

    out[...] = mm(act_o[...], d_o[...]) + mm(act_x[...], d_x[...])

    @pl.when(i == 0)
    def _():
        for copy in copies[len(for_down) :]:
            copy.wait()

    grad[...] = mm(hid_o[...], w_o[...], NT) + mm(hid_x[...], w_x[...], NT)


def dense_last_kernel(
    index, tokens, gains, ffn, grad_two, context_a, context_b, mixed_a, mixed_b, qkv, out_w, r0, r1, r2, r3,
    sums, pulled_send, pulled_keep, part_send, part_keep, m_a, m_b, o_a, o_b, sems,
):
    i = pl.program_id(0)
    steps = pl.num_programs(0)
    rest = (r0, r1, r2, r3)
    pairs = qkv_pairs(index, 0, qkv, rest, m_a) + qkv_pairs(index, 1, qkv, rest, m_b)
    copies = [pltpu.make_async_copy(a, b, sems.at[n]) for n, (a, b) in enumerate(pairs)]

    @pl.when(i == 0)
    def _():
        for copy in copies:
            copy.start()
        load_out(index, 0, out_w, rest, o_a, sems, len(pairs))
        load_out(index, 1, out_w, rest, o_b, sems, len(pairs))

    part = ffn[...] + mm(context_a[...], o_a[...]) + mm(context_b[...], o_b[...])

    @pl.when(i == 0)
    def _():
        for copy in copies:
            copy.wait()

    two = grad_two[...]
    one = mm(mixed_a[...], m_a[...], NT) + mm(mixed_b[...], m_b[...], NT)
    rows = tokens[...].astype(F32)
    centred = rows - jnp.mean(rows, axis=-1, keepdims=True)
    unit = centred * lax.rsqrt(jnp.mean(centred * centred, axis=-1, keepdims=True) + EPSILON)
    sums_here = jnp.concatenate(
        [jnp.sum(v, axis=0, keepdims=True) for v in (one * unit, one, two * unit, two)], axis=0
    )
    pulled = one * gains[0:1, :] + two * gains[2:3, :]

    @pl.when(i == 0)
    def _():
        sums[...] = sums_here

    @pl.when(i != 0)
    def _():
        sums[...] += sums_here

    @pl.when(i < steps // 2)
    def _():
        pulled_send[...] = pulled
        part_send[...] = part

    @pl.when(i >= steps // 2)
    def _():
        pulled_keep[...] = pulled
        part_keep[...] = part


def last_kernel(tokens, cot, gains, pulled_keep, pulled_recv, part_keep, part_recv, out, grad):
    rows = tokens[...].astype(F32)
    centred = rows - jnp.mean(rows, axis=-1, keepdims=True)
    spread = lax.rsqrt(jnp.mean(centred * centred, axis=-1, keepdims=True) + EPSILON)
    unit = centred * spread
    pulled = pulled_keep[...] + pulled_recv[...]
    inward = spread * (
        pulled
        - jnp.mean(pulled, axis=-1, keepdims=True)
        - unit * jnp.mean(pulled * unit, axis=-1, keepdims=True)
    )
    grad[...] = (cot[...].astype(F32) + inward).astype(BF)
    out[...] = (rows + (part_keep[...] + part_recv[...]) + (gains[4:5, :] + gains[5:6, :])).astype(BF)


def tables_kernel(index, doc_col, doc_row, inverse, cosine, sine_low, sine_high):
    length = doc_row.shape[1]
    few = ROT // 2
    ones = jnp.ones((HD - ROT, length), F32)
    zeros = jnp.zeros((HD - ROT, length), F32)
    none = jnp.zeros((few, length), F32)
    for s in range(2):
        rows = slice(s * length, (s + 1) * length)
        before = jnp.sum((doc_col[rows, :] < doc_row[s : s + 1, :]).astype(F32), axis=0, keepdims=True)
        offsets = lax.broadcasted_iota(jnp.int32, (1, length), 1).astype(F32) - before
        angles = inverse[...] * offsets
        cos, sine = jnp.cos(angles), jnp.sin(angles)
        cosine[rows, :] = jnp.concatenate([cos, cos, ones] * 2, axis=0).T
        sine_low[rows, :] = jnp.concatenate([-sine, none, zeros] * 2, axis=0).T
        sine_high[rows, :] = jnp.concatenate([none, sine, zeros] * 2, axis=0).T


def split_kernel(groups, index, *refs):
    outs = refs[sum(count for count, _ in groups) :]
    at = used = 0
    for g, (count, n) in enumerate(groups):
        addends = refs[used : used + count]
        used += count
        for t in range(n):
            for k, out in enumerate(outs):
                side = index[g] ^ k
                total = addends[0][t, side].astype(F32)
                for ref in addends[1:]:
                    total += ref[t, side].astype(F32)
                out[at] = total.astype(BF)
            at += 1


def stack_kernel(index, *refs):
    *pieces, out = refs
    for n, piece in enumerate(pieces):
        out[n] = piece[...]


def place_rows(index, y_rel, z_rel, rows, many):
    row = ((y_rel ^ index[2]) * many + (z_rel ^ index[4])) * rows
    return pl.ds(pl.multiple_of(row, rows), rows)


def join_kernel(index, down_keep, down_recv, up_keep, up_recv, c_keep, c_recv, out):
    half = c_keep.shape[2]
    for t in range(4):
        out[t] = (down_keep[t].astype(F32) + down_recv[t].astype(F32)).astype(BF)
        out[4 + t] = (up_keep[t].astype(F32) + up_recv[t ^ 2].astype(F32)).astype(BF)
        for n, c in enumerate((t, 3 + t) if t < 3 else (6, 7)):
            out[8 + t, :, n * half : (n + 1) * half] = (c_keep[c].astype(F32) + c_recv[c].astype(F32)).astype(BF)


def sum_kernel(index, *refs):
    *parts, out = refs
    sums = [part[...] for part in parts]
    while len(sums) > 1:
        sums = [a + b for a, b in zip(sums[::2], sums[1::2])]
    out[...] = sums[0]


def reverse(k, count):
    out = 0
    while count > 1:
        out, k, count = 2 * out + k % 2, k // 2, count // 2
    return out


def widen_kernel(index, piece, down, up, qkv, out, slots, sems):
    many, _, _, _, rows, _ = piece.shape
    x = index[0]
    c = pl.program_id(0)
    quarter = TILE // 2

    def moves(job, core):
        slot = slots.at[job % 3]
        if job < 2:
            row = pl.multiple_of((2 * core + job) * TILE, TILE)
            return [(slot, down.at[pl.ds(row, TILE), :])]
        if job < 4:
            col = pl.multiple_of((4 * (x ^ (job - 2)) + 2 * core) * TILE, TILE)
            return [(slot, up.at[:, pl.ds(col, 2 * TILE)])]
        pairs = []
        for n in range(2 if job == 4 else 1):
            for g in range(2):
                col = pl.multiple_of((4 * (2 * (job - 4) + n) + 2 * g + core) * quarter, quarter)
                pairs.append((slot.at[:, pl.ds(n * TILE + g * quarter, quarter)], qkv.at[:, pl.ds(col, quarter)]))
        if job == 5:
            row = pl.multiple_of(core * quarter, quarter)
            for h in range(2):
                pairs.append(
                    (slot.at[pl.ds(h * quarter, quarter), pl.ds(TILE, TILE)], out.at[pl.ds(row, quarter), pl.ds(h * TILE, TILE)])
                )
        return pairs

    def copies(job, core):
        return [pltpu.make_async_copy(a, b, sems.at[job % 3, n]) for n, (a, b) in enumerate(moves(job, core))]

    def settle(job, core):
        for copy in copies(job, core):
            copy.wait()

    for job in range(6):
        if job < 3:

            @pl.when(c > 0)
            def _(job=job):
                settle(job + 3, c - 1)

        else:
            settle(job - 3, c)
        tiles = (2 * job, 2 * job + 1)
        for n, tile in enumerate(tiles):
            for y in range(2):
                for z in range(many):
                    row = (y * many + reverse(z, many)) * rows
                    slots[job % 3, row : row + rows, n * TILE : (n + 1) * TILE] = piece[z, y, 0, tile].astype(F32)
        for copy in copies(job, c):
            copy.start()

    @pl.when(c == pl.num_programs(0) - 1)
    def _():
        for job in range(3, 6):
            settle(job, c)


def build(reps):
    bits = reps.bit_length() - 1
    many = reps // 4

    def flip(array, bit):
        return lax.ppermute(array, "rep", [(i, i ^ (1 << bit)) for i in range(reps)])

    def hop(array, k):
        return lax.ppermute(array, "rep", [(i, i ^ (k << 2)) for i in range(reps)])

    def flip_x(array):
        return lax.ppermute(array, "shard", [(0, 1), (1, 0)])

    def call(kernel, grid, in_specs, out_specs, out_shape, scratch=(), est=None, after=(), aliases=(), mib=62):
        n_in, n_after, n_out = len(in_specs), len(after), len(out_shape)

        def wrapped(index, *refs):
            rest = refs[n_in + n_after :]
            kernel(index, *refs[:n_in], *rest[:n_out], *rest[n_out + 1 :])
            rest[n_out][...] = jnp.zeros((8, 128), F32)

        run = pl.pallas_call(
            wrapped,
            grid_spec=pltpu.PrefetchScalarGridSpec(
                num_scalar_prefetch=1,
                grid=grid,
                in_specs=list(in_specs) + [ANY] * n_after,
                out_specs=list(out_specs) + [pl.BlockSpec((8, 128), lambda *_: (0, 0))],
                scratch_shapes=list(scratch),
            ),
            out_shape=list(out_shape) + [sds((8, 128), F32)],
            compiler_params=params(mib),
            cost_estimate=est,
            input_output_aliases=dict(aliases),
        )
        return lambda index, *args: run(index, *args, *after)

    def on_device(
        tokens, segments, norm1_gain, norm1_shift, norm2_gain, norm2_shift, qkv_weight, qkv_bias,
        out_weight, out_bias, up_weight, up_bias, down_weight, down_bias, cotangent,
    ):
        half, width = out_weight.shape
        length = tokens.shape[0]
        ff_half = down_weight.shape[0]
        units = ff_half // 2
        toks = 2 * length
        xi = lax.axis_index("shard").astype(jnp.int32)
        ri = lax.axis_index("rep").astype(jnp.int32)
        rbit = [(ri >> b) & 1 for b in range(bits)]
        ci, yi = rbit[0], rbit[1]
        z_order = 0 * ri
        for bit in range(2, bits):
            z_order = 2 * z_order + rbit[bit]
        index = jnp.stack([xi, ci, yi, rbit[2], z_order])

        dma = pltpu.SemaphoreType.DMA
        wide = half // 2
        pair_rows = (half // 2, units)

        def corner(i, n):
            return 2 * (i[2] ^ n) + (i[3] ^ n)

        def from_qkv(n, t, h):
            return pl.BlockSpec((half // 4, wide), lambda g, i: (corner(i, n), 4 * t + 2 * h + i[1]))

        def whole(shape):
            return pl.BlockSpec(shape, lambda *_: (0,) * len(shape))

        def touch(arrays, after):
            n = len(arrays)
            shapes = [sds(a.shape, a.dtype) for a in arrays]
            return call(
                touch_kernel, (1,), [ANY] * n, [ANY] * n, shapes, (), cost(1, 1), after, {1 + k: k for k in range(n)}
            )(index, *arrays)

        def lay(vector, at, total):
            return jnp.pad(vector.astype(F32), (at, total - at - vector.shape[0]))

        tokens_other = flip(tokens, 0)
        cot_other = flip(cotangent, 0)
        vectors = [norm1_gain, norm1_shift, norm2_gain, norm2_shift, out_bias, down_bias, qkv_bias, up_bias]
        starts = [sum(v.shape[0] for v in vectors[:n]) for n in range(len(vectors) + 1)]
        small_own = sum(lay(v, s, starts[-1]) for v, s in zip(vectors, starts))
        small_other = flip_x(small_own)
        up_first, up_second, mark = call(
            pack_up_kernel, (1,),
            [pl.BlockSpec(pair_rows, lambda n, i: (i[2], 2 * i[0] + i[1])),
             pl.BlockSpec(pair_rows, lambda n, i: (i[2], 2 * (1 - i[0]) + i[1]))],
            [whole(pair_rows)] * 2, [sds(pair_rows, BF)] * 2, (), cost(1, 4 * MIB), [small_other],
        )(index, up_weight, up_weight)
        up_first = flip_x(up_first)

        segments_other = flip(segments, 0)

        low = jnp.where(xi == 0, small_own, small_other).reshape(-1, half)
        high = jnp.where(xi == 0, small_other, small_own).reshape(-1, half)
        gains = jnp.concatenate([low[:6], high[:6]], axis=1)
        qkv_b = jnp.concatenate([low[6:9], high[6:9]], axis=0).reshape(3, 2, 2, wide)
        qkv_b = lax.dynamic_index_in_dim(qkv_b, ci, 2, keepdims=False)
        up_b = jnp.concatenate([low[9:13], high[9:13]], axis=0).reshape(2, 2, units)
        up_b = lax.dynamic_index_in_dim(up_b, ci, 1, keepdims=False)
        up_b_own = lax.dynamic_slice_in_dim(up_b, xi, 1, 0)
        up_b_other = lax.dynamic_slice_in_dim(up_b, 1 - xi, 1, 0)

        rows = 256
        blocks = toks // rows

        def lower(i, *_):
            return (jnp.minimum(i, blocks // 2 - 1), 0)

        def upper_half(i, *_):
            return (jnp.maximum(i - blocks // 2, 0), 0)

        row_out = pl.BlockSpec((rows, width), lambda i, *_: (i, 0))
        column_out = pl.BlockSpec((width, rows), lambda i, *_: (0, i))
        turned_acts = sds((width, toks), BF)
        first_half, second_half = pl.BlockSpec((rows, width), lower), pl.BlockSpec((rows, width), upper_half)
        normed_one, normed_two, one_t, two_t, cot, mark = call(
            norm_kernel, (blocks,), [first_half, second_half] * 2 + [held((6, width))],
            [row_out, row_out, column_out, column_out, row_out],
            [sds((toks, width), BF)] * 2 + [turned_acts] * 2 + [sds((toks, width), BF)], (),
            cost(20 * toks * width, 14 * toks * width), [mark],
        )(index, tokens, tokens_other, cotangent, cot_other, gains)
        up_first, up_second, mark = touch([up_first, up_second], [mark])
        first_pieces = (up_first, flip(up_first, 1))
        up_second = flip_x(up_second)
        documents = jnp.concatenate([segments, segments_other], 0)
        doc_col = documents.reshape(toks, 1)
        pair = 2 * HD
        inverse = 1.0 / 10000.0 ** (jnp.arange(0, ROT, 2, dtype=F32) / ROT)
        inverse = inverse.reshape(ROT // 2, 1)
        cosine, sine_low, sine_high, mark = call(
            tables_kernel, (1,), [whole((toks, 1)), whole((2, length)), whole((ROT // 2, 1))], [whole((toks, pair))] * 3,
            [sds((toks, pair), F32)] * 3, (), cost(100 * toks * pair, 12 * toks * pair), [mark],
        )(index, doc_col, documents, inverse)

        part_shapes = [(units // 4, width), (half // 4, 4 * half)] * 2
        in_specs, sources = [], []
        for n in range(2):
            in_specs.append(pl.BlockSpec((units // 4, width), lambda g, i, n=n: (4 * i[1] + corner(i, n), 0)))
            in_specs += [from_qkv(n, t, h) for t in range(3) for h in range(2)]
            in_specs.append(pl.BlockSpec((half // 8, width), lambda g, i, n=n: (4 * i[1] + corner(i, n), 0)))
            sources += [down_weight] + [qkv_weight] * 6 + [out_weight]
        down_part, rest_part, down_far, rest_far, mark = call(
            pack_kernel, (1,), in_specs,
            [whole(s) for s in part_shapes], [sds(s, BF) for s in part_shapes], (), cost(1, 8 * MIB), [mark],
        )(index, *sources)
        down_part, down_far = flip_x(down_part), flip_x(down_far)
        rest_part, rest_far = flip_x(rest_part), flip_x(rest_far)

        up_second, mark = touch([up_second], [mark])
        second_pieces = (up_second, flip(up_second, 1))
        steps = units // BLOCK
        column = pl.BlockSpec((toks, BLOCK), lambda j, *_: (0, j))
        bias_block = pl.BlockSpec((1, BLOCK), lambda j, *_: (0, j))
        by_z = pl.BlockSpec((1, 2, 2, half // 4, BLOCK), lambda j, *_: (j, 0, 0, 0, 0))
        z_shape = sds((2, 2, 2, half // 4, TILE), BF)
        by_y = pl.BlockSpec((1, 2, half // 2, BLOCK), lambda j, *_: (j, 0, 0, 0))
        y_shape = sds((2, 2, half // 2, TILE), BF)
        two_tiles, two_halves = sds((2, TILE, TILE), BF), sds((2, TILE // 2, TILE), BF)
        four_halves = sds((4, TILE // 2, TILE), BF)
        unit_act = sds((toks, units), BF)
        full = held((toks, width))
        w_scratch = pltpu.VMEM((width, units), BF)
        d_scratch = pltpu.VMEM((units, width), BF)
        g_scratch = pltpu.VMEM((width, BLOCK), BF)
        one_mm = 2 * toks * width * units
        act_x, slope_x, da_send, other_keep, other_send, mark = call(
            ffn_other_kernel, (steps,), [full, full, bias_block] + [ANY] * 3,
            [column, column, whole(two_tiles.shape), whole(two_halves.shape), whole(two_halves.shape)],
            [unit_act, unit_act, two_tiles, two_halves, two_halves],
            [w_scratch, pltpu.VMEM((BLOCK, width), BF), dma((3,))], cost(5 * one_mm, 14 * MIB), [mark],
        )(index, normed_two, cot, up_b_other, up_weight, *first_pieces)
        down_part, mark = touch([down_part], [mark])
        down_pieces = (down_part, flip(down_part, 1), flip(down_part, 2), down_far)
        act_o, hid_o, da_keep, db_keep, db_send, uo_keep, uo_send, colsum_o, mark = call(
            ffn_own_kernel, (steps,),
            [full, full, full, bias_block, pl.BlockSpec((BLOCK, width), lambda j, i: (i[1] * steps + j, 0))]
            + [ANY] * 3 + [held(two_halves.shape)] * 2,
            [column, column, whole(two_tiles.shape), whole(four_halves.shape), whole(four_halves.shape), by_z, by_z, bias_block],
            [unit_act, unit_act, two_tiles, four_halves, four_halves, z_shape, z_shape, sds((1, units), F32)],
            [w_scratch, pltpu.VMEM((BLOCK, width), BF), g_scratch, dma((3,))], cost(8 * one_mm, 18 * MIB), [mark],
        )(index, normed_two, two_t, cot, up_b_own, down_weight, up_weight, *second_pieces, other_keep, other_send)
        rest_part, mark = touch([rest_part], [mark])
        rest_pieces = (rest_part, flip(rest_part, 1), flip(rest_part, 2), rest_far)
        da_send, db_send, mark = touch([da_send, db_send], [mark])
        da_recv, db_recv = flip_x(da_send), flip(db_send, 1)
        hid_x, ux_keep, ux_send, colsum_x, mark = call(
            ffn_back_kernel, (steps,), [full, full, column] + [ANY] * 4,
            [column, by_y, by_y, bias_block],
            [unit_act, y_shape, y_shape, sds((1, units), F32)],
            [d_scratch, g_scratch, dma((4,))], cost(4 * one_mm, 14 * MIB), [mark],
        )(index, two_t, cot, slope_x, *down_pieces)
        uo_recv, ux_recv = flip(uo_send, 2), flip(ux_send, 1)

        table = held((toks, pair))
        sum_shape = sds((1, 3 * wide), F32)
        out_tiles = sds((2, half, wide), BF)
        x_tiles = sds((3, half, wide), BF)
        y_tiles = sds((3, 2, wide, wide), BF)
        heads_out = [sds((toks, wide), BF), sds((toks, 3 * wide), BF), sum_shape]

        def attend(group, extra, shapes, scratch, after):
            specs = [full, full, full, table, table, table, held((toks, 1)), held((2, length)), held((1, 3 * wide))]
            return call(
                partial(attention_kernel, group), (1,),
                specs + [ANY] * 6 + [held(e.shape) for e in extra],
                [held(s.shape) for s in shapes], shapes,
                [pltpu.VMEM((width, 3 * wide), BF), pltpu.VMEM((wide, width), BF),
                 pltpu.VMEM((2, length, length), F32)] + scratch + [dma((24,))],
                cost(6e9, 4 * MIB), after,
            )(
                index, normed_one, one_t, cot, cosine, sine_low, sine_high, doc_col, documents,
                qkv_b[:, group].reshape(1, 3 * wide), qkv_weight, out_weight, *rest_pieces, *extra,
            )

        a_send, a_keep, out_early, context_a, mixed_a, colsum_a, mark = attend(
            0, [], [x_tiles, x_tiles, out_tiles] + heads_out, [], [mark]
        )

        def split(groups, ways, after):
            cols = groups[0][0][0].shape[-1]
            small = groups[0][0][0].size // groups[0][1] // cols // ways
            views = [(n, ways, small, cols) for addends, n, _ in groups for _ in addends]
            total = sum(n for _, n, _ in groups)
            out = (total, small, cols)
            return call(
                partial(split_kernel, [(len(addends), n) for addends, n, _ in groups]), (1,),
                [whole(v) for v in views], [whole(out)] * ways, [sds(out, BF)] * ways, (),
                cost(4 * total * small * cols, 12 * total * small * cols), after,
            )(
                jnp.stack([side for _, _, side in groups]),
                *[a.reshape(v) for a, v in zip([a for addends, _, _ in groups for a in addends], views)],
            )

        def add(parts, after):
            n = parts[0].size // parts[0].shape[-1] // parts[0].shape[-2]
            return split([(parts, n, 0 * xi)], 1, after)

        def stack(pieces, after):
            shape = (len(pieces),) + pieces[0].shape
            return call(
                stack_kernel, (1,), [whole(shape[1:])] * len(pieces), [whole(shape)], [sds(shape, BF)], (),
                cost(1, 4 * pieces[0].size * len(pieces)), after,
            )(index, *pieces)

        token_rows = pl.BlockSpec((rows, units), lambda i, *_: (i, 0))
        token_out = pl.BlockSpec((rows, width), lambda i, *_: (i, 0))
        wide_f32 = sds((toks, width), F32)

        def turned(cols):
            return pl.BlockSpec((rows, cols), lambda i, *_: ((i + blocks // 2) % blocks, 0))

        sums_block = pl.BlockSpec((4, width), lambda i, *_: (0, 0))
        send_block, keep_block = pl.BlockSpec((rows, width), lower), pl.BlockSpec((rows, width), upper_half)
        own_f32 = sds((length, width), F32)
        m_scratch = pltpu.VMEM((width, 3 * wide), BF)
        out_scratch = pltpu.VMEM((wide, width), BF)

        def dense_last(i, tokens_ref, other_ref, *refs):
            mine = pl.program_id(0) >= blocks // 2
            dense_last_kernel(i, jnp.where(mine, tokens_ref[...], other_ref[...]), *refs)

        a_recv = flip_x(a_send)
        last_bits = list(range(3, bits))
        one = 1 + 0 * xi

        da_keep, da_send, mark = split([([da_keep, da_recv], 2, yi)], 2, [mark])
        da_recv = flip(da_send, 1)
        db_keep, db_send, mark = split([([db_keep, db_recv], 1, one)], 2, [mark])
        db_recv = flip_x(db_send)
        uo_keep, uo_send, mark = split([([uo_keep, uo_recv], 4, yi)], 2, [mark])
        uo_recv = flip(uo_send, 1)
        b_send, b_keep, out_send, out_keep, context_b, mixed_b, colsum_b, mark = attend(
            1, [out_early], [y_tiles, y_tiles, out_tiles, out_tiles] + heads_out,
            [pltpu.VMEM((2, half, wide), BF)], [mark],
        )
        da_recv, db_recv, uo_recv, ux_recv, b_send, out_send, mark = touch(
            [da_recv, db_recv, uo_recv, ux_recv, b_send, out_send], [mark]
        )
        b_recv = flip(b_send, 1)
        out_recv = flip_x(out_send)
        ux_keep, ux_send, mark = split([([ux_keep, ux_recv], 4, rbit[2])], 2, [mark])
        ux_recv = flip(ux_send, 2)
        a_keep, a_send, mark = split([([a_keep, a_recv], 3, yi)], 2, [mark])
        a_recv = flip(a_send, 1)
        d_keep, d_send, mark = split([([da_keep, da_recv], 2, rbit[2]), ([db_keep, db_recv], 2, rbit[2])], 2, [mark])
        d_recv = flip(d_send, 2)
        u_parts = [([uo_keep, uo_recv], 4), ([ux_keep, ux_recv], 4)]
        for bit in last_bits:
            u_keep, u_send, mark = split([(p, n, rbit[bit]) for p, n in u_parts], 2, [mark])
            u_parts = [([u_keep, flip(u_send, bit)], 8)]
        b_keep, b_send, mark = split([([b_keep, b_recv], 3, xi)], 2, [mark])
        b_recv = flip_x(b_send)
        out_keep, out_send, mark = split([([out_keep, out_recv], 2, yi)], 2, [mark])
        out_recv = flip(out_send, 1)
        for bit in last_bits:
            d_keep, d_send, mark = split([([d_keep, d_recv], 4, rbit[bit])], 2, [mark])
            d_recv = flip(d_send, bit)
        c_keep, c_send, mark = split(
            [([k, v], n, rbit[2]) for k, v, n in ((a_keep, a_recv, 3), (b_keep, b_recv, 3), (out_keep, out_recv, 2))], 2, [mark]
        )
        c_recv = flip(c_send, 2)
        u_keep, u_send, mark = split([(p, n // 2, xi) for p, n in u_parts], 2, [mark])
        u_recv = flip_x(u_send)
        for bit in last_bits:
            c_keep, c_send, mark = split([([c_keep, c_recv], 8, rbit[bit])], 2, [mark])
            c_recv = flip(c_send, bit)
        r = half // reps * 2
        piece, mark = call(
            join_kernel, (1,), [whole((4, r, TILE))] * 4 + [whole((8, r, wide))] * 2, [whole((12, r, TILE))],
            [sds((12, r, TILE), BF)], (), cost(1, 1), [mark],
        )(index, d_keep, d_recv, u_keep, u_recv, c_keep, c_recv)
        gathered = lax.all_gather(piece, "rep", axis=0, tiled=False).reshape(many, 2, 2, 12, r, TILE)

        ffn_part, grad_two, mark = call(
            dense_ffn_kernel, (blocks,), [token_rows] * 4 + [ANY] * 10, [token_out] * 2, [wide_f32] * 2,
            [w_scratch, w_scratch, d_scratch, d_scratch, dma((15,))], cost(6 * one_mm, 24 * MIB), [mark],
        )(index, act_o, act_x, hid_o, hid_x, down_weight, *down_pieces, up_weight, *first_pieces, *second_pieces)
        sums, pulled_send, pulled_keep, part_send, part_keep, mark = call(
            dense_last, (blocks,),
            [keep_block, send_block, held((6, width)), turned(width), turned(width)] + [turned(wide)] * 2
            + [turned(3 * wide)] * 2 + [ANY] * 6,
            [sums_block, send_block, keep_block, send_block, keep_block],
            [sds((4, width), F32)] + [own_f32] * 4,
            [m_scratch, m_scratch, out_scratch, out_scratch, dma((40,))],
            cost(4 * one_mm, 30 * MIB), [mark],
        )(
            index, tokens, tokens_other, gains, ffn_part, grad_two, context_a, context_b, mixed_a, mixed_b,
            qkv_weight, out_weight, *rest_pieces,
        )
        pulled_recv = flip(pulled_send, 0)
        part_recv = flip(part_send, 0)

        def spread_core(vector, parts):
            size = vector.size // parts
            v = vector.reshape(parts, 1, size)
            keep = (jnp.arange(2) == ci)[None, :, None]
            return jnp.where(keep, v, 0.0).reshape(-1, width)

        column_sum = jnp.sum(cotangent.astype(F32), axis=0, keepdims=True)
        colsum_up = jnp.where(
            xi == 0, jnp.concatenate([colsum_o, colsum_x], 0), jnp.concatenate([colsum_x, colsum_o], 0)
        )
        colsum_q = jnp.stack([colsum_a.reshape(3, wide), colsum_b.reshape(3, wide)], axis=1)
        small = jnp.concatenate([sums, column_sum, spread_core(colsum_q, 6), spread_core(colsum_up, 2)], axis=0)

        def meet(own, masks, after):
            size = 2 * reps
            parts = [own] + [
                lax.ppermute(own, ("rep", "shard"), [(i, i ^ m) for i in range(size)]) for m in masks
            ]
            return call(
                sum_kernel, (1,), [whole(own.shape)] * len(parts), [whole(own.shape)], [sds(own.shape, F32)], (),
                cost(1, 1), after,
            )(index, *parts)

        small, mark = meet(small, (1, 2, 3), [mark])
        output, grad_tokens, mark = call(
            lambda i, *refs: last_kernel(*refs), (length // rows,),
            [token_out, token_out, held((6, width))] + [token_out] * 4, [token_out] * 2,
            [sds((length, width), BF)] * 2, (), cost(40 * length * width, 24 * length * width), [mark],
        )(index, tokens, cotangent, gains, pulled_keep, pulled_recv, part_keep, part_recv)
        for bit in range(2, bits + 1, 2):
            masks = (1 << bit, 2 << bit, 3 << bit) if bit < bits else (1 << bit,)
            small, mark = meet(small, masks, [mark])

        down_grad, up_grad, qkv_grad, out_grad, mark = call(
            widen_kernel, (2,), [pl.BlockSpec((many, 2, 1, 12, r, TILE), lambda c, i: (0, 0, c, 0, 0, 0))], [ANY] * 4,
            [sds((ff_half, width), F32), sds((half, 2 * ff_half), F32), sds((half, 6 * half), F32), sds((half, width), F32)],
            [pltpu.VMEM((3, TILE, 2 * TILE), F32), dma((3, 4))], cost(1, 40 * MIB), [mark],
        )(index, gathered)

        def owned(row, count=1):
            v = small[row : row + count].reshape(2, -1)
            return lax.dynamic_index_in_dim(v, xi, 0, keepdims=False)

        bias_out = owned(4)
        return (
            output, grad_tokens, owned(0), owned(1), owned(2), owned(3), qkv_grad, owned(5, 3),
            out_grad, bias_out, up_grad, owned(8, 4), down_grad, bias_out,
        )

    return on_device


def solution(mesh):
    both = P(("rep", "shard"), None)
    vector = P("shard")
    matrix = P("shard", None)
    weights = (
        vector, vector, vector, vector, matrix, vector, matrix, vector, matrix, vector, matrix, vector,
    )
    return jax.shard_map(
        build(mesh.shape["rep"]),
        mesh=mesh,
        in_specs=(both, both) + weights + (both,),
        out_specs=(both, both) + weights,
        check_vma=False,
    )
```

```python
from functools import partial

import jax
import jax.numpy as jnp
from jax import lax
from jax.experimental import pallas as pl
from jax.experimental.pallas import tpu as pltpu
from jax.sharding import PartitionSpec as P

HD = 64
ROT = 16
EPSILON = 1e-05
MASKED = -1e30
BF = jnp.bfloat16
F32 = jnp.float32
TILE = 512
MIB = 1 << 20
NN = (((1,), (0,)), ((), ()))
NT = (((1,), (1,)), ((), ()))
TN = (((0,), (0,)), ((), ()))


def mm(left, right, dims=NN):
    return lax.dot_general(left, right, dims, preferred_element_type=F32)


def cost(flops, nbytes):
    return pl.CostEstimate(flops=int(flops), bytes_accessed=int(nbytes), transcendentals=0)


def params(mib=62):
    return pltpu.CompilerParams(vmem_limit_bytes=mib * MIB)


ANY = pl.BlockSpec(memory_space=pltpu.HBM)


def held(shape):
    return pl.BlockSpec(shape, lambda *_: (0,) * len(shape), pipeline_mode=pl.Buffered(1))


def sds(shape, kind):
    return jax.ShapeDtypeStruct(shape, kind)


def copy_all(pairs, sems, first=0):
    copies = [pltpu.make_async_copy(a, b, sems.at[first + n]) for n, (a, b) in enumerate(pairs)]
    for c in copies:
        c.start()
    for c in copies:
        c.wait()


def place(index):
    return index[0], index[1], index[2], index[3]


def quarters(index):
    _, _, y, z = place(index)
    return (2 * y + z, 2 * (1 - y) + z, 2 * y + (1 - z), 2 * (1 - y) + (1 - z))


def pack_up_kernel(index, first, second, first_out, second_out):
    first_out[...] = first[...]
    second_out[...] = second[...]


def pack_kernel(index, *refs):
    ins, outs = refs[:16], refs[16:]
    for n in range(2):
        down, *qkv, out_w = ins[8 * n : 8 * n + 8]
        down_out, rest_out = outs[2 * n : 2 * n + 2]
        down_out[...] = down[...]
        wide = qkv[0].shape[1]
        for m, piece in enumerate(qkv):
            rest_out[:, m * wide : (m + 1) * wide] = piece[...]
        rows, width = out_w.shape
        for h in range(2):
            rest_out[h * rows : (h + 1) * rows, 6 * wide :] = out_w[:, h * (width // 2) : (h + 1) * (width // 2)]


def touch_kernel(index, *refs):
    pass


def up_pairs(index, weight, pieces, dest, side):
    x, c, y, _ = place(index)
    half = weight.shape[0]
    rows = half // 2
    wide = weight.shape[1] // 4
    pairs = [
        (
            weight.at[:, pl.ds(pl.multiple_of((2 * side + c) * wide, wide), wide)],
            dest.at[pl.ds(pl.multiple_of(x * half, half), half)],
        )
    ]
    for q, piece in zip((y, 1 - y), pieces):
        pairs.append((piece, dest.at[pl.ds(pl.multiple_of((1 - x) * half + q * rows, rows), rows)]))
    return pairs


BLOCK = 512


def gelu_parts(hidden):
    cdf = 0.5 * (1.0 + lax.erf(hidden * (0.5**0.5)))
    slope = cdf + hidden * jnp.exp(-0.5 * hidden * hidden) * ((2.0 * jnp.pi) ** -0.5)
    return (hidden * cdf).astype(BF), slope


def by_bit(ref, rows, bit, parts):
    for k, part in enumerate(parts):
        for n in range(ref.shape[0] // (2 * rows)):
            here = pl.ds(pl.multiple_of((2 * n + (bit ^ k)) * rows, rows), rows)
            yield k, n, part, ref[here, :]


def ffn_other_kernel(
    index, normed, cot, bias, weight, p0, p1, act, slope, a_send, b_keep, b_send, w_all, g_all, sems
):
    x, _, y, _ = place(index)
    j = pl.program_id(0)

    @pl.when(j == 0)
    def _():
        copy_all(up_pairs(index, weight, (p0, p1), w_all, 1 - x), sems)

    w = w_all[:, pl.ds(pl.multiple_of(j * BLOCK, BLOCK), BLOCK)]
    hidden = mm(normed[...], w) + bias[...]
    a, s = gelu_parts(hidden)
    act[...] = a
    slope[...] = s.astype(BF)
    g = mm(a, cot[...], TN).astype(BF)

    @pl.when(j == 0)
    def _():
        for t in range(2):
            a_send[t] = g[:, t * TILE : (t + 1) * TILE]

    @pl.when(j == 1)
    def _():
        g_all[...] = g
        for _k, _n, part, half in by_bit(g_all, TILE // 2, y, (b_keep, b_send)):
            for t in range(2):
                part[t] = half[:, t * TILE : (t + 1) * TILE]


def ffn_own_kernel(
    index, normed, normed_t, cot, bias, down, weight, p0, p1, other_keep, other_send,
    act, hid, a_keep, b_keep, b_send, up_keep, up_send, colsum, w_all, g_all, u_all, sems,
):
    x, _, y, z = place(index)
    j = pl.program_id(0)

    @pl.when(j == 0)
    def _():
        copy_all(up_pairs(index, weight, (p0, p1), w_all, x), sems)

    w = w_all[:, pl.ds(pl.multiple_of(j * BLOCK, BLOCK), BLOCK)]
    hidden = mm(normed[...], w) + bias[...]
    a, s = gelu_parts(hidden)
    act[...] = a
    g = mm(a, cot[...], TN).astype(BF)

    @pl.when(j == 0)
    def _():
        for t in range(2):
            a_keep[t] = g[:, t * TILE : (t + 1) * TILE]

    @pl.when(j == 1)
    def _():
        g_all[...] = g
        for _k, _n, part, half in by_bit(g_all, TILE // 2, y, (b_keep, b_send)):
            for t in range(2):
                part[2 + t] = half[:, t * TILE : (t + 1) * TILE]
        b_keep[:2] = other_keep[...]
        b_send[:2] = other_send[...]

    low = (mm(cot[...], down[...], NT) * s).astype(BF)
    hid[...] = low
    colsum[...] = jnp.sum(low.astype(F32), axis=0, keepdims=True)
    u_all[...] = mm(normed_t[...], low).astype(BF)
    for _k, n, part, half in by_bit(u_all, up_keep.shape[3], z, (up_keep, up_send)):
        part[0, n // 2, n % 2] = half


def ffn_back_kernel(
    index, normed_t, cot, slope, d0, d1, d2, d3, hid, up_keep, up_send, colsum, d_all, u_all, sems
):
    y = index[2]
    j = pl.program_id(0)
    rows = d0.shape[0]

    @pl.when(j == 0)
    def _():
        copy_all(
            [
                (piece, d_all.at[pl.ds(pl.multiple_of(q * rows, rows), rows)])
                for q, piece in zip(quarters(index), (d0, d1, d2, d3))
            ],
            sems,
        )

    d = d_all[pl.ds(pl.multiple_of(j * BLOCK, BLOCK), BLOCK), :]
    low = (mm(cot[...], d, NT) * slope[...].astype(F32)).astype(BF)
    hid[...] = low
    colsum[...] = jnp.sum(low.astype(F32), axis=0, keepdims=True)
    u_all[...] = mm(normed_t[...], low).astype(BF)
    for _k, n, part, half in by_bit(u_all, up_keep.shape[2], y, (up_keep, up_send)):
        part[0, n] = half


def qkv_pairs(index, group, qkv, pieces, dest):
    x, c, _, _ = place(index)
    half = qkv.shape[0]
    quarter, wide = half // 4, half // 2
    own = pl.ds(pl.multiple_of(x * half, half), half)
    pairs = []
    for t in range(3):
        col = pl.multiple_of((4 * t + 2 * group + c) * wide, wide)
        pairs.append((qkv.at[:, pl.ds(col, wide)], dest.at[own, pl.ds(t * wide, wide)]))
    for q, piece in zip(quarters(index), pieces):
        row = pl.ds(pl.multiple_of((1 - x) * half + q * quarter, quarter), quarter)
        for t in range(3):
            pairs.append((piece.at[:, pl.ds((2 * t + group) * wide, wide)], dest.at[row, pl.ds(t * wide, wide)]))
    return pairs


def load_out(index, group, out_w, pieces, dest, sems, first):
    x, c, _, _ = place(index)
    half = out_w.shape[0]
    eighth, wide = half // 8, half // 2

    @pl.when(x == group)
    def _():
        copy_all([(out_w.at[pl.ds(pl.multiple_of(c * wide, wide), wide)], dest)], sems, first)

    @pl.when(x != group)
    def _():
        pairs = []
        for q, piece in zip(quarters(index), pieces):
            row = pl.ds(pl.multiple_of(q * eighth, eighth), eighth)
            for h in range(2):
                source = piece.at[pl.ds(h * eighth, eighth), pl.ds(3 * half, half)]
                pairs.append((source, dest.at[row, pl.ds(h * half, half)]))
        copy_all(pairs, sems, first + 1)


def attention_kernel(
    group, index, normed, normed_t, cot, cosine, sine_low, sine_high, doc_col, doc_row, bias,
    qkv, out_w, p0, p1, p2, p3, *refs
):
    if group == 0:
        send, keep, out_grad, context_out, mixed_out, colsum, w_all, o_all, mask, sems = refs
    else:
        early, send, keep, out_send, out_keep, context_out, mixed_out, colsum, w_all, o_all, mask, late, sems = refs
        out_grad = late
    x, c, y, _ = place(index)
    half = qkv.shape[0]
    wide = half // 2
    pair = 2 * HD
    length = doc_row.shape[1]

    def prepare():
        pairs = qkv_pairs(index, group, qkv, (p0, p1, p2, p3), w_all)
        copies = [pltpu.make_async_copy(a, b, sems.at[n]) for n, (a, b) in enumerate(pairs)]
        for copy in copies:
            copy.start()
        load_out(index, group, out_w, (p0, p1, p2, p3), o_all, sems, len(pairs))
        for s in range(2):
            keys = lax.broadcasted_iota(jnp.int32, (length, length), 0)
            queries = lax.broadcasted_iota(jnp.int32, (length, length), 1)
            same = doc_col[s * length : (s + 1) * length, :] == doc_row[s : s + 1, :]
            mask[s] = jnp.where(same & (keys <= queries), 0.0, MASKED)
        for copy in copies:
            copy.wait()

    prepare()
    pairs_here = wide // pair
    cs, lo, hi = cosine[...], sine_low[...], sine_high[...]

    def turn(v, sign):
        return v * cs + sign * (pltpu.roll(v, pair - ROT // 2, 1) * lo + pltpu.roll(v, ROT // 2, 1) * hi)

    scale = HD**-0.5
    mixed_all = mm(normed[...], w_all[...]) + bias[...]
    gc_both = mm(cot[...], o_all[...], NT).astype(BF)
    lane = lax.broadcasted_iota(jnp.int32, (length, pair), 1)
    first = lane < HD
    zero = jnp.zeros((length, pair), BF)
    part = length // 2
    turned_all = []
    for p in range(pairs_here):
        mixed = [mixed_all[:, t * wide + p * pair : t * wide + (p + 1) * pair] for t in range(3)]
        q_all = (turn(mixed[0], 1.0).astype(BF).astype(F32) * scale).astype(BF)
        k_all = turn(mixed[1], 1.0).astype(BF)
        v_all = mixed[2].astype(BF)
        gc_all = gc_both[:, p * pair : (p + 1) * pair]
        contexts_t, mixed_grads = [], []
        for s in range(2):
            row = slice(s * length, (s + 1) * length)
            q, k, v, gc = q_all[row], k_all[row], v_all[row], gc_all[row]
            k_turned, v_turned = k.T, v.T
            context_t, query_t, grad_k, grad_v = [], [], [], []
            mine = [first, ~first]
            qm = [jnp.where(m, q, zero) for m in mine]
            gm = [jnp.where(m, gc, zero) for m in mine]
            cts, qts, dks, dvs = [[], []], [[], []], [None, None], [None, None]
            for block in range(2):
                kk = part * (block + 1)
                qs = slice(block * part, (block + 1) * part)
                hs = range(2)
                scores = [mm(k[:kk], qm[h][qs], NT) + mask[s, :kk, qs] for h in hs]
                grad_probs = [mm(v[:kk], gm[h][qs], NT) for h in hs]
                weights = [jnp.exp(x - jnp.max(x, axis=0, keepdims=True)) for x in scores]
                probs = [x * (1.0 / jnp.sum(x, axis=0, keepdims=True)) for x in weights]
                low = [x.astype(BF) for x in probs]
                inner = [jnp.sum(a * b, axis=0, keepdims=True) for a, b in zip(probs, grad_probs)]
                ds = [(a * (b - c)).astype(BF) for a, b, c in zip(probs, grad_probs, inner)]
                for h in hs:
                    rows_h = slice(h * HD, (h + 1) * HD)
                    cts[h].append(mm(v_turned[rows_h, :kk], low[h]))
                    qts[h].append(mm(k_turned[rows_h, :kk], ds[h]))
                    dv_b, dk_b = mm(low[h], gc[qs]), mm(ds[h], q[qs])
                    if block == 0:
                        dvs[h], dks[h] = dv_b, dk_b
                    else:
                        dvs[h] = jnp.concatenate([dvs[h] + dv_b[:part], dv_b[part:]], axis=0)
                        dks[h] = jnp.concatenate([dks[h] + dk_b[:part], dk_b[part:]], axis=0)
            turned = jnp.concatenate([jnp.concatenate(c, axis=1) for c in cts], axis=0).astype(BF)
            contexts_t.append(turned)
            context_out[row, p * pair : (p + 1) * pair] = turned.T
            dq = jnp.concatenate([jnp.concatenate(c, axis=1) for c in qts], axis=0).T * scale
            mixed_grads.append((dq, jnp.where(first, dks[0], dks[1]), jnp.where(first, dvs[0], dvs[1])))
        dq, dk, dv = (jnp.concatenate([m[n] for m in mixed_grads], axis=0) for n in range(3))
        for t, v in enumerate((turn(dq, -1.0), turn(dk, -1.0), dv)):
            mixed_out[:, t * wide + p * pair : t * wide + (p + 1) * pair] = v.astype(BF)
        turned_all.append(jnp.concatenate(contexts_t, axis=1))
    grad_mixed = mixed_out[...]
    colsum[...] = jnp.sum(grad_mixed.astype(F32), axis=0, keepdims=True)
    if group == 0:
        for ref, side in ((keep, x), (send, 1 - x)):
            g = mm(normed_t[pl.ds(pl.multiple_of(side * half, half), half), :], grad_mixed).astype(BF)
            for t in range(3):
                ref[t] = g[:, t * wide : (t + 1) * wide]
    else:
        for ref, side in ((keep, y), (send, 1 - y)):
            for xr in range(2):
                rows = pl.ds(pl.multiple_of(xr * half + side * wide, wide), wide)
                g = mm(normed_t[rows, :], grad_mixed).astype(BF)
                for t in range(3):
                    ref[t, xr] = g[:, t * wide : (t + 1) * wide]
    g = mm(jnp.concatenate(turned_all, axis=0), cot[...]).astype(BF)
    for h in range(2):
        for cc in range(2):
            start = h * half + cc * wide
            out_grad[cc, h * wide : (h + 1) * wide, :] = g[:, start : start + wide]

    if group == 1:

        @pl.when(x == 0)
        def _():
            out_send[...] = late[...]
            out_keep[...] = early[...]

        @pl.when(x == 1)
        def _():
            out_send[...] = early[...]
            out_keep[...] = late[...]


def norm_kernel(index, tokens, other, cot, cot_other, gains, one, two, one_t, two_t, cot_out):
    mine = pl.program_id(0) < pl.num_programs(0) // 2
    rows = jnp.where(mine, tokens[...], other[...]).astype(F32)
    centred = rows - jnp.mean(rows, axis=-1, keepdims=True)
    unit = centred * lax.rsqrt(jnp.mean(centred * centred, axis=-1, keepdims=True) + EPSILON)
    first = unit * gains[0:1, :] + gains[1:2, :]
    second = unit * gains[2:3, :] + gains[3:4, :]
    one[...] = first.astype(BF)
    two[...] = second.astype(BF)
    one_t[...] = first.T.astype(BF)
    two_t[...] = second.T.astype(BF)
    cot_out[...] = jnp.where(mine, cot[...], cot_other[...])


def dense_ffn_kernel(
    index, act_o, act_x, hid_o, hid_x, down, d0, d1, d2, d3, up, p0, p1, q0, q1,
    out, grad, w_o, w_x, d_o, d_x, sems,
):
    x, c = index[0], index[1]
    i = pl.program_id(0)
    rows_d, wide = d0.shape[0], d_o.shape[0]
    for_down = [(down.at[pl.ds(pl.multiple_of(c * wide, wide), wide)], d_o)]
    for q, piece in zip(quarters(index), (d0, d1, d2, d3)):
        for_down.append((piece, d_x.at[pl.ds(pl.multiple_of(q * rows_d, rows_d), rows_d)]))
    for_up = up_pairs(index, up, (p0, p1), w_x, 1 - x) + up_pairs(index, up, (q0, q1), w_o, x)
    copies = [pltpu.make_async_copy(a, b, sems.at[n]) for n, (a, b) in enumerate(for_down + for_up)]

    @pl.when(i == 0)
    def _():
        for copy in copies:
            copy.start()
        for copy in copies[: len(for_down)]:
            copy.wait()

    out[...] = mm(act_o[...], d_o[...]) + mm(act_x[...], d_x[...])

    @pl.when(i == 0)
    def _():
        for copy in copies[len(for_down) :]:
            copy.wait()

    grad[...] = mm(hid_o[...], w_o[...], NT) + mm(hid_x[...], w_x[...], NT)


def dense_last_kernel(
    index, tokens, gains, ffn, grad_two, context_a, context_b, mixed_a, mixed_b, qkv, out_w, r0, r1, r2, r3,
    sums, pulled_send, pulled_keep, part_send, part_keep, m_a, m_b, o_a, o_b, sems,
):
    i = pl.program_id(0)
    steps = pl.num_programs(0)
    rest = (r0, r1, r2, r3)
    pairs = qkv_pairs(index, 0, qkv, rest, m_a) + qkv_pairs(index, 1, qkv, rest, m_b)
    copies = [pltpu.make_async_copy(a, b, sems.at[n]) for n, (a, b) in enumerate(pairs)]

    @pl.when(i == 0)
    def _():
        for copy in copies:
            copy.start()
        load_out(index, 0, out_w, rest, o_a, sems, len(pairs))
        load_out(index, 1, out_w, rest, o_b, sems, len(pairs))

    part = ffn[...] + mm(context_a[...], o_a[...]) + mm(context_b[...], o_b[...])

    @pl.when(i == 0)
    def _():
        for copy in copies:
            copy.wait()

    two = grad_two[...]
    one = mm(mixed_a[...], m_a[...], NT) + mm(mixed_b[...], m_b[...], NT)
    rows = tokens[...].astype(F32)
    centred = rows - jnp.mean(rows, axis=-1, keepdims=True)
    unit = centred * lax.rsqrt(jnp.mean(centred * centred, axis=-1, keepdims=True) + EPSILON)
    sums_here = jnp.concatenate(
        [jnp.sum(v, axis=0, keepdims=True) for v in (one * unit, one, two * unit, two)], axis=0
    )
    pulled = one * gains[0:1, :] + two * gains[2:3, :]

    @pl.when(i == 0)
    def _():
        sums[...] = sums_here

    @pl.when(i != 0)
    def _():
        sums[...] += sums_here

    @pl.when(i < steps // 2)
    def _():
        pulled_send[...] = pulled
        part_send[...] = part

    @pl.when(i >= steps // 2)
    def _():
        pulled_keep[...] = pulled
        part_keep[...] = part


def last_kernel(tokens, cot, gains, pulled_keep, pulled_recv, part_keep, part_recv, out, grad):
    rows = tokens[...].astype(F32)
    centred = rows - jnp.mean(rows, axis=-1, keepdims=True)
    spread = lax.rsqrt(jnp.mean(centred * centred, axis=-1, keepdims=True) + EPSILON)
    unit = centred * spread
    pulled = pulled_keep[...] + pulled_recv[...]
    inward = spread * (
        pulled
        - jnp.mean(pulled, axis=-1, keepdims=True)
        - unit * jnp.mean(pulled * unit, axis=-1, keepdims=True)
    )
    grad[...] = (cot[...].astype(F32) + inward).astype(BF)
    out[...] = (rows + (part_keep[...] + part_recv[...]) + (gains[4:5, :] + gains[5:6, :])).astype(BF)


def tables_kernel(index, doc_col, doc_row, inverse, cosine, sine_low, sine_high):
    length = doc_row.shape[1]
    few = ROT // 2
    ones = jnp.ones((HD - ROT, length), F32)
    zeros = jnp.zeros((HD - ROT, length), F32)
    none = jnp.zeros((few, length), F32)
    for s in range(2):
        rows = slice(s * length, (s + 1) * length)
        before = jnp.sum((doc_col[rows, :] < doc_row[s : s + 1, :]).astype(F32), axis=0, keepdims=True)
        offsets = lax.broadcasted_iota(jnp.int32, (1, length), 1).astype(F32) - before
        angles = inverse[...] * offsets
        cos, sine = jnp.cos(angles), jnp.sin(angles)
        cosine[rows, :] = jnp.concatenate([cos, cos, ones] * 2, axis=0).T
        sine_low[rows, :] = jnp.concatenate([-sine, none, zeros] * 2, axis=0).T
        sine_high[rows, :] = jnp.concatenate([none, sine, zeros] * 2, axis=0).T


def split_kernel(groups, index, *refs):
    outs = refs[sum(count for count, _ in groups) :]
    at = used = 0
    for g, (count, n) in enumerate(groups):
        addends = refs[used : used + count]
        used += count
        for t in range(n):
            for k, out in enumerate(outs):
                side = index[g] ^ k
                total = addends[0][t, side].astype(F32)
                for ref in addends[1:]:
                    total += ref[t, side].astype(F32)
                out[at] = total.astype(BF)
            at += 1


def batch_kernel(groups, index, *refs):
    outs = refs[sum(count for count, _ in groups) :]
    used = 0
    for g, (count, n) in enumerate(groups):
        addends = refs[used : used + count]
        used += count
        for t in range(n):
            for k in range(2):
                side = index[g] ^ k
                total = addends[0][t, side].astype(F32)
                for ref in addends[1:]:
                    total += ref[t, side].astype(F32)
                outs[2 * g + k][t] = total.astype(BF)


def cross_kernel(index, keep, recv, keep_out, send_out):
    for t in range(4):
        for k, out in enumerate((keep_out, send_out)):
            side = index[0] ^ k
            out[t] = (keep[t, side].astype(F32) + recv[t ^ 2, side].astype(F32)).astype(BF)


def stack_kernel(index, *refs):
    *pieces, out = refs
    for n, piece in enumerate(pieces):
        out[n] = piece[...]


def place_rows(index, y_rel, z_rel, rows, many):
    row = ((y_rel ^ index[2]) * many + (z_rel ^ index[4])) * rows
    return pl.ds(pl.multiple_of(row, rows), rows)


def join_kernel(index, down_keep, down_recv, up_keep, up_recv, c_keep, c_recv, out):
    half = c_keep.shape[2]
    for t in range(4):
        out[t] = (down_keep[t].astype(F32) + down_recv[t].astype(F32)).astype(BF)
        out[4 + t] = (up_keep[t].astype(F32) + up_recv[t].astype(F32)).astype(BF)
        for n, c in enumerate((t, 3 + t) if t < 3 else (6, 7)):
            out[8 + t, :, n * half : (n + 1) * half] = (c_keep[c].astype(F32) + c_recv[c].astype(F32)).astype(BF)


def sum_kernel(index, *refs):
    *parts, out = refs
    sums = [part[...] for part in parts]
    while len(sums) > 1:
        sums = [a + b for a, b in zip(sums[::2], sums[1::2])]
    out[...] = sums[0]


def reverse(k, count):
    out = 0
    while count > 1:
        out, k, count = 2 * out + k % 2, k // 2, count // 2
    return out


def widen_kernel(index, piece, down, up, qkv, out, slots, sems):
    many, _, _, _, rows, _ = piece.shape
    x = index[0]
    c = pl.program_id(0)
    quarter = TILE // 2

    def moves(job, core):
        slot = slots.at[job % 3]
        if job < 2:
            row = pl.multiple_of((2 * core + job) * TILE, TILE)
            return [(slot, down.at[pl.ds(row, TILE), :])]
        if job < 4:
            col = pl.multiple_of((4 * (x ^ (job - 2)) + 2 * core) * TILE, TILE)
            return [(slot, up.at[:, pl.ds(col, 2 * TILE)])]
        pairs = []
        for n in range(2 if job == 4 else 1):
            for g in range(2):
                col = pl.multiple_of((4 * (2 * (job - 4) + n) + 2 * g + core) * quarter, quarter)
                pairs.append((slot.at[:, pl.ds(n * TILE + g * quarter, quarter)], qkv.at[:, pl.ds(col, quarter)]))
        if job == 5:
            row = pl.multiple_of(core * quarter, quarter)
            for h in range(2):
                pairs.append(
                    (slot.at[pl.ds(h * quarter, quarter), pl.ds(TILE, TILE)], out.at[pl.ds(row, quarter), pl.ds(h * TILE, TILE)])
                )
        return pairs

    def copies(job, core):
        return [pltpu.make_async_copy(a, b, sems.at[job % 3, n]) for n, (a, b) in enumerate(moves(job, core))]

    def settle(job, core):
        for copy in copies(job, core):
            copy.wait()

    for job in range(6):
        if job < 3:

            @pl.when(c > 0)
            def _(job=job):
                settle(job + 3, c - 1)

        else:
            settle(job - 3, c)
        tiles = (2 * job, 2 * job + 1)
        for n, tile in enumerate(tiles):
            for y in range(2):
                for z in range(many):
                    row = (y * many + reverse(z, many)) * rows
                    slots[job % 3, row : row + rows, n * TILE : (n + 1) * TILE] = piece[z, y, 0, tile].astype(F32)
        for copy in copies(job, c):
            copy.start()

    @pl.when(c == pl.num_programs(0) - 1)
    def _():
        for job in range(3, 6):
            settle(job, c)


def build(reps):
    bits = reps.bit_length() - 1
    many = reps // 4

    def flip(array, bit):
        return lax.ppermute(array, "rep", [(i, i ^ (1 << bit)) for i in range(reps)])

    def hop(array, k):
        return lax.ppermute(array, "rep", [(i, i ^ (k << 2)) for i in range(reps)])

    def flip_x(array):
        return lax.ppermute(array, "shard", [(0, 1), (1, 0)])

    def call(kernel, grid, in_specs, out_specs, out_shape, scratch=(), est=None, after=(), aliases=(), mib=62):
        n_in, n_after, n_out = len(in_specs), len(after), len(out_shape)

        def wrapped(index, *refs):
            rest = refs[n_in + n_after :]
            kernel(index, *refs[:n_in], *rest[:n_out], *rest[n_out + 1 :])
            rest[n_out][...] = jnp.zeros((8, 128), F32)

        run = pl.pallas_call(
            wrapped,
            grid_spec=pltpu.PrefetchScalarGridSpec(
                num_scalar_prefetch=1,
                grid=grid,
                in_specs=list(in_specs) + [ANY] * n_after,
                out_specs=list(out_specs) + [pl.BlockSpec((8, 128), lambda *_: (0, 0))],
                scratch_shapes=list(scratch),
            ),
            out_shape=list(out_shape) + [sds((8, 128), F32)],
            compiler_params=params(mib),
            cost_estimate=est,
            input_output_aliases=dict(aliases),
        )
        return lambda index, *args: run(index, *args, *after)

    def on_device(
        tokens, segments, norm1_gain, norm1_shift, norm2_gain, norm2_shift, qkv_weight, qkv_bias,
        out_weight, out_bias, up_weight, up_bias, down_weight, down_bias, cotangent,
    ):
        half, width = out_weight.shape
        length = tokens.shape[0]
        ff_half = down_weight.shape[0]
        units = ff_half // 2
        toks = 2 * length
        xi = lax.axis_index("shard").astype(jnp.int32)
        ri = lax.axis_index("rep").astype(jnp.int32)
        rbit = [(ri >> b) & 1 for b in range(bits)]
        ci, yi = rbit[0], rbit[1]
        z_order = 0 * ri
        for bit in range(2, bits):
            z_order = 2 * z_order + rbit[bit]
        index = jnp.stack([xi, ci, yi, rbit[2], z_order])

        dma = pltpu.SemaphoreType.DMA
        wide = half // 2
        pair_rows = (half // 2, units)

        def corner(i, n):
            return 2 * (i[2] ^ n) + (i[3] ^ n)

        def from_qkv(n, t, h):
            return pl.BlockSpec((half // 4, wide), lambda g, i: (corner(i, n), 4 * t + 2 * h + i[1]))

        def whole(shape):
            return pl.BlockSpec(shape, lambda *_: (0,) * len(shape))

        def touch(arrays, after):
            n = len(arrays)
            shapes = [sds(a.shape, a.dtype) for a in arrays]
            return call(
                touch_kernel, (1,), [ANY] * n, [ANY] * n, shapes, (), cost(1, 1), after, {1 + k: k for k in range(n)}
            )(index, *arrays)

        def lay(vector, at, total):
            return jnp.pad(vector.astype(F32), (at, total - at - vector.shape[0]))

        tokens_other = flip(tokens, 0)
        cot_other = flip(cotangent, 0)
        vectors = [norm1_gain, norm1_shift, norm2_gain, norm2_shift, out_bias, down_bias, qkv_bias, up_bias]
        starts = [sum(v.shape[0] for v in vectors[:n]) for n in range(len(vectors) + 1)]
        small_own = sum(lay(v, s, starts[-1]) for v, s in zip(vectors, starts))
        small_other = flip_x(small_own)
        up_first, up_second, mark = call(
            pack_up_kernel, (1,),
            [pl.BlockSpec(pair_rows, lambda n, i: (i[2], 2 * i[0] + i[1])),
             pl.BlockSpec(pair_rows, lambda n, i: (i[2], 2 * (1 - i[0]) + i[1]))],
            [whole(pair_rows)] * 2, [sds(pair_rows, BF)] * 2, (), cost(1, 4 * MIB), [small_other],
        )(index, up_weight, up_weight)
        up_first = flip_x(up_first)

        segments_other = flip(segments, 0)

        low = jnp.where(xi == 0, small_own, small_other).reshape(-1, half)
        high = jnp.where(xi == 0, small_other, small_own).reshape(-1, half)
        gains = jnp.concatenate([low[:6], high[:6]], axis=1)
        qkv_b = jnp.concatenate([low[6:9], high[6:9]], axis=0).reshape(3, 2, 2, wide)
        qkv_b = lax.dynamic_index_in_dim(qkv_b, ci, 2, keepdims=False)
        up_b = jnp.concatenate([low[9:13], high[9:13]], axis=0).reshape(2, 2, units)
        up_b = lax.dynamic_index_in_dim(up_b, ci, 1, keepdims=False)
        up_b_own = lax.dynamic_slice_in_dim(up_b, xi, 1, 0)
        up_b_other = lax.dynamic_slice_in_dim(up_b, 1 - xi, 1, 0)

        rows = 256
        blocks = toks // rows

        def lower(i, *_):
            return (jnp.minimum(i, blocks // 2 - 1), 0)

        def upper_half(i, *_):
            return (jnp.maximum(i - blocks // 2, 0), 0)

        row_out = pl.BlockSpec((rows, width), lambda i, *_: (i, 0))
        column_out = pl.BlockSpec((width, rows), lambda i, *_: (0, i))
        turned_acts = sds((width, toks), BF)
        first_half, second_half = pl.BlockSpec((rows, width), lower), pl.BlockSpec((rows, width), upper_half)
        normed_one, normed_two, one_t, two_t, cot, mark = call(
            norm_kernel, (blocks,), [first_half, second_half] * 2 + [held((6, width))],
            [row_out, row_out, column_out, column_out, row_out],
            [sds((toks, width), BF)] * 2 + [turned_acts] * 2 + [sds((toks, width), BF)], (),
            cost(20 * toks * width, 14 * toks * width), [mark],
        )(index, tokens, tokens_other, cotangent, cot_other, gains)
        up_first, up_second, mark = touch([up_first, up_second], [mark])
        first_pieces = (up_first, flip(up_first, 1))
        up_second = flip_x(up_second)
        part_shapes = [(units // 4, width), (half // 4, 4 * half)] * 2
        in_specs, sources = [], []
        for n in range(2):
            in_specs.append(pl.BlockSpec((units // 4, width), lambda g, i, n=n: (4 * i[1] + corner(i, n), 0)))
            in_specs += [from_qkv(n, t, h) for t in range(3) for h in range(2)]
            in_specs.append(pl.BlockSpec((half // 8, width), lambda g, i, n=n: (4 * i[1] + corner(i, n), 0)))
            sources += [down_weight] + [qkv_weight] * 6 + [out_weight]
        down_part, rest_part, down_far, rest_far, mark = call(
            pack_kernel, (1,), in_specs,
            [whole(s) for s in part_shapes], [sds(s, BF) for s in part_shapes], (), cost(1, 8 * MIB), [mark],
        )(index, *sources)
        down_part, down_far = flip_x(down_part), flip_x(down_far)
        rest_part, rest_far = flip_x(rest_part), flip_x(rest_far)

        documents = jnp.concatenate([segments, segments_other], 0)
        doc_col = documents.reshape(toks, 1)
        pair = 2 * HD
        inverse = 1.0 / 10000.0 ** (jnp.arange(0, ROT, 2, dtype=F32) / ROT)
        inverse = inverse.reshape(ROT // 2, 1)
        cosine, sine_low, sine_high, mark = call(
            tables_kernel, (1,), [whole((toks, 1)), whole((2, length)), whole((ROT // 2, 1))], [whole((toks, pair))] * 3,
            [sds((toks, pair), F32)] * 3, (), cost(100 * toks * pair, 12 * toks * pair), [mark],
        )(index, doc_col, documents, inverse)

        up_second, mark = touch([up_second], [mark])
        second_pieces = (up_second, flip(up_second, 1))
        steps = units // BLOCK
        column = pl.BlockSpec((toks, BLOCK), lambda j, *_: (0, j))
        bias_block = pl.BlockSpec((1, BLOCK), lambda j, *_: (0, j))
        by_z = pl.BlockSpec((1, 2, 2, half // 4, BLOCK), lambda j, *_: (j, 0, 0, 0, 0))
        z_shape = sds((2, 2, 2, half // 4, TILE), BF)
        by_y = pl.BlockSpec((1, 2, half // 2, BLOCK), lambda j, *_: (j, 0, 0, 0))
        y_shape = sds((2, 2, half // 2, TILE), BF)
        two_tiles, two_halves = sds((2, TILE, TILE), BF), sds((2, TILE // 2, TILE), BF)
        four_halves = sds((4, TILE // 2, TILE), BF)
        unit_act = sds((toks, units), BF)
        full = held((toks, width))
        w_scratch = pltpu.VMEM((width, units), BF)
        d_scratch = pltpu.VMEM((units, width), BF)
        g_scratch = pltpu.VMEM((width, BLOCK), BF)
        one_mm = 2 * toks * width * units
        act_x, slope_x, da_send, other_keep, other_send, mark = call(
            ffn_other_kernel, (steps,), [full, full, bias_block] + [ANY] * 3,
            [column, column, whole(two_tiles.shape), whole(two_halves.shape), whole(two_halves.shape)],
            [unit_act, unit_act, two_tiles, two_halves, two_halves],
            [w_scratch, pltpu.VMEM((BLOCK, width), BF), dma((3,))], cost(5 * one_mm, 14 * MIB), [mark],
        )(index, normed_two, cot, up_b_other, up_weight, *first_pieces)
        down_part, mark = touch([down_part], [mark])
        down_pieces = (down_part, flip(down_part, 1), flip(down_part, 2), down_far)
        act_o, hid_o, da_keep, db_keep, db_send, uo_keep, uo_send, colsum_o, mark = call(
            ffn_own_kernel, (steps,),
            [full, full, full, bias_block, pl.BlockSpec((BLOCK, width), lambda j, i: (i[1] * steps + j, 0))]
            + [ANY] * 3 + [held(two_halves.shape)] * 2,
            [column, column, whole(two_tiles.shape), whole(four_halves.shape), whole(four_halves.shape), by_z, by_z, bias_block],
            [unit_act, unit_act, two_tiles, four_halves, four_halves, z_shape, z_shape, sds((1, units), F32)],
            [w_scratch, pltpu.VMEM((BLOCK, width), BF), g_scratch, dma((3,))], cost(8 * one_mm, 18 * MIB), [mark],
        )(index, normed_two, two_t, cot, up_b_own, down_weight, up_weight, *second_pieces, other_keep, other_send)
        rest_part, mark = touch([rest_part], [mark])
        rest_pieces = (rest_part, flip(rest_part, 1), flip(rest_part, 2), rest_far)
        da_recv, db_recv = flip_x(da_send), flip(db_send, 1)
        hid_x, ux_keep, ux_send, colsum_x, mark = call(
            ffn_back_kernel, (steps,), [full, full, column] + [ANY] * 4,
            [column, by_y, by_y, bias_block],
            [unit_act, y_shape, y_shape, sds((1, units), F32)],
            [d_scratch, g_scratch, dma((4,))], cost(4 * one_mm, 14 * MIB), [mark],
        )(index, two_t, cot, slope_x, *down_pieces)
        uo_recv, ux_recv = flip(uo_send, 2), flip(ux_send, 1)

        table = held((toks, pair))
        sum_shape = sds((1, 3 * wide), F32)
        out_tiles = sds((2, half, wide), BF)
        x_tiles = sds((3, half, wide), BF)
        y_tiles = sds((3, 2, wide, wide), BF)
        heads_out = [sds((toks, wide), BF), sds((toks, 3 * wide), BF), sum_shape]

        def attend(group, extra, shapes, scratch, after):
            specs = [full, full, full, table, table, table, held((toks, 1)), held((2, length)), held((1, 3 * wide))]
            return call(
                partial(attention_kernel, group), (1,),
                specs + [ANY] * 6 + [held(e.shape) for e in extra],
                [held(s.shape) for s in shapes], shapes,
                [pltpu.VMEM((width, 3 * wide), BF), pltpu.VMEM((wide, width), BF),
                 pltpu.VMEM((2, length, length), F32)] + scratch + [dma((24,))],
                cost(6e9, 4 * MIB), after,
            )(
                index, normed_one, one_t, cot, cosine, sine_low, sine_high, doc_col, documents,
                qkv_b[:, group].reshape(1, 3 * wide), qkv_weight, out_weight, *rest_pieces, *extra,
            )

        a_send, a_keep, out_early, context_a, mixed_a, colsum_a, mark = attend(
            0, [], [x_tiles, x_tiles, out_tiles] + heads_out, [], [mark]
        )

        def split(groups, ways, after):
            cols = groups[0][0][0].shape[-1]
            small = groups[0][0][0].size // groups[0][1] // cols // ways
            views = [(n, ways, small, cols) for addends, n, _ in groups for _ in addends]
            total = sum(n for _, n, _ in groups)
            out = (total, small, cols)
            return call(
                partial(split_kernel, [(len(addends), n) for addends, n, _ in groups]), (1,),
                [whole(v) for v in views], [whole(out)] * ways, [sds(out, BF)] * ways, (),
                cost(4 * total * small * cols, 12 * total * small * cols), after,
            )(
                jnp.stack([side for _, _, side in groups]),
                *[a.reshape(v) for a, v in zip([a for addends, _, _ in groups for a in addends], views)],
            )

        def batch(groups, after):
            views, outs = [], []
            for addends, n, _ in groups:
                cols = addends[0].shape[-1]
                small = addends[0].size // n // cols // 2
                views += [(n, 2, small, cols)] * len(addends)
                outs += [(n, small, cols)] * 2
            *results, mark = call(
                partial(batch_kernel, [(len(addends), n) for addends, n, _ in groups]), (1,),
                [whole(v) for v in views], [whole(o) for o in outs], [sds(o, BF) for o in outs], (),
                cost(1, 8 * MIB), after,
            )(
                jnp.stack([side for _, _, side in groups]),
                *[a.reshape(v) for a, v in zip([a for addends, _, _ in groups for a in addends], views)],
            )
            return [results[2 * g : 2 * g + 2] for g in range(len(groups))] + [mark]

        def split_cross(keep, recv, side, after):
            small, cols = keep.size // 8 // keep.shape[-1], keep.shape[-1]
            view, out = (4, 2, small, cols), (4, small, cols)
            return call(
                cross_kernel, (1,), [whole(view)] * 2, [whole(out)] * 2, [sds(out, BF)] * 2, (), cost(1, 1 * MIB), after, (), 20,
            )(side.reshape(1), keep.reshape(view), recv.reshape(view))

        def add(parts, after):
            n = parts[0].size // parts[0].shape[-1] // parts[0].shape[-2]
            return split([(parts, n, 0 * xi)], 1, after)

        def stack(pieces, after):
            shape = (len(pieces),) + pieces[0].shape
            return call(
                stack_kernel, (1,), [whole(shape[1:])] * len(pieces), [whole(shape)], [sds(shape, BF)], (),
                cost(1, 4 * pieces[0].size * len(pieces)), after,
            )(index, *pieces)

        token_rows = pl.BlockSpec((rows, units), lambda i, *_: (i, 0))
        token_out = pl.BlockSpec((rows, width), lambda i, *_: (i, 0))
        wide_f32 = sds((toks, width), F32)

        def turned(cols):
            return pl.BlockSpec((rows, cols), lambda i, *_: ((i + blocks // 2) % blocks, 0))

        sums_block = pl.BlockSpec((4, width), lambda i, *_: (0, 0))
        send_block, keep_block = pl.BlockSpec((rows, width), lower), pl.BlockSpec((rows, width), upper_half)
        own_f32 = sds((length, width), F32)
        m_scratch = pltpu.VMEM((width, 3 * wide), BF)
        out_scratch = pltpu.VMEM((wide, width), BF)

        def dense_last(i, tokens_ref, other_ref, *refs):
            mine = pl.program_id(0) >= blocks // 2
            dense_last_kernel(i, jnp.where(mine, tokens_ref[...], other_ref[...]), *refs)

        a_recv = flip_x(a_send)
        last_bits = list(range(3, bits))
        one = 1 + 0 * xi

        (da_keep, da_send), (db_keep, db_send), mark = batch(
            [([da_keep, da_recv], 2, yi), ([db_keep, db_recv], 1, one)], [mark]
        )
        da_recv = flip(da_send, 1)
        db_recv = flip_x(db_send)
        b_send, b_keep, out_send, out_keep, context_b, mixed_b, colsum_b, mark = attend(
            1, [out_early], [y_tiles, y_tiles, out_tiles, out_tiles] + heads_out,
            [pltpu.VMEM((2, half, wide), BF)], [mark],
        )
        da_recv, db_recv, b_send, out_send, mark = touch([da_recv, db_recv, b_send, out_send], [mark])
        b_recv = flip(b_send, 1)
        out_recv = flip_x(out_send)
        (a_keep, a_send), (ux_keep, ux_send), mark = batch(
            [([a_keep, a_recv], 3, yi), ([ux_keep, ux_recv], 4, rbit[2])], [mark]
        )
        a_recv, ux_recv = flip(a_send, 1), flip(ux_send, 2)
        d_keep, d_send, mark = split([([da_keep, da_recv], 2, rbit[2]), ([db_keep, db_recv], 2, rbit[2])], 2, [mark])
        d_recv = flip(d_send, 2)
        out_keep, out_send, mark = split([([out_keep, out_recv], 2, yi)], 2, [mark])
        out_recv = flip(out_send, 1)
        uo_keep, uo_send, mark = split([([uo_keep, uo_recv], 4, yi)], 2, [mark])
        uo_recv = flip(uo_send, 1)
        b_keep, b_send, mark = split([([b_keep, b_recv], 3, xi)], 2, [mark])
        b_recv = flip_x(b_send)
        d_parts = [([d_keep, d_recv], 4)]
        for bit in last_bits:
            d_keep, d_send, mark = split([(p, n, rbit[bit]) for p, n in d_parts], 2, [mark])
            d_recv = flip(d_send, bit)
            d_parts = [([d_keep, d_recv], 4)]
        c_keep, c_send, mark = split(
            [([k, v], n, rbit[2]) for k, v, n in ((a_keep, a_recv, 3), (b_keep, b_recv, 3), (out_keep, out_recv, 2))], 2, [mark]
        )
        c_recv = flip(c_send, 2)
        u_keep, u_send, mark = split([([uo_keep, uo_recv], 2, xi), ([ux_keep, ux_recv], 2, xi)], 2, [mark])
        u_recv = flip_x(u_send)
        for bit in last_bits:
            c_keep, c_send, mark = split([([c_keep, c_recv], 8, rbit[bit])], 2, [mark])
            c_recv = flip(c_send, bit)
        u_cross = True
        for bit in last_bits:
            u_keep, u_send, mark = split_cross(u_keep, u_recv, rbit[bit], [mark]) if u_cross else split(
                [([u_keep, u_recv], 4, rbit[bit])], 2, [mark]
            )
            u_cross = False
            u_recv = flip(u_send, bit)
        r = half // reps * 2
        piece, mark = call(
            join_kernel, (1,), [whole((4, r, TILE))] * 4 + [whole((8, r, wide))] * 2, [whole((12, r, TILE))],
            [sds((12, r, TILE), BF)], (), cost(1, 1), [mark],
        )(index, d_keep, d_recv, u_keep, u_recv, c_keep, c_recv)
        gathered = lax.all_gather(piece, "rep", axis=0, tiled=False).reshape(many, 2, 2, 12, r, TILE)

        ffn_part, grad_two, mark = call(
            dense_ffn_kernel, (blocks,), [token_rows] * 4 + [ANY] * 10, [token_out] * 2, [wide_f32] * 2,
            [w_scratch, w_scratch, d_scratch, d_scratch, dma((15,))], cost(6 * one_mm, 24 * MIB), [mark],
        )(index, act_o, act_x, hid_o, hid_x, down_weight, *down_pieces, up_weight, *first_pieces, *second_pieces)
        sums, pulled_send, pulled_keep, part_send, part_keep, mark = call(
            dense_last, (blocks,),
            [keep_block, send_block, held((6, width)), turned(width), turned(width)] + [turned(wide)] * 2
            + [turned(3 * wide)] * 2 + [ANY] * 6,
            [sums_block, send_block, keep_block, send_block, keep_block],
            [sds((4, width), F32)] + [own_f32] * 4,
            [m_scratch, m_scratch, out_scratch, out_scratch, dma((40,))],
            cost(4 * one_mm, 30 * MIB), [mark],
        )(
            index, tokens, tokens_other, gains, ffn_part, grad_two, context_a, context_b, mixed_a, mixed_b,
            qkv_weight, out_weight, *rest_pieces,
        )
        pulled_recv = flip(pulled_send, 0)
        part_recv = flip(part_send, 0)

        def spread_core(vector, parts):
            size = vector.size // parts
            v = vector.reshape(parts, 1, size)
            keep = (jnp.arange(2) == ci)[None, :, None]
            return jnp.where(keep, v, 0.0).reshape(-1, width)

        column_sum = jnp.sum(cotangent.astype(F32), axis=0, keepdims=True)
        colsum_up = jnp.where(
            xi == 0, jnp.concatenate([colsum_o, colsum_x], 0), jnp.concatenate([colsum_x, colsum_o], 0)
        )
        colsum_q = jnp.stack([colsum_a.reshape(3, wide), colsum_b.reshape(3, wide)], axis=1)
        small = jnp.concatenate([sums, column_sum, spread_core(colsum_q, 6), spread_core(colsum_up, 2)], axis=0)

        def meet(own, masks, after):
            size = 2 * reps
            parts = [own] + [
                lax.ppermute(own, ("rep", "shard"), [(i, i ^ m) for i in range(size)]) for m in masks
            ]
            return call(
                sum_kernel, (1,), [whole(own.shape)] * len(parts), [whole(own.shape)], [sds(own.shape, F32)], (),
                cost(1, 1), after,
            )(index, *parts)

        small, mark = meet(small, (1, 2, 3), [mark])
        output, grad_tokens, mark = call(
            lambda i, *refs: last_kernel(*refs), (length // rows,),
            [token_out, token_out, held((6, width))] + [token_out] * 4, [token_out] * 2,
            [sds((length, width), BF)] * 2, (), cost(40 * length * width, 24 * length * width), [mark],
        )(index, tokens, cotangent, gains, pulled_keep, pulled_recv, part_keep, part_recv)
        for bit in range(2, bits + 1, 2):
            masks = (1 << bit, 2 << bit, 3 << bit) if bit < bits else (1 << bit,)
            small, mark = meet(small, masks, [mark])

        down_grad, up_grad, qkv_grad, out_grad, mark = call(
            widen_kernel, (2,), [pl.BlockSpec((many, 2, 1, 12, r, TILE), lambda c, i: (0, 0, c, 0, 0, 0))], [ANY] * 4,
            [sds((ff_half, width), F32), sds((half, 2 * ff_half), F32), sds((half, 6 * half), F32), sds((half, width), F32)],
            [pltpu.VMEM((3, TILE, 2 * TILE), F32), dma((3, 4))], cost(1, 40 * MIB), [mark],
        )(index, gathered)

        def owned(row, count=1):
            v = small[row : row + count].reshape(2, -1)
            return lax.dynamic_index_in_dim(v, xi, 0, keepdims=False)

        bias_out = owned(4)
        return (
            output, grad_tokens, owned(0), owned(1), owned(2), owned(3), qkv_grad, owned(5, 3),
            out_grad, bias_out, up_grad, owned(8, 4), down_grad, bias_out,
        )

    return on_device


def solution(mesh):
    both = P(("rep", "shard"), None)
    vector = P("shard")
    matrix = P("shard", None)
    weights = (
        vector, vector, vector, vector, matrix, vector, matrix, vector, matrix, vector, matrix, vector,
    )
    return jax.shard_map(
        build(mesh.shape["rep"]),
        mesh=mesh,
        in_specs=(both, both) + weights + (both,),
        out_specs=(both, both) + weights,
        check_vma=False,
    )
```

```python
from functools import partial

import jax
import jax.numpy as jnp
from jax import lax
from jax.experimental import pallas as pl
from jax.experimental.pallas import tpu as pltpu
from jax.sharding import PartitionSpec as P

HD = 64
ROT = 16
EPSILON = 1e-05
MASKED = -1e30
BF = jnp.bfloat16
F32 = jnp.float32
TILE = 512
MIB = 1 << 20
NN = (((1,), (0,)), ((), ()))
NT = (((1,), (1,)), ((), ()))
TN = (((0,), (0,)), ((), ()))


def mm(left, right, dims=NN):
    return lax.dot_general(left, right, dims, preferred_element_type=F32)


def cost(flops, nbytes):
    return pl.CostEstimate(flops=int(flops), bytes_accessed=int(nbytes), transcendentals=0)


def params(mib=62):
    return pltpu.CompilerParams(vmem_limit_bytes=mib * MIB)


ANY = pl.BlockSpec(memory_space=pltpu.HBM)


def held(shape):
    return pl.BlockSpec(shape, lambda *_: (0,) * len(shape), pipeline_mode=pl.Buffered(1))


def sds(shape, kind):
    return jax.ShapeDtypeStruct(shape, kind)


def copy_all(pairs, sems, first=0):
    copies = [pltpu.make_async_copy(a, b, sems.at[first + n]) for n, (a, b) in enumerate(pairs)]
    for c in copies:
        c.start()
    for c in copies:
        c.wait()


def place(index):
    return index[0], index[1], index[2], index[3]


def quarters(index):
    _, _, y, z = place(index)
    return (2 * y + z, 2 * (1 - y) + z, 2 * y + (1 - z), 2 * (1 - y) + (1 - z))


def pack_up_kernel(index, first, second, first_out, second_out):
    first_out[...] = first[...]
    second_out[...] = second[...]


def pack_kernel(index, *refs):
    ins, outs = refs[:16], refs[16:]
    for n in range(2):
        down, *qkv, out_w = ins[8 * n : 8 * n + 8]
        down_out, rest_out = outs[2 * n : 2 * n + 2]
        down_out[...] = down[...]
        wide = qkv[0].shape[1]
        for m, piece in enumerate(qkv):
            rest_out[:, m * wide : (m + 1) * wide] = piece[...]
        rows, width = out_w.shape
        for h in range(2):
            rest_out[h * rows : (h + 1) * rows, 6 * wide :] = out_w[:, h * (width // 2) : (h + 1) * (width // 2)]


def touch_kernel(index, *refs):
    pass


def up_pairs(index, weight, pieces, dest, side):
    x, c, y, _ = place(index)
    half = weight.shape[0]
    rows = half // 2
    wide = weight.shape[1] // 4
    pairs = [
        (
            weight.at[:, pl.ds(pl.multiple_of((2 * side + c) * wide, wide), wide)],
            dest.at[pl.ds(pl.multiple_of(x * half, half), half)],
        )
    ]
    for q, piece in zip((y, 1 - y), pieces):
        pairs.append((piece, dest.at[pl.ds(pl.multiple_of((1 - x) * half + q * rows, rows), rows)]))
    return pairs


BLOCK = 512


def gelu_parts(hidden):
    cdf = 0.5 * (1.0 + lax.erf(hidden * (0.5**0.5)))
    slope = cdf + hidden * jnp.exp(-0.5 * hidden * hidden) * ((2.0 * jnp.pi) ** -0.5)
    return (hidden * cdf).astype(BF), slope


def by_bit(ref, rows, bit, parts):
    for k, part in enumerate(parts):
        for n in range(ref.shape[0] // (2 * rows)):
            here = pl.ds(pl.multiple_of((2 * n + (bit ^ k)) * rows, rows), rows)
            yield k, n, part, ref[here, :]


def ffn_other_kernel(
    index, normed, cot, bias, weight, p0, p1, act, slope, a_send, b_keep, b_send, w_all, g_all, sems
):
    x, _, y, _ = place(index)
    j = pl.program_id(0)

    @pl.when(j == 0)
    def _():
        copy_all(up_pairs(index, weight, (p0, p1), w_all, 1 - x), sems)

    w = w_all[:, pl.ds(pl.multiple_of(j * BLOCK, BLOCK), BLOCK)]
    hidden = mm(normed[...], w) + bias[...]
    a, s = gelu_parts(hidden)
    act[...] = a
    slope[...] = s.astype(BF)
    g = mm(a, cot[...], TN).astype(BF)

    @pl.when(j == 0)
    def _():
        for t in range(2):
            a_send[t] = g[:, t * TILE : (t + 1) * TILE]

    @pl.when(j == 1)
    def _():
        g_all[...] = g
        for _k, _n, part, half in by_bit(g_all, TILE // 2, y, (b_keep, b_send)):
            for t in range(2):
                part[t] = half[:, t * TILE : (t + 1) * TILE]


def ffn_own_kernel(
    index, normed, normed_t, cot, bias, down, weight, p0, p1, other_keep, other_send,
    act, hid, a_keep, b_keep, b_send, up_keep, up_send, colsum, w_all, g_all, u_all, sems,
):
    x, _, y, z = place(index)
    j = pl.program_id(0)

    @pl.when(j == 0)
    def _():
        copy_all(up_pairs(index, weight, (p0, p1), w_all, x), sems)

    w = w_all[:, pl.ds(pl.multiple_of(j * BLOCK, BLOCK), BLOCK)]
    hidden = mm(normed[...], w) + bias[...]
    a, s = gelu_parts(hidden)
    act[...] = a
    g = mm(a, cot[...], TN).astype(BF)

    @pl.when(j == 0)
    def _():
        for t in range(2):
            a_keep[t] = g[:, t * TILE : (t + 1) * TILE]

    @pl.when(j == 1)
    def _():
        g_all[...] = g
        for _k, _n, part, half in by_bit(g_all, TILE // 2, y, (b_keep, b_send)):
            for t in range(2):
                part[2 + t] = half[:, t * TILE : (t + 1) * TILE]
        b_keep[:2] = other_keep[...]
        b_send[:2] = other_send[...]

    low = (mm(cot[...], down[...], NT) * s).astype(BF)
    hid[...] = low
    colsum[...] = jnp.sum(low.astype(F32), axis=0, keepdims=True)
    u_all[...] = mm(normed_t[...], low).astype(BF)
    for _k, n, part, half in by_bit(u_all, up_keep.shape[3], z, (up_keep, up_send)):
        part[0, n // 2, n % 2] = half


def ffn_back_kernel(
    index, normed_t, cot, slope, d0, d1, d2, d3, hid, up_keep, up_send, colsum, d_all, u_all, sems
):
    y = index[2]
    j = pl.program_id(0)
    rows = d0.shape[0]

    @pl.when(j == 0)
    def _():
        copy_all(
            [
                (piece, d_all.at[pl.ds(pl.multiple_of(q * rows, rows), rows)])
                for q, piece in zip(quarters(index), (d0, d1, d2, d3))
            ],
            sems,
        )

    d = d_all[pl.ds(pl.multiple_of(j * BLOCK, BLOCK), BLOCK), :]
    low = (mm(cot[...], d, NT) * slope[...].astype(F32)).astype(BF)
    hid[...] = low
    colsum[...] = jnp.sum(low.astype(F32), axis=0, keepdims=True)
    u_all[...] = mm(normed_t[...], low).astype(BF)
    for _k, n, part, half in by_bit(u_all, up_keep.shape[2], y, (up_keep, up_send)):
        part[0, n] = half


def qkv_pairs(index, group, qkv, pieces, dest):
    x, c, _, _ = place(index)
    half = qkv.shape[0]
    quarter, wide = half // 4, half // 2
    own = pl.ds(pl.multiple_of(x * half, half), half)
    pairs = []
    for t in range(3):
        col = pl.multiple_of((4 * t + 2 * group + c) * wide, wide)
        pairs.append((qkv.at[:, pl.ds(col, wide)], dest.at[own, pl.ds(t * wide, wide)]))
    for q, piece in zip(quarters(index), pieces):
        row = pl.ds(pl.multiple_of((1 - x) * half + q * quarter, quarter), quarter)
        for t in range(3):
            pairs.append((piece.at[:, pl.ds((2 * t + group) * wide, wide)], dest.at[row, pl.ds(t * wide, wide)]))
    return pairs


def load_out(index, group, out_w, pieces, dest, sems, first):
    x, c, _, _ = place(index)
    half = out_w.shape[0]
    eighth, wide = half // 8, half // 2

    @pl.when(x == group)
    def _():
        copy_all([(out_w.at[pl.ds(pl.multiple_of(c * wide, wide), wide)], dest)], sems, first)

    @pl.when(x != group)
    def _():
        pairs = []
        for q, piece in zip(quarters(index), pieces):
            row = pl.ds(pl.multiple_of(q * eighth, eighth), eighth)
            for h in range(2):
                source = piece.at[pl.ds(h * eighth, eighth), pl.ds(3 * half, half)]
                pairs.append((source, dest.at[row, pl.ds(h * half, half)]))
        copy_all(pairs, sems, first + 1)


def attention_kernel(
    group, index, normed, normed_t, cot, cosine, sine_low, sine_high, doc_col, doc_row, bias,
    qkv, out_w, p0, p1, p2, p3, *refs
):
    if group == 0:
        send, keep, out_grad, context_out, mixed_out, colsum, w_all, o_all, mask, sems = refs
    else:
        early, send, keep, out_send, out_keep, context_out, mixed_out, colsum, w_all, o_all, mask, late, sems = refs
        out_grad = late
    x, c, y, _ = place(index)
    half = qkv.shape[0]
    wide = half // 2
    pair = 2 * HD
    length = doc_row.shape[1]

    def prepare():
        pairs = qkv_pairs(index, group, qkv, (p0, p1, p2, p3), w_all)
        copies = [pltpu.make_async_copy(a, b, sems.at[n]) for n, (a, b) in enumerate(pairs)]
        for copy in copies:
            copy.start()
        load_out(index, group, out_w, (p0, p1, p2, p3), o_all, sems, len(pairs))
        for s in range(2):
            keys = lax.broadcasted_iota(jnp.int32, (length, length), 0)
            queries = lax.broadcasted_iota(jnp.int32, (length, length), 1)
            same = doc_col[s * length : (s + 1) * length, :] == doc_row[s : s + 1, :]
            mask[s] = jnp.where(same & (keys <= queries), 0.0, MASKED)
        for copy in copies:
            copy.wait()

    prepare()
    pairs_here = wide // pair
    cs, lo, hi = cosine[...], sine_low[...], sine_high[...]

    def turn(v, sign):
        return v * cs + sign * (pltpu.roll(v, pair - ROT // 2, 1) * lo + pltpu.roll(v, ROT // 2, 1) * hi)

    scale = HD**-0.5
    mixed_all = mm(normed[...], w_all[...]) + bias[...]
    gc_both = mm(cot[...], o_all[...], NT).astype(BF)
    lane = lax.broadcasted_iota(jnp.int32, (length, pair), 1)
    first = lane < HD
    zero = jnp.zeros((length, pair), BF)
    part = length // 2
    turned_all = []
    for p in range(pairs_here):
        mixed = [mixed_all[:, t * wide + p * pair : t * wide + (p + 1) * pair] for t in range(3)]
        q_all = (turn(mixed[0], 1.0).astype(BF).astype(F32) * scale).astype(BF)
        k_all = turn(mixed[1], 1.0).astype(BF)
        v_all = mixed[2].astype(BF)
        gc_all = gc_both[:, p * pair : (p + 1) * pair]
        contexts_t, mixed_grads = [], []
        for s in range(2):
            row = slice(s * length, (s + 1) * length)
            q, k, v, gc = q_all[row], k_all[row], v_all[row], gc_all[row]
            k_turned, v_turned = k.T, v.T
            context_t, query_t, grad_k, grad_v = [], [], [], []
            mine = [first, ~first]
            qm = [jnp.where(m, q, zero) for m in mine]
            gm = [jnp.where(m, gc, zero) for m in mine]
            cts, qts, dks, dvs = [[], []], [[], []], [None, None], [None, None]
            for block in range(2):
                kk = part * (block + 1)
                qs = slice(block * part, (block + 1) * part)
                hs = range(2)
                scores = [mm(k[:kk], qm[h][qs], NT) + mask[s, :kk, qs] for h in hs]
                grad_probs = [mm(v[:kk], gm[h][qs], NT) for h in hs]
                weights = [jnp.exp(x - jnp.max(x, axis=0, keepdims=True)) for x in scores]
                probs = [x * (1.0 / jnp.sum(x, axis=0, keepdims=True)) for x in weights]
                low = [x.astype(BF) for x in probs]
                inner = [jnp.sum(a * b, axis=0, keepdims=True) for a, b in zip(probs, grad_probs)]
                ds = [(a * (b - c)).astype(BF) for a, b, c in zip(probs, grad_probs, inner)]
                for h in hs:
                    rows_h = slice(h * HD, (h + 1) * HD)
                    cts[h].append(mm(v_turned[rows_h, :kk], low[h]))
                    qts[h].append(mm(k_turned[rows_h, :kk], ds[h]))
                    dv_b, dk_b = mm(low[h], gc[qs]), mm(ds[h], q[qs])
                    if block == 0:
                        dvs[h], dks[h] = dv_b, dk_b
                    else:
                        dvs[h] = jnp.concatenate([dvs[h] + dv_b[:part], dv_b[part:]], axis=0)
                        dks[h] = jnp.concatenate([dks[h] + dk_b[:part], dk_b[part:]], axis=0)
            turned = jnp.concatenate([jnp.concatenate(c, axis=1) for c in cts], axis=0).astype(BF)
            contexts_t.append(turned)
            context_out[row, p * pair : (p + 1) * pair] = turned.T
            dq = jnp.concatenate([jnp.concatenate(c, axis=1) for c in qts], axis=0).T * scale
            mixed_grads.append((dq, jnp.where(first, dks[0], dks[1]), jnp.where(first, dvs[0], dvs[1])))
        dq, dk, dv = (jnp.concatenate([m[n] for m in mixed_grads], axis=0) for n in range(3))
        for t, v in enumerate((turn(dq, -1.0), turn(dk, -1.0), dv)):
            mixed_out[:, t * wide + p * pair : t * wide + (p + 1) * pair] = v.astype(BF)
        turned_all.append(jnp.concatenate(contexts_t, axis=1))
    grad_mixed = mixed_out[...]
    colsum[...] = jnp.sum(grad_mixed.astype(F32), axis=0, keepdims=True)
    if group == 0:
        for ref, side in ((keep, x), (send, 1 - x)):
            g = mm(normed_t[pl.ds(pl.multiple_of(side * half, half), half), :], grad_mixed).astype(BF)
            for t in range(3):
                ref[t] = g[:, t * wide : (t + 1) * wide]
    else:
        for ref, side in ((keep, y), (send, 1 - y)):
            for xr in range(2):
                rows = pl.ds(pl.multiple_of(xr * half + side * wide, wide), wide)
                g = mm(normed_t[rows, :], grad_mixed).astype(BF)
                for t in range(3):
                    ref[t, xr] = g[:, t * wide : (t + 1) * wide]
    g = mm(jnp.concatenate(turned_all, axis=0), cot[...]).astype(BF)
    for h in range(2):
        for cc in range(2):
            start = h * half + cc * wide
            out_grad[cc, h * wide : (h + 1) * wide, :] = g[:, start : start + wide]

    if group == 1:

        @pl.when(x == 0)
        def _():
            out_send[...] = late[...]
            out_keep[...] = early[...]

        @pl.when(x == 1)
        def _():
            out_send[...] = early[...]
            out_keep[...] = late[...]


def norm_kernel(index, tokens, other, cot, cot_other, gains, one, two, one_t, two_t, cot_out):
    mine = pl.program_id(0) < pl.num_programs(0) // 2
    rows = jnp.where(mine, tokens[...], other[...]).astype(F32)
    centred = rows - jnp.mean(rows, axis=-1, keepdims=True)
    unit = centred * lax.rsqrt(jnp.mean(centred * centred, axis=-1, keepdims=True) + EPSILON)
    first = unit * gains[0:1, :] + gains[1:2, :]
    second = unit * gains[2:3, :] + gains[3:4, :]
    one[...] = first.astype(BF)
    two[...] = second.astype(BF)
    one_t[...] = first.T.astype(BF)
    two_t[...] = second.T.astype(BF)
    cot_out[...] = jnp.where(mine, cot[...], cot_other[...])


def dense_ffn_kernel(
    index, act_o, act_x, hid_o, hid_x, down, d0, d1, d2, d3, up, p0, p1, q0, q1,
    out, grad, w_o, w_x, d_o, d_x, sems,
):
    x, c = index[0], index[1]
    i = pl.program_id(0)
    rows_d, wide = d0.shape[0], d_o.shape[0]
    for_down = [(down.at[pl.ds(pl.multiple_of(c * wide, wide), wide)], d_o)]
    for q, piece in zip(quarters(index), (d0, d1, d2, d3)):
        for_down.append((piece, d_x.at[pl.ds(pl.multiple_of(q * rows_d, rows_d), rows_d)]))
    for_up = up_pairs(index, up, (p0, p1), w_x, 1 - x) + up_pairs(index, up, (q0, q1), w_o, x)
    copies = [pltpu.make_async_copy(a, b, sems.at[n]) for n, (a, b) in enumerate(for_down + for_up)]

    @pl.when(i == 0)
    def _():
        for copy in copies:
            copy.start()
        for copy in copies[: len(for_down)]:
            copy.wait()

    out[...] = mm(act_o[...], d_o[...]) + mm(act_x[...], d_x[...])

    @pl.when(i == 0)
    def _():
        for copy in copies[len(for_down) :]:
            copy.wait()

    grad[...] = mm(hid_o[...], w_o[...], NT) + mm(hid_x[...], w_x[...], NT)


def dense_last_kernel(
    index, tokens, gains, ffn, grad_two, context_a, context_b, mixed_a, mixed_b, qkv, out_w, r0, r1, r2, r3,
    sums, pulled_send, pulled_keep, part_send, part_keep, m_a, m_b, o_a, o_b, sems,
):
    i = pl.program_id(0)
    steps = pl.num_programs(0)
    rest = (r0, r1, r2, r3)
    pairs = qkv_pairs(index, 0, qkv, rest, m_a) + qkv_pairs(index, 1, qkv, rest, m_b)
    copies = [pltpu.make_async_copy(a, b, sems.at[n]) for n, (a, b) in enumerate(pairs)]

    @pl.when(i == 0)
    def _():
        for copy in copies:
            copy.start()
        load_out(index, 0, out_w, rest, o_a, sems, len(pairs))
        load_out(index, 1, out_w, rest, o_b, sems, len(pairs))

    part = ffn[...] + mm(context_a[...], o_a[...]) + mm(context_b[...], o_b[...])

    @pl.when(i == 0)
    def _():
        for copy in copies:
            copy.wait()

    two = grad_two[...]
    one = mm(mixed_a[...], m_a[...], NT) + mm(mixed_b[...], m_b[...], NT)
    rows = tokens[...].astype(F32)
    centred = rows - jnp.mean(rows, axis=-1, keepdims=True)
    unit = centred * lax.rsqrt(jnp.mean(centred * centred, axis=-1, keepdims=True) + EPSILON)
    sums_here = jnp.concatenate(
        [jnp.sum(v, axis=0, keepdims=True) for v in (one * unit, one, two * unit, two)], axis=0
    )
    pulled = one * gains[0:1, :] + two * gains[2:3, :]

    @pl.when(i == 0)
    def _():
        sums[...] = sums_here

    @pl.when(i != 0)
    def _():
        sums[...] += sums_here

    @pl.when(i < steps // 2)
    def _():
        pulled_send[...] = pulled
        part_send[...] = part

    @pl.when(i >= steps // 2)
    def _():
        pulled_keep[...] = pulled
        part_keep[...] = part


def last_kernel(tokens, cot, gains, pulled_keep, pulled_recv, part_keep, part_recv, out, grad):
    rows = tokens[...].astype(F32)
    centred = rows - jnp.mean(rows, axis=-1, keepdims=True)
    spread = lax.rsqrt(jnp.mean(centred * centred, axis=-1, keepdims=True) + EPSILON)
    unit = centred * spread
    pulled = pulled_keep[...] + pulled_recv[...]
    inward = spread * (
        pulled
        - jnp.mean(pulled, axis=-1, keepdims=True)
        - unit * jnp.mean(pulled * unit, axis=-1, keepdims=True)
    )
    grad[...] = (cot[...].astype(F32) + inward).astype(BF)
    out[...] = (rows + (part_keep[...] + part_recv[...]) + (gains[4:5, :] + gains[5:6, :])).astype(BF)


def tables_kernel(index, doc_col, doc_row, inverse, cosine, sine_low, sine_high):
    length = doc_row.shape[1]
    few = ROT // 2
    ones = jnp.ones((HD - ROT, length), F32)
    zeros = jnp.zeros((HD - ROT, length), F32)
    none = jnp.zeros((few, length), F32)
    for s in range(2):
        rows = slice(s * length, (s + 1) * length)
        before = jnp.sum((doc_col[rows, :] < doc_row[s : s + 1, :]).astype(F32), axis=0, keepdims=True)
        offsets = lax.broadcasted_iota(jnp.int32, (1, length), 1).astype(F32) - before
        angles = inverse[...] * offsets
        cos, sine = jnp.cos(angles), jnp.sin(angles)
        cosine[rows, :] = jnp.concatenate([cos, cos, ones] * 2, axis=0).T
        sine_low[rows, :] = jnp.concatenate([-sine, none, zeros] * 2, axis=0).T
        sine_high[rows, :] = jnp.concatenate([none, sine, zeros] * 2, axis=0).T


def split_kernel(groups, index, *refs):
    outs = refs[sum(count for count, _ in groups) :]
    at = used = 0
    for g, (count, n) in enumerate(groups):
        addends = refs[used : used + count]
        used += count
        for t in range(n):
            for k, out in enumerate(outs):
                side = index[g] ^ k
                total = addends[0][t, side].astype(F32)
                for ref in addends[1:]:
                    total += ref[t, side].astype(F32)
                out[at] = total.astype(BF)
            at += 1


def batch_kernel(groups, index, *refs):
    outs = refs[sum(count for count, _ in groups) :]
    used = 0
    for g, (count, n) in enumerate(groups):
        addends = refs[used : used + count]
        used += count
        for t in range(n):
            for k in range(2):
                side = index[g] ^ k
                total = addends[0][t, side].astype(F32)
                for ref in addends[1:]:
                    total += ref[t, side].astype(F32)
                outs[2 * g + k][t] = total.astype(BF)


def cross_kernel(index, keep, recv, keep_out, send_out):
    for t in range(4):
        for k, out in enumerate((keep_out, send_out)):
            side = index[0] ^ k
            out[t] = (keep[t, side].astype(F32) + recv[t ^ 2, side].astype(F32)).astype(BF)


def stack_kernel(index, *refs):
    *pieces, out = refs
    for n, piece in enumerate(pieces):
        out[n] = piece[...]


def place_rows(index, y_rel, z_rel, rows, many):
    row = ((y_rel ^ index[2]) * many + (z_rel ^ index[4])) * rows
    return pl.ds(pl.multiple_of(row, rows), rows)


def join_kernel(index, down_keep, down_recv, up_keep, up_recv, c_keep, c_recv, out):
    half = c_keep.shape[2]
    for t in range(4):
        out[t] = (down_keep[t].astype(F32) + down_recv[t].astype(F32)).astype(BF)
        out[4 + t] = (up_keep[t].astype(F32) + up_recv[t].astype(F32)).astype(BF)
        for n, c in enumerate((t, 3 + t) if t < 3 else (6, 7)):
            out[8 + t, :, n * half : (n + 1) * half] = (c_keep[c].astype(F32) + c_recv[c].astype(F32)).astype(BF)


def sum_kernel(index, *refs):
    *parts, out = refs
    sums = [part[...] for part in parts]
    while len(sums) > 1:
        sums = [a + b for a, b in zip(sums[::2], sums[1::2])]
    out[...] = sums[0]


def reverse(k, count):
    out = 0
    while count > 1:
        out, k, count = 2 * out + k % 2, k // 2, count // 2
    return out


def widen_kernel(index, piece, down, up, qkv, out, slots, sems):
    many, _, _, _, rows, _ = piece.shape
    x = index[0]
    c = pl.program_id(0)
    quarter = TILE // 2

    def moves(job, core):
        slot = slots.at[job % 3]
        if job < 2:
            row = pl.multiple_of((2 * core + job) * TILE, TILE)
            return [(slot, down.at[pl.ds(row, TILE), :])]
        if job < 4:
            col = pl.multiple_of((4 * (x ^ (job - 2)) + 2 * core) * TILE, TILE)
            return [(slot, up.at[:, pl.ds(col, 2 * TILE)])]
        pairs = []
        for n in range(2 if job == 4 else 1):
            for g in range(2):
                col = pl.multiple_of((4 * (2 * (job - 4) + n) + 2 * g + core) * quarter, quarter)
                pairs.append((slot.at[:, pl.ds(n * TILE + g * quarter, quarter)], qkv.at[:, pl.ds(col, quarter)]))
        if job == 5:
            row = pl.multiple_of(core * quarter, quarter)
            for h in range(2):
                pairs.append(
                    (slot.at[pl.ds(h * quarter, quarter), pl.ds(TILE, TILE)], out.at[pl.ds(row, quarter), pl.ds(h * TILE, TILE)])
                )
        return pairs

    def copies(job, core):
        return [pltpu.make_async_copy(a, b, sems.at[job % 3, n]) for n, (a, b) in enumerate(moves(job, core))]

    def settle(job, core):
        for copy in copies(job, core):
            copy.wait()

    for job in range(6):
        if job < 3:

            @pl.when(c > 0)
            def _(job=job):
                settle(job + 3, c - 1)

        else:
            settle(job - 3, c)
        tiles = (2 * job, 2 * job + 1)
        for n, tile in enumerate(tiles):
            for y in range(2):
                for z in range(many):
                    row = (y * many + reverse(z, many)) * rows
                    slots[job % 3, row : row + rows, n * TILE : (n + 1) * TILE] = piece[z, y, 0, tile].astype(F32)
        for copy in copies(job, c):
            copy.start()

    @pl.when(c == pl.num_programs(0) - 1)
    def _():
        for job in range(3, 6):
            settle(job, c)


def build(reps):
    bits = reps.bit_length() - 1
    many = reps // 4

    def flip(array, bit):
        return lax.ppermute(array, "rep", [(i, i ^ (1 << bit)) for i in range(reps)])

    def hop(array, k):
        return lax.ppermute(array, "rep", [(i, i ^ (k << 2)) for i in range(reps)])

    def flip_x(array):
        return lax.ppermute(array, "shard", [(0, 1), (1, 0)])

    def call(kernel, grid, in_specs, out_specs, out_shape, scratch=(), est=None, after=(), aliases=(), mib=62):
        n_in, n_after, n_out = len(in_specs), len(after), len(out_shape)

        def wrapped(index, *refs):
            rest = refs[n_in + n_after :]
            kernel(index, *refs[:n_in], *rest[:n_out], *rest[n_out + 1 :])
            rest[n_out][...] = jnp.zeros((8, 128), F32)

        run = pl.pallas_call(
            wrapped,
            grid_spec=pltpu.PrefetchScalarGridSpec(
                num_scalar_prefetch=1,
                grid=grid,
                in_specs=list(in_specs) + [ANY] * n_after,
                out_specs=list(out_specs) + [pl.BlockSpec((8, 128), lambda *_: (0, 0))],
                scratch_shapes=list(scratch),
            ),
            out_shape=list(out_shape) + [sds((8, 128), F32)],
            compiler_params=params(mib),
            cost_estimate=est,
            input_output_aliases=dict(aliases),
        )
        return lambda index, *args: run(index, *args, *after)

    def on_device(
        tokens, segments, norm1_gain, norm1_shift, norm2_gain, norm2_shift, qkv_weight, qkv_bias,
        out_weight, out_bias, up_weight, up_bias, down_weight, down_bias, cotangent,
    ):
        half, width = out_weight.shape
        length = tokens.shape[0]
        ff_half = down_weight.shape[0]
        units = ff_half // 2
        toks = 2 * length
        xi = lax.axis_index("shard").astype(jnp.int32)
        ri = lax.axis_index("rep").astype(jnp.int32)
        rbit = [(ri >> b) & 1 for b in range(bits)]
        ci, yi = rbit[0], rbit[1]
        z_order = 0 * ri
        for bit in range(2, bits):
            z_order = 2 * z_order + rbit[bit]
        index = jnp.stack([xi, ci, yi, rbit[2], z_order])

        dma = pltpu.SemaphoreType.DMA
        wide = half // 2
        pair_rows = (half // 2, units)

        def corner(i, n):
            return 2 * (i[2] ^ n) + (i[3] ^ n)

        def from_qkv(n, t, h):
            return pl.BlockSpec((half // 4, wide), lambda g, i: (corner(i, n), 4 * t + 2 * h + i[1]))

        def whole(shape):
            return pl.BlockSpec(shape, lambda *_: (0,) * len(shape))

        def touch(arrays, after):
            n = len(arrays)
            shapes = [sds(a.shape, a.dtype) for a in arrays]
            return call(
                touch_kernel, (1,), [ANY] * n, [ANY] * n, shapes, (), cost(1, 1), after, {1 + k: k for k in range(n)}
            )(index, *arrays)

        def lay(vector, at, total):
            return jnp.pad(vector.astype(F32), (at, total - at - vector.shape[0]))

        tokens_other = flip(tokens, 0)
        cot_other = flip(cotangent, 0)
        vectors = [norm1_gain, norm1_shift, norm2_gain, norm2_shift, out_bias, down_bias, qkv_bias, up_bias]
        starts = [sum(v.shape[0] for v in vectors[:n]) for n in range(len(vectors) + 1)]
        small_own = sum(lay(v, s, starts[-1]) for v, s in zip(vectors, starts))
        small_other = flip_x(small_own)
        up_first, up_second, mark = call(
            pack_up_kernel, (1,),
            [pl.BlockSpec(pair_rows, lambda n, i: (i[2], 2 * i[0] + i[1])),
             pl.BlockSpec(pair_rows, lambda n, i: (i[2], 2 * (1 - i[0]) + i[1]))],
            [whole(pair_rows)] * 2, [sds(pair_rows, BF)] * 2, (), cost(1, 4 * MIB), [small_other],
        )(index, up_weight, up_weight)
        up_first = flip_x(up_first)

        segments_other = flip(segments, 0)

        low = jnp.where(xi == 0, small_own, small_other).reshape(-1, half)
        high = jnp.where(xi == 0, small_other, small_own).reshape(-1, half)
        gains = jnp.concatenate([low[:6], high[:6]], axis=1)
        qkv_b = jnp.concatenate([low[6:9], high[6:9]], axis=0).reshape(3, 2, 2, wide)
        qkv_b = lax.dynamic_index_in_dim(qkv_b, ci, 2, keepdims=False)
        up_b = jnp.concatenate([low[9:13], high[9:13]], axis=0).reshape(2, 2, units)
        up_b = lax.dynamic_index_in_dim(up_b, ci, 1, keepdims=False)
        up_b_own = lax.dynamic_slice_in_dim(up_b, xi, 1, 0)
        up_b_other = lax.dynamic_slice_in_dim(up_b, 1 - xi, 1, 0)

        rows = 256
        blocks = toks // rows

        def lower(i, *_):
            return (jnp.minimum(i, blocks // 2 - 1), 0)

        def upper_half(i, *_):
            return (jnp.maximum(i - blocks // 2, 0), 0)

        row_out = pl.BlockSpec((rows, width), lambda i, *_: (i, 0))
        column_out = pl.BlockSpec((width, rows), lambda i, *_: (0, i))
        turned_acts = sds((width, toks), BF)
        first_half, second_half = pl.BlockSpec((rows, width), lower), pl.BlockSpec((rows, width), upper_half)
        normed_one, normed_two, one_t, two_t, cot, mark = call(
            norm_kernel, (blocks,), [first_half, second_half] * 2 + [held((6, width))],
            [row_out, row_out, column_out, column_out, row_out],
            [sds((toks, width), BF)] * 2 + [turned_acts] * 2 + [sds((toks, width), BF)], (),
            cost(20 * toks * width, 14 * toks * width), [mark],
        )(index, tokens, tokens_other, cotangent, cot_other, gains)
        up_first, up_second, mark = touch([up_first, up_second], [mark])
        first_pieces = (up_first, flip(up_first, 1))
        up_second = flip_x(up_second)
        part_shapes = [(units // 4, width), (half // 4, 4 * half)] * 2
        in_specs, sources = [], []
        for n in range(2):
            in_specs.append(pl.BlockSpec((units // 4, width), lambda g, i, n=n: (4 * i[1] + corner(i, n), 0)))
            in_specs += [from_qkv(n, t, h) for t in range(3) for h in range(2)]
            in_specs.append(pl.BlockSpec((half // 8, width), lambda g, i, n=n: (4 * i[1] + corner(i, n), 0)))
            sources += [down_weight] + [qkv_weight] * 6 + [out_weight]
        down_part, rest_part, down_far, rest_far, mark = call(
            pack_kernel, (1,), in_specs,
            [whole(s) for s in part_shapes], [sds(s, BF) for s in part_shapes], (), cost(1, 8 * MIB), [mark],
        )(index, *sources)
        down_part, down_far = flip_x(down_part), flip_x(down_far)
        rest_part, rest_far = flip_x(rest_part), flip_x(rest_far)

        documents = jnp.concatenate([segments, segments_other], 0)
        doc_col = documents.reshape(toks, 1)
        pair = 2 * HD
        inverse = 1.0 / 10000.0 ** (jnp.arange(0, ROT, 2, dtype=F32) / ROT)
        inverse = inverse.reshape(ROT // 2, 1)
        cosine, sine_low, sine_high, mark = call(
            tables_kernel, (1,), [whole((toks, 1)), whole((2, length)), whole((ROT // 2, 1))], [whole((toks, pair))] * 3,
            [sds((toks, pair), F32)] * 3, (), cost(100 * toks * pair, 12 * toks * pair), [mark],
        )(index, doc_col, documents, inverse)

        up_second, mark = touch([up_second], [mark])
        second_pieces = (up_second, flip(up_second, 1))
        steps = units // BLOCK
        column = pl.BlockSpec((toks, BLOCK), lambda j, *_: (0, j))
        bias_block = pl.BlockSpec((1, BLOCK), lambda j, *_: (0, j))
        by_z = pl.BlockSpec((1, 2, 2, half // 4, BLOCK), lambda j, *_: (j, 0, 0, 0, 0))
        z_shape = sds((2, 2, 2, half // 4, TILE), BF)
        by_y = pl.BlockSpec((1, 2, half // 2, BLOCK), lambda j, *_: (j, 0, 0, 0))
        y_shape = sds((2, 2, half // 2, TILE), BF)
        two_tiles, two_halves = sds((2, TILE, TILE), BF), sds((2, TILE // 2, TILE), BF)
        four_halves = sds((4, TILE // 2, TILE), BF)
        unit_act = sds((toks, units), BF)
        full = held((toks, width))
        w_scratch = pltpu.VMEM((width, units), BF)
        d_scratch = pltpu.VMEM((units, width), BF)
        g_scratch = pltpu.VMEM((width, BLOCK), BF)
        one_mm = 2 * toks * width * units
        act_x, slope_x, da_send, other_keep, other_send, mark = call(
            ffn_other_kernel, (steps,), [full, full, bias_block] + [ANY] * 3,
            [column, column, whole(two_tiles.shape), whole(two_halves.shape), whole(two_halves.shape)],
            [unit_act, unit_act, two_tiles, two_halves, two_halves],
            [w_scratch, pltpu.VMEM((BLOCK, width), BF), dma((3,))], cost(5 * one_mm, 14 * MIB), [mark],
        )(index, normed_two, cot, up_b_other, up_weight, *first_pieces)
        down_part, mark = touch([down_part], [mark])
        down_pieces = (down_part, flip(down_part, 1), flip(down_part, 2), down_far)
        act_o, hid_o, da_keep, db_keep, db_send, uo_keep, uo_send, colsum_o, mark = call(
            ffn_own_kernel, (steps,),
            [full, full, full, bias_block, pl.BlockSpec((BLOCK, width), lambda j, i: (i[1] * steps + j, 0))]
            + [ANY] * 3 + [held(two_halves.shape)] * 2,
            [column, column, whole(two_tiles.shape), whole(four_halves.shape), whole(four_halves.shape), by_z, by_z, bias_block],
            [unit_act, unit_act, two_tiles, four_halves, four_halves, z_shape, z_shape, sds((1, units), F32)],
            [w_scratch, pltpu.VMEM((BLOCK, width), BF), g_scratch, dma((3,))], cost(8 * one_mm, 18 * MIB), [mark],
        )(index, normed_two, two_t, cot, up_b_own, down_weight, up_weight, *second_pieces, other_keep, other_send)
        rest_part, mark = touch([rest_part], [mark])
        rest_pieces = (rest_part, flip(rest_part, 1), flip(rest_part, 2), rest_far)
        da_recv, db_recv = flip_x(da_send), flip(db_send, 1)
        hid_x, ux_keep, ux_send, colsum_x, mark = call(
            ffn_back_kernel, (steps,), [full, full, column] + [ANY] * 4,
            [column, by_y, by_y, bias_block],
            [unit_act, y_shape, y_shape, sds((1, units), F32)],
            [d_scratch, g_scratch, dma((4,))], cost(4 * one_mm, 14 * MIB), [mark],
        )(index, two_t, cot, slope_x, *down_pieces)
        uo_recv, ux_recv = flip(uo_send, 2), flip(ux_send, 1)

        table = held((toks, pair))
        sum_shape = sds((1, 3 * wide), F32)
        out_tiles = sds((2, half, wide), BF)
        x_tiles = sds((3, half, wide), BF)
        y_tiles = sds((3, 2, wide, wide), BF)
        heads_out = [sds((toks, wide), BF), sds((toks, 3 * wide), BF), sum_shape]

        def attend(group, extra, shapes, scratch, after):
            specs = [full, full, full, table, table, table, held((toks, 1)), held((2, length)), held((1, 3 * wide))]
            return call(
                partial(attention_kernel, group), (1,),
                specs + [ANY] * 6 + [held(e.shape) for e in extra],
                [held(s.shape) for s in shapes], shapes,
                [pltpu.VMEM((width, 3 * wide), BF), pltpu.VMEM((wide, width), BF),
                 pltpu.VMEM((2, length, length), F32)] + scratch + [dma((24,))],
                cost(6e9, 4 * MIB), after,
            )(
                index, normed_one, one_t, cot, cosine, sine_low, sine_high, doc_col, documents,
                qkv_b[:, group].reshape(1, 3 * wide), qkv_weight, out_weight, *rest_pieces, *extra,
            )

        a_send, a_keep, out_early, context_a, mixed_a, colsum_a, mark = attend(
            0, [], [x_tiles, x_tiles, out_tiles] + heads_out, [], [mark]
        )

        def split(groups, ways, after):
            cols = groups[0][0][0].shape[-1]
            small = groups[0][0][0].size // groups[0][1] // cols // ways
            views = [(n, ways, small, cols) for addends, n, _ in groups for _ in addends]
            total = sum(n for _, n, _ in groups)
            out = (total, small, cols)
            return call(
                partial(split_kernel, [(len(addends), n) for addends, n, _ in groups]), (1,),
                [whole(v) for v in views], [whole(out)] * ways, [sds(out, BF)] * ways, (),
                cost(4 * total * small * cols, 12 * total * small * cols), after,
            )(
                jnp.stack([side for _, _, side in groups]),
                *[a.reshape(v) for a, v in zip([a for addends, _, _ in groups for a in addends], views)],
            )

        def batch(groups, after):
            views, outs = [], []
            for addends, n, _ in groups:
                cols = addends[0].shape[-1]
                small = addends[0].size // n // cols // 2
                views += [(n, 2, small, cols)] * len(addends)
                outs += [(n, small, cols)] * 2
            *results, mark = call(
                partial(batch_kernel, [(len(addends), n) for addends, n, _ in groups]), (1,),
                [whole(v) for v in views], [whole(o) for o in outs], [sds(o, BF) for o in outs], (),
                cost(1, 8 * MIB), after,
            )(
                jnp.stack([side for _, _, side in groups]),
                *[a.reshape(v) for a, v in zip([a for addends, _, _ in groups for a in addends], views)],
            )
            return [results[2 * g : 2 * g + 2] for g in range(len(groups))] + [mark]

        def split_cross(keep, recv, side, after):
            small, cols = keep.size // 8 // keep.shape[-1], keep.shape[-1]
            view, out = (4, 2, small, cols), (4, small, cols)
            return call(
                cross_kernel, (1,), [whole(view)] * 2, [whole(out)] * 2, [sds(out, BF)] * 2, (), cost(1, 1 * MIB), after, (), 20,
            )(side.reshape(1), keep.reshape(view), recv.reshape(view))

        def add(parts, after):
            n = parts[0].size // parts[0].shape[-1] // parts[0].shape[-2]
            return split([(parts, n, 0 * xi)], 1, after)

        def stack(pieces, after):
            shape = (len(pieces),) + pieces[0].shape
            return call(
                stack_kernel, (1,), [whole(shape[1:])] * len(pieces), [whole(shape)], [sds(shape, BF)], (),
                cost(1, 4 * pieces[0].size * len(pieces)), after,
            )(index, *pieces)

        token_rows = pl.BlockSpec((rows, units), lambda i, *_: (i, 0))
        token_out = pl.BlockSpec((rows, width), lambda i, *_: (i, 0))
        wide_f32 = sds((toks, width), F32)

        def turned(cols):
            return pl.BlockSpec((rows, cols), lambda i, *_: ((i + blocks // 2) % blocks, 0))

        sums_block = pl.BlockSpec((4, width), lambda i, *_: (0, 0))
        send_block, keep_block = pl.BlockSpec((rows, width), lower), pl.BlockSpec((rows, width), upper_half)
        own_f32 = sds((length, width), F32)
        m_scratch = pltpu.VMEM((width, 3 * wide), BF)
        out_scratch = pltpu.VMEM((wide, width), BF)

        def dense_last(i, tokens_ref, other_ref, *refs):
            mine = pl.program_id(0) >= blocks // 2
            dense_last_kernel(i, jnp.where(mine, tokens_ref[...], other_ref[...]), *refs)

        a_recv = flip_x(a_send)
        last_bits = list(range(3, bits))
        one = 1 + 0 * xi

        (da_keep, da_send), (db_keep, db_send), mark = batch(
            [([da_keep, da_recv], 2, yi), ([db_keep, db_recv], 1, one)], [mark]
        )
        da_recv = flip(da_send, 1)
        db_recv = flip_x(db_send)
        b_send, b_keep, out_send, out_keep, context_b, mixed_b, colsum_b, mark = attend(
            1, [out_early], [y_tiles, y_tiles, out_tiles, out_tiles] + heads_out,
            [pltpu.VMEM((2, half, wide), BF)], [mark],
        )
        da_recv, db_recv, b_send, out_send, mark = touch([da_recv, db_recv, b_send, out_send], [mark])
        b_recv = flip(b_send, 1)
        out_recv = flip_x(out_send)
        (a_keep, a_send), (ux_keep, ux_send), mark = batch(
            [([a_keep, a_recv], 3, yi), ([ux_keep, ux_recv], 4, rbit[2])], [mark]
        )
        a_recv, ux_recv = flip(a_send, 1), flip(ux_send, 2)
        d_keep, d_send, mark = split([([da_keep, da_recv], 2, rbit[2]), ([db_keep, db_recv], 2, rbit[2])], 2, [mark])
        d_recv = flip(d_send, 2)
        (out_keep, out_send), (uo_keep, uo_send), mark = batch(
            [([out_keep, out_recv], 2, yi), ([uo_keep, uo_recv], 4, yi)], [mark]
        )
        out_recv, uo_recv = flip(out_send, 1), flip(uo_send, 1)
        b_keep, b_send, mark = split([([b_keep, b_recv], 3, xi)], 2, [mark])
        b_recv = flip_x(b_send)
        d_parts = [([d_keep, d_recv], 4)]
        for bit in last_bits:
            d_keep, d_send, mark = split([(p, n, rbit[bit]) for p, n in d_parts], 2, [mark])
            d_recv = flip(d_send, bit)
            d_parts = [([d_keep, d_recv], 4)]
        c_keep, c_send, mark = split(
            [([k, v], n, rbit[2]) for k, v, n in ((a_keep, a_recv, 3), (b_keep, b_recv, 3), (out_keep, out_recv, 2))], 2, [mark]
        )
        c_recv = flip(c_send, 2)
        u_keep, u_send, mark = split([([uo_keep, uo_recv], 2, xi), ([ux_keep, ux_recv], 2, xi)], 2, [mark])
        u_recv = flip_x(u_send)
        for bit in last_bits:
            c_keep, c_send, mark = split([([c_keep, c_recv], 8, rbit[bit])], 2, [mark])
            c_recv = flip(c_send, bit)
        u_cross = True
        for bit in last_bits:
            u_keep, u_send, mark = split_cross(u_keep, u_recv, rbit[bit], [mark]) if u_cross else split(
                [([u_keep, u_recv], 4, rbit[bit])], 2, [mark]
            )
            u_cross = False
            u_recv = flip(u_send, bit)
        r = half // reps * 2
        piece, mark = call(
            join_kernel, (1,), [whole((4, r, TILE))] * 4 + [whole((8, r, wide))] * 2, [whole((12, r, TILE))],
            [sds((12, r, TILE), BF)], (), cost(1, 1), [mark],
        )(index, d_keep, d_recv, u_keep, u_recv, c_keep, c_recv)
        gathered = lax.all_gather(piece, "rep", axis=0, tiled=False).reshape(many, 2, 2, 12, r, TILE)

        ffn_part, grad_two, mark = call(
            dense_ffn_kernel, (blocks,), [token_rows] * 4 + [ANY] * 10, [token_out] * 2, [wide_f32] * 2,
            [w_scratch, w_scratch, d_scratch, d_scratch, dma((15,))], cost(6 * one_mm, 24 * MIB), [mark],
        )(index, act_o, act_x, hid_o, hid_x, down_weight, *down_pieces, up_weight, *first_pieces, *second_pieces)
        sums, pulled_send, pulled_keep, part_send, part_keep, mark = call(
            dense_last, (blocks,),
            [keep_block, send_block, held((6, width)), turned(width), turned(width)] + [turned(wide)] * 2
            + [turned(3 * wide)] * 2 + [ANY] * 6,
            [sums_block, send_block, keep_block, send_block, keep_block],
            [sds((4, width), F32)] + [own_f32] * 4,
            [m_scratch, m_scratch, out_scratch, out_scratch, dma((40,))],
            cost(4 * one_mm, 30 * MIB), [mark],
        )(
            index, tokens, tokens_other, gains, ffn_part, grad_two, context_a, context_b, mixed_a, mixed_b,
            qkv_weight, out_weight, *rest_pieces,
        )
        pulled_recv = flip(pulled_send, 0)
        part_recv = flip(part_send, 0)

        def spread_core(vector, parts):
            size = vector.size // parts
            v = vector.reshape(parts, 1, size)
            keep = (jnp.arange(2) == ci)[None, :, None]
            return jnp.where(keep, v, 0.0).reshape(-1, width)

        column_sum = jnp.sum(cotangent.astype(F32), axis=0, keepdims=True)
        colsum_up = jnp.where(
            xi == 0, jnp.concatenate([colsum_o, colsum_x], 0), jnp.concatenate([colsum_x, colsum_o], 0)
        )
        colsum_q = jnp.stack([colsum_a.reshape(3, wide), colsum_b.reshape(3, wide)], axis=1)
        small = jnp.concatenate([sums, column_sum, spread_core(colsum_q, 6), spread_core(colsum_up, 2)], axis=0)

        def meet(own, masks, after):
            size = 2 * reps
            parts = [own] + [
                lax.ppermute(own, ("rep", "shard"), [(i, i ^ m) for i in range(size)]) for m in masks
            ]
            return call(
                sum_kernel, (1,), [whole(own.shape)] * len(parts), [whole(own.shape)], [sds(own.shape, F32)], (),
                cost(1, 1), after,
            )(index, *parts)

        small, mark = meet(small, (1, 2, 3), [mark])
        output, grad_tokens, mark = call(
            lambda i, *refs: last_kernel(*refs), (length // rows,),
            [token_out, token_out, held((6, width))] + [token_out] * 4, [token_out] * 2,
            [sds((length, width), BF)] * 2, (), cost(40 * length * width, 24 * length * width), [mark],
        )(index, tokens, cotangent, gains, pulled_keep, pulled_recv, part_keep, part_recv)
        for bit in range(2, bits + 1, 2):
            masks = (1 << bit, 2 << bit, 3 << bit) if bit < bits else (1 << bit,)
            small, mark = meet(small, masks, [mark])

        down_grad, up_grad, qkv_grad, out_grad, mark = call(
            widen_kernel, (2,), [pl.BlockSpec((many, 2, 1, 12, r, TILE), lambda c, i: (0, 0, c, 0, 0, 0))], [ANY] * 4,
            [sds((ff_half, width), F32), sds((half, 2 * ff_half), F32), sds((half, 6 * half), F32), sds((half, width), F32)],
            [pltpu.VMEM((3, TILE, 2 * TILE), F32), dma((3, 4))], cost(1, 40 * MIB), [mark],
        )(index, gathered)

        def owned(row, count=1):
            v = small[row : row + count].reshape(2, -1)
            return lax.dynamic_index_in_dim(v, xi, 0, keepdims=False)

        bias_out = owned(4)
        return (
            output, grad_tokens, owned(0), owned(1), owned(2), owned(3), qkv_grad, owned(5, 3),
            out_grad, bias_out, up_grad, owned(8, 4), down_grad, bias_out,
        )

    return on_device


def solution(mesh):
    both = P(("rep", "shard"), None)
    vector = P("shard")
    matrix = P("shard", None)
    weights = (
        vector, vector, vector, vector, matrix, vector, matrix, vector, matrix, vector, matrix, vector,
    )
    return jax.shard_map(
        build(mesh.shape["rep"]),
        mesh=mesh,
        in_specs=(both, both) + weights + (both,),
        out_specs=(both, both) + weights,
        check_vma=False,
    )
```
